256 devices in a mesh: band: 64 (over z, x, core), rep: 4 (over y).
Axes of the slice: x: 4, y: 4, z: 8, core: 2. Of those that a mesh axis runs over, the one named last changes fastest.
Arguments:
- points: bfloat16 [262144, 256], P('band'), may hold values from -6 to 6
- rank_source: int32 [262144], replicated, may hold values from 0 to 262143, as said below
- thresholds: int32 [262144], replicated, may hold values from 1000 to 1399
- kept_tiles: int32 [32, 10], replicated, may hold values from -1 to 15, as said below
Outputs:
- degrees: float32 [262144], P('band')
The draws below stay inside these ranges and needn't reach their ends.
Inputs may be any that keep to these rules, and one draw needn't show every extreme that they name: `rank_source`: A permutation of the input indices; each block of 4096 consecutive input indices holds exactly 64 points of each band (band = rank // 4096). `kept_tiles`: row q lists distinct codes a * 4 + c with 0 <= a <= c < 4, then -1 entries; every row lists at least 5 codes, some row lists all 10.
All inputs are finite; a program needn't handle non-finite values.
Results may differ from the reference program's by a relative error of at most 0.0003.
Values may be sent and summed in bfloat16 or wider, within the bound.
No kernel may reach another device: no remote copies, remote signals or barrier semaphores. Data moves between devices by JAX's collectives and lax.ppermute only.
A program may use at most 64 MiB of HBM per device.

```python
import jax
import jax.numpy as jnp
import numpy as np
from jax import lax

DIM = 256
TILE = 2048
PTS_DEV = 4096
NPTS = 262144
NPAIRS = 32
TB2 = 4
KMAX = 10
KMIN = 5


def draw_rank_source(key, part):
    base_key = jax.random.fold_in(key, 11)
    label_key, noise_key = jax.random.split(base_key)
    band_total = NPTS // PTS_DEV
    per_group = PTS_DEV // band_total
    pattern = jnp.repeat(jnp.arange(band_total, dtype=jnp.int32), per_group)
    shard_keys = jax.random.split(label_key, band_total)
    labels = jax.vmap(lambda shard_key: jax.random.permutation(shard_key, pattern))(shard_keys).reshape(NPTS)
    noise = jax.random.permutation(noise_key, NPTS).astype(jnp.int32)
    scores = labels * NPTS + noise
    return jnp.argsort(scores).astype(jnp.int32)


def draw_kept_tiles(key, part):
    base_key = jax.random.fold_in(key, 23)
    tile_span = TB2
    code_table = jnp.asarray(np.array([left_tile * tile_span + right_tile for left_tile in range(tile_span) for right_tile in range(left_tile, tile_span)], dtype=np.int32))
    shuffle_key, count_key, pick_key = jax.random.split(base_key, 3)
    shuffles = jax.vmap(lambda pair_key: jax.random.permutation(pair_key, KMAX))(jax.random.split(shuffle_key, NPAIRS))
    counts = jax.random.randint(count_key, (NPAIRS,), KMIN, KMAX + 1)
    full_pair = jax.random.randint(pick_key, (), 0, NPAIRS)
    pair_ids = jnp.arange(NPAIRS)
    counts = jnp.where(pair_ids == full_pair, KMAX, counts)
    counts = jnp.where(pair_ids == (full_pair + 1) % NPAIRS, KMIN, counts)
    slot_ids = jnp.arange(KMAX)[None, :]
    return jnp.where(slot_ids < counts[:, None], code_table[shuffles], -1).astype(jnp.int32)


def set_ends(entries, rng, low, largest):
    longest = entries.shape.index(max(entries.shape))
    spots = []
    for shift in (0, 1):
        where = [jax.random.randint(jax.random.fold_in(rng, axis), (), 0, length) for axis, length in enumerate(entries.shape)]
        where[longest] = (where[longest] + shift) % entries.shape[longest]
        spots.append(tuple(where))
    return entries.at[spots[0]].set(low).at[spots[1]].set(largest)


def steps_of(rng, dims, pieces, least, largest):
    gain = 1.0
    for axis_at, shards_of in pieces:
        steps = jax.random.uniform(jax.random.fold_in(jax.random.fold_in(rng, 6), axis_at), (shards_of,), jnp.float32, least / len(pieces), largest / len(pieces))
        gain = gain * jnp.repeat(jnp.exp(steps), dims[axis_at] // shards_of).reshape((-1,) + (1,) * (len(dims) - 1 - axis_at))
    return gain


def normal_values(stream_key, extent, spread, most, shards=(), kind=jnp.bfloat16):
    gain = steps_of(stream_key, extent, shards, -0.22, 0.18) if shards else 1.0
    entries = jax.random.normal(stream_key, extent, jnp.float32) * spread * gain
    return jnp.minimum(jnp.maximum(entries, -most), most).astype(kind)


def setup_inputs(seed: int = 0) -> dict:
    streams_of = jax.random.split(jax.random.key(seed), 5)
    return {
        "points": normal_values(streams_of[0], (NPTS, DIM), 1.0, 6.0, ((0, 64),)),
        "rank_source": draw_rank_source(jax.random.fold_in(streams_of[4], 71), 0),
        "thresholds": set_ends(jax.random.randint(streams_of[2], (NPTS,), 1000, 1400), jax.random.fold_in(streams_of[2], 1), 1000, 1399).astype(jnp.int32),
        "kept_tiles": draw_kept_tiles(jax.random.fold_in(streams_of[4], 71), 0),
    }


def inverse_norm(block):
    values = block.astype(jnp.float32)
    return lax.rsqrt(lax.optimization_barrier(jnp.sum(values * values, axis=1)) + 1e-06)

def cosine_tile(left_rows, right_rows, left_inv, right_inv, left_rad, right_rad, same_tile):
    products = lax.dot_general(left_rows, right_rows, (((1,), (1,)), ((), ())), preferred_element_type=jnp.float32)
    distance = 1.0 - products * left_inv[:, None] * right_inv[None, :]
    radius = jnp.minimum(left_rad[:, None], right_rad[None, :])
    weight = jnp.maximum(0.0, 1.0 - distance / radius)
    row_ids = lax.broadcasted_iota(jnp.int32, weight.shape, 0)
    col_ids = lax.broadcasted_iota(jnp.int32, weight.shape, 1)
    return jnp.where(same_tile & (row_ids == col_ids), 0.0, weight)

def reference(points, rank_source, thresholds, kept_tiles):
    tile_count = PTS_DEV // TILE
    tile_span = 2 * tile_count
    band_total = NPTS // PTS_DEV
    by_rank = points[rank_source]
    inverses = inverse_norm(by_rank)
    radius_all = thresholds.astype(jnp.float32) / 1024.0

    def tile_start(pair_index, tile_index):
        low_start = pair_index * PTS_DEV + tile_index * TILE
        high_start = (band_total - 1 - pair_index) * PTS_DEV + (tile_index - tile_count) * TILE
        return jnp.where(tile_index < tile_count, low_start, high_start).astype(jnp.int32)

    def visit(degree, scan_item):
        pair_index, tile_code = scan_item
        is_valid = (tile_code >= 0).astype(jnp.float32)
        safe_code = jnp.maximum(tile_code, 0)
        left_tile = safe_code // tile_span
        right_tile = safe_code % tile_span
        left_start = tile_start(pair_index, left_tile)
        right_start = tile_start(pair_index, right_tile)
        weight = cosine_tile(lax.dynamic_slice_in_dim(by_rank, left_start, TILE, 0), lax.dynamic_slice_in_dim(by_rank, right_start, TILE, 0), lax.dynamic_slice_in_dim(inverses, left_start, TILE, 0), lax.dynamic_slice_in_dim(inverses, right_start, TILE, 0), lax.dynamic_slice_in_dim(radius_all, left_start, TILE, 0), lax.dynamic_slice_in_dim(radius_all, right_start, TILE, 0), left_tile == right_tile)
        row_sums = lax.optimization_barrier(jnp.sum(weight, axis=1)) * is_valid
        col_sums = lax.optimization_barrier(jnp.sum(weight, axis=0)) * is_valid * (left_tile != right_tile).astype(jnp.float32)
        current = lax.dynamic_slice_in_dim(degree, left_start, TILE, 0)
        degree = lax.dynamic_update_slice_in_dim(degree, current + row_sums, left_start, 0)
        current = lax.dynamic_slice_in_dim(degree, right_start, TILE, 0)
        degree = lax.dynamic_update_slice_in_dim(degree, current + col_sums, right_start, 0)
        return (degree, None)
    pair_list = jnp.repeat(jnp.arange(NPAIRS, dtype=jnp.int32), KMAX)
    code_list = kept_tiles.reshape(-1).astype(jnp.int32)
    degree, unused = lax.scan(visit, jnp.zeros((NPTS,), jnp.float32), (pair_list, code_list))
    return degree / TILE
```

```python
import jax
import jax.numpy as jnp
from jax import lax
from jax.experimental import pallas as pl
from jax.experimental.pallas import tpu as pltpu
from jax.sharding import PartitionSpec as P

TILE = 2048
LANES = 128
VMEM_LIMIT = 48 * 1024 * 1024
NT = (((1,), (1,)), ((), ()))


def prefix_matrix():
    row = lax.broadcasted_iota(jnp.int32, (LANES, 2 * LANES), 0)
    col = lax.broadcasted_iota(jnp.int32, (LANES, 2 * LANES), 1)
    return jnp.where((row <= col) | (col >= LANES), 1.0, 0.0).astype(jnp.bfloat16)


def block_band(device):
    return device if device % 2 == 0 else 64 - device


def send_kernel(s_ref, rank_ref, points_ref, out_ref, pos_ref, loc_ref, acc_ref, row_ref, hot_ref):
    shard = s_ref[0]
    first = s_ref[1]
    prefix = prefix_matrix()
    carry = jnp.zeros((64, LANES), jnp.float32)
    base = (first + 1).astype(jnp.float32)
    for j in range(32):
        source = rank_ref[pl.ds(j, 64, stride=32), :]
        mine = (source >> 12) == shard
        counts = jnp.dot(
            jnp.where(mine, 1.0, 0.0).astype(jnp.bfloat16), prefix, preferred_element_type=jnp.float32
        )
        pos_ref[j] = jnp.where(mine, carry + counts[:, :LANES] - base, -1.0)
        loc_ref[j] = source & 4095
        carry = carry + counts[:, LANES:]

    @pl.loop(0, 8)
    def _(g):
        accs = [jnp.zeros((8, LANES), jnp.int32) for _ in range(16)]
        rows = pl.ds(pl.multiple_of(g * 8, 8), 8)
        for j in range(32):
            pos = pos_ref[j, rows, :]
            loc = loc_ref[j, rows, :]
            for s in range(16):
                accs[s] = jnp.where(pos == float(s), loc, accs[s])
        for s in range(16):
            acc_ref[pl.ds(pl.multiple_of(g * 128 + s * 8, 8), 8), :] = accs[s]

    ones = jnp.ones((LANES, LANES), jnp.bfloat16)
    acc = acc_ref[...]
    high = (acc >> 6).astype(jnp.float32).astype(jnp.bfloat16)
    low = (acc & 63).astype(jnp.float32).astype(jnp.bfloat16)
    row_ref[...] = 64.0 * jnp.dot(high, ones, preferred_element_type=jnp.float32) + jnp.dot(
        low, ones, preferred_element_type=jnp.float32
    )
    lane = lax.broadcasted_iota(jnp.int32, (256, LANES), 1).astype(jnp.float32)
    for blk in range(4):
        parts = []
        for i in range(16):
            band = block_band(blk * 16 + i)
            parts.append(row_ref[pl.ds((band // 8) * 128 + band % 8, 16, stride=8), :])
        local = jnp.concatenate(parts, axis=0)
        for ch in range(32):
            hot_ref[:, ch * 128 : (ch + 1) * 128] = jnp.where(
                local == lane + float(ch * 128), 1.0, 0.0
            ).astype(jnp.bfloat16)
        out_ref[blk * 256 : (blk + 1) * 256, :] = jnp.dot(
            hot_ref[...], points_ref[...], preferred_element_type=jnp.float32
        ).astype(jnp.bfloat16)


def send_rows(scalars, rank2d, points):
    return pl.pallas_call(
        send_kernel,
        out_shape=jax.ShapeDtypeStruct((1024, 256), jnp.bfloat16),
        in_specs=[
            pl.BlockSpec(memory_space=pltpu.SMEM),
            pl.BlockSpec(memory_space=pltpu.VMEM),
            pl.BlockSpec(memory_space=pltpu.VMEM),
        ],
        out_specs=pl.BlockSpec(memory_space=pltpu.VMEM),
        scratch_shapes=[
            pltpu.VMEM((32, 64, LANES), jnp.float32),
            pltpu.VMEM((32, 64, LANES), jnp.int32),
            pltpu.VMEM((1024, LANES), jnp.int32),
            pltpu.VMEM((1024, LANES), jnp.float32),
            pltpu.VMEM((256, 4096), jnp.bfloat16),
        ],
        compiler_params=pltpu.CompilerParams(vmem_limit_bytes=VMEM_LIMIT),
        name="send_rows",
    )(scalars, rank2d, points)


def place_kernel(s_ref, rank_ref, thr_ref, row_ref, col_ref, place_ref, u_ref, v_ref):
    rep = s_ref[2]
    prefix = prefix_matrix()
    shard_iota = lax.broadcasted_iota(jnp.int32, (64, LANES), 0)
    u_iota = lax.broadcasted_iota(jnp.int32, (32, LANES), 0)
    v_iota = lax.broadcasted_iota(jnp.int32, (LANES, LANES), 0)
    for x in range(3):
        start = pl.multiple_of(s_ref[3 + x] * 32, 32)
        carry = jnp.zeros((64, LANES), jnp.float32)
        source = rank_ref[pl.ds(start, 32), :] >> 12
        thr = thr_ref[pl.ds(start, 32), :]
        for j in range(32):
            shard = source[j : j + 1, :]
            hot = shard == shard_iota
            counts = jnp.dot(
                jnp.where(hot, 1.0, 0.0).astype(jnp.bfloat16), prefix, preferred_element_type=jnp.float32
            )
            slot = jnp.sum(jnp.where(hot, carry + counts[:, :LANES], 0.0), axis=0, keepdims=True)
            slot = slot.astype(jnp.int32) - 1
            carry = carry + counts[:, LANES:]
            quarter = slot >> 4
            v = (shard & 7) * 16 + (slot & 15)
            if x == 2:
                place_ref[j : j + 1, :] = (((rep - quarter) & 3) * 8 + (shard >> 3)) * 128 + v
            else:
                u = ((quarter - rep) & 3) * 8 + (shard >> 3)
                u_hot = u == u_iota
                t = thr[j : j + 1, :]
                lanes = slice(j * LANES, (j + 1) * LANES)
                u_ref[0:32, lanes] = jnp.where(u_hot, (t >> 4).astype(jnp.float32), 0.0).astype(jnp.bfloat16)
                u_ref[32:64, lanes] = jnp.where(u_hot, (t & 15).astype(jnp.float32), 0.0).astype(jnp.bfloat16)
                u_ref[64:96, lanes] = jnp.where(u_hot, float(j >= 16), 0.0).astype(jnp.bfloat16)
                v_ref[:, lanes] = jnp.where(v == v_iota, 1.0, 0.0).astype(jnp.bfloat16)
        if x < 2:
            us = u_ref[...]
            vs = v_ref[...]
            rows = lax.dot_general(us, vs, NT, preferred_element_type=jnp.float32)
            cols = lax.dot_general(vs, us, NT, preferred_element_type=jnp.float32)
            row_ref[x, 0:32, :] = 1024.0 / (rows[0:32] * 16.0 + rows[32:64])
            row_ref[x, 32:64, :] = rows[64:96]
            col_ref[x, :, 0:32] = 1024.0 / (cols[:, 0:32] * 16.0 + cols[:, 32:64])
            col_ref[x, :, 32:64] = cols[:, 64:96]


def place(scalars, rank2d, thr2d):
    return pl.pallas_call(
        place_kernel,
        out_shape=(
            jax.ShapeDtypeStruct((2, 64, LANES), jnp.float32),
            jax.ShapeDtypeStruct((2, LANES, 64), jnp.float32),
            jax.ShapeDtypeStruct((32, LANES), jnp.int32),
        ),
        in_specs=[
            pl.BlockSpec(memory_space=pltpu.SMEM),
            pl.BlockSpec(memory_space=pltpu.VMEM),
            pl.BlockSpec(memory_space=pltpu.VMEM),
        ],
        out_specs=(pl.BlockSpec(memory_space=pltpu.VMEM),) * 3,
        scratch_shapes=[
            pltpu.VMEM((96, 4096), jnp.bfloat16),
            pltpu.VMEM((LANES, 4096), jnp.bfloat16),
        ],
        compiler_params=pltpu.CompilerParams(vmem_limit_bytes=VMEM_LIMIT),
        cost_estimate=pl.CostEstimate(flops=2 * 10**9, bytes_accessed=10**7, transcendentals=0),
        name="place",
    )(scalars, rank2d, thr2d)


def square_parts(block):
    values = block.astype(jnp.float32)
    square = values * values
    high = square.astype(jnp.bfloat16)
    low = (square - high.astype(jnp.float32)).astype(jnp.bfloat16)
    return high, low


def inverse_column(high, low):
    ones = jnp.ones((256, LANES), jnp.bfloat16)
    total = jnp.dot(high, ones, preferred_element_type=jnp.float32)
    total = total + jnp.dot(low, ones, preferred_element_type=jnp.float32)
    return lax.rsqrt(total + 1e-06)


def inverse_row(high, low):
    ones = jnp.ones((8, 256), jnp.bfloat16)
    total = lax.dot_general(ones, high, NT, preferred_element_type=jnp.float32)
    total = total + lax.dot_general(ones, low, NT, preferred_element_type=jnp.float32)
    return lax.rsqrt(total + 1e-06)


def load_column_meta(slot, col_ref, band, quarter, dest_ref):
    for u in range(8):
        rows = slice(u * LANES, (u + 1) * LANES)
        at = quarter * 8 + u
        dest_ref[slot, 1, rows, :] = jnp.broadcast_to(col_ref[band, :, at : at + 1], (LANES, LANES))
        dest_ref[slot, 2, rows, :] = jnp.broadcast_to(col_ref[band, :, 32 + at : 33 + at], (LANES, LANES))


def load_row_meta(slot, row_ref, band, quarter, dest_ref):
    for u in range(8):
        lanes = slice(u * LANES, (u + 1) * LANES)
        at = quarter * 8 + u
        dest_ref[slot, 1, :, lanes] = jnp.broadcast_to(row_ref[band, at : at + 1, :], (8, LANES))
        dest_ref[slot, 2, :, lanes] = jnp.broadcast_to(row_ref[band, 32 + at : 33 + at, :], (8, LANES))


def keep_rows(keep_ref, row_offset, col_offset, row_meta_ref, slot, dest_ref):
    upper = row_meta_ref[slot, 2] > 0.5
    for t in range(2):
        at = (row_offset + t) * 4 + col_offset
        dest_ref[t] = jnp.where(upper, keep_ref[at + 1], keep_ref[at])


def weigh(left_ref, left_at, left_meta, left_slot, right_ref, right_at, right_meta, right_slot,
          keep, prod_ref, row_sum_ref, col_sum_ref, left_sum, right_sum, diagonal):
    prod_ref[...] = lax.dot_general(
        left_ref[pl.ds(left_at, 256), :], right_ref[pl.ds(right_at, 512), :], NT,
        preferred_element_type=jnp.float32,
    )

    def strip(i, sums):
        at = pl.multiple_of(i * 32, 32)
        rows = pl.ds(pl.multiple_of(left_at + at, 32), 32)
        inv_i = left_meta[left_slot, 0, rows, :]
        rho_i = left_meta[left_slot, 1, rows, :]
        upper = left_meta[left_slot, 2, rows, :] > 0.5
        total = row_sum_ref[left_sum, rows, :]
        out = []
        for ch in range(4):
            cols = pl.ds(pl.multiple_of(right_at + ch * LANES, LANES), LANES)
            inv_j = right_meta[right_slot, 0, 0:1, cols]
            rho_j = right_meta[right_slot, 1, 0:1, cols]
            kept = jnp.where(upper, keep[1, 0:1, cols], keep[0, 0:1, cols])
            p = prod_ref[pl.ds(at, 32), ch * LANES : (ch + 1) * LANES]
            near = (p * inv_i) * inv_j - 1.0
            w = jnp.maximum(near * jnp.maximum(rho_i, rho_j) + kept, 0.0)
            if diagonal:
                row_ids = left_at + at + lax.broadcasted_iota(jnp.int32, w.shape, 0)
                col_ids = right_at + ch * LANES + lax.broadcasted_iota(jnp.int32, w.shape, 1)
                w = jnp.where(row_ids == col_ids, 0.0, w)
            total = total + w
            if not diagonal:
                out.append(sums[ch] + ((w[0:8] + w[8:16]) + (w[16:24] + w[24:32])))
        row_sum_ref[left_sum, rows, :] = total
        return tuple(out)

    zeros = () if diagonal else tuple(jnp.zeros((8, LANES), jnp.float32) for _ in range(4))
    sums = lax.fori_loop(0, 8, strip, zeros)
    if not diagonal:
        for ch in range(4):
            cols = pl.ds(pl.multiple_of(right_at + ch * LANES, LANES), LANES)
            col_sum_ref[right_sum, :, cols] += sums[ch]


def rows_to_lanes(row_sum_ref, slot):
    row = lax.broadcasted_iota(jnp.int32, (LANES, LANES), 0)
    lane = lax.broadcasted_iota(jnp.int32, (LANES, LANES), 1)
    out = []
    for u in range(8):
        total = jnp.sum(row_sum_ref[slot, u * LANES : (u + 1) * LANES, :], axis=1, keepdims=True)
        out.append(jnp.sum(jnp.where(row == lane, total, 0.0), axis=0, keepdims=True))
    return out


def cols_to_lanes(col_sum_ref, slot):
    return [
        jnp.sum(col_sum_ref[slot, :, u * LANES : (u + 1) * LANES], axis=0, keepdims=True)
        for u in range(8)
    ]


def near_kernel(s_ref, keep_ref, own_ref, other_ref, row_ref, col_ref, out_ref,
                left_meta, right_meta, keep, prod_ref, row_sum, col_sum):
    core = s_ref[6]
    own_offset = s_ref[7]
    other_offset = s_ref[8]
    high, low = square_parts(own_ref[...])
    left_meta[0, 0] = inverse_column(high, low)
    right_meta[0, 0] = inverse_row(high, low)
    high, low = square_parts(other_ref[...])
    right_meta[1, 0] = inverse_row(high, low)
    load_column_meta(0, col_ref, 0, 0, left_meta)
    load_row_meta(0, row_ref, 0, 0, right_meta)
    load_row_meta(1, row_ref, 1, 0, right_meta)
    row_sum[...] = jnp.zeros_like(row_sum)
    col_sum[...] = jnp.zeros_like(col_sum)

    keep_rows(keep_ref, own_offset, own_offset, right_meta, 0, keep)

    @pl.loop(0, 8)
    def _(i):
        weigh(own_ref, pl.multiple_of((i >> 1) * 256, 256), left_meta, 0, own_ref,
              pl.multiple_of((i & 1) * 512, 512), right_meta, 0,
              keep, prod_ref, row_sum, col_sum, 0, 0, True)

    keep_rows(keep_ref, own_offset, other_offset, right_meta, 1, keep)

    @pl.loop(0, 4)
    def _(i):
        weigh(own_ref, pl.multiple_of(i * 256, 256), left_meta, 0, other_ref,
              pl.multiple_of(((i >> 1) ^ core) * 512, 512), right_meta, 1,
              keep, prod_ref, row_sum, col_sum, 0, 0, False)

    for u, value in enumerate(rows_to_lanes(row_sum, 0)):
        out_ref[0, u : u + 1, :] = value
    for u, value in enumerate(cols_to_lanes(col_sum, 0)):
        out_ref[1, u : u + 1, :] = value


def far_kernel(s_ref, keep_ref, own_ref, other_ref, right_ref, left_ref, row_ref, col_ref, near_ref,
               out_ref, left_meta, right_meta, keep, prod_ref, row_sum, col_sum):
    own_offset = s_ref[7]
    other_offset = s_ref[8]
    cross = s_ref[9]
    left_offset = s_ref[10]
    high, low = square_parts(own_ref[...])
    left_meta[0, 0] = inverse_column(high, low)
    high, low = square_parts(other_ref[...])
    left_meta[1, 0] = inverse_column(high, low)
    high, low = square_parts(left_ref[...])
    left_meta[2, 0] = inverse_column(high, low)
    high, low = square_parts(right_ref[...])
    right_meta[0, 0] = inverse_row(high, low)
    load_column_meta(0, col_ref, 0, 0, left_meta)
    load_column_meta(1, col_ref, 1, 0, left_meta)
    load_column_meta(2, col_ref, cross, 3, left_meta)
    load_row_meta(0, row_ref, 0, 1, right_meta)
    row_sum[...] = jnp.zeros_like(row_sum)
    col_sum[...] = jnp.zeros_like(col_sum)
    for slot, (block_ref, offset) in enumerate(
        ((own_ref, own_offset), (other_ref, other_offset), (left_ref, left_offset))
    ):
        keep_rows(keep_ref, offset, own_offset, right_meta, 0, keep)

        @pl.loop(0, 8)
        def _(i):
            weigh(block_ref, pl.multiple_of((i >> 1) * 256, 256), left_meta, slot, right_ref,
                  pl.multiple_of((i & 1) * 512, 512), right_meta, 0,
                  keep, prod_ref, row_sum, col_sum, slot, 0, False)

    for slot in range(3):
        for u, value in enumerate(rows_to_lanes(row_sum, slot)):
            if slot < 2:
                value = value + near_ref[slot, u : u + 1, :]
            out_ref[slot, u : u + 1, :] = value
    for u, value in enumerate(cols_to_lanes(col_sum, 0)):
        out_ref[3, u : u + 1, :] = value


def pair_scratch(lefts, rights):
    return [
        pltpu.VMEM((lefts, 3, 1024, LANES), jnp.float32),
        pltpu.VMEM((rights, 3, 8, 1024), jnp.float32),
        pltpu.VMEM((2, 8, 1024), jnp.float32),
        pltpu.VMEM((256, 512), jnp.float32),
        pltpu.VMEM((lefts, 1024, LANES), jnp.float32),
        pltpu.VMEM((1, 8, 1024), jnp.float32),
    ]


def smem():
    return pl.BlockSpec(memory_space=pltpu.SMEM)


def vmem():
    return pl.BlockSpec(memory_space=pltpu.VMEM)


def near_pairs(scalars, keep, own, other, rows, cols):
    return pl.pallas_call(
        near_kernel,
        out_shape=jax.ShapeDtypeStruct((2, 8, LANES), jnp.float32),
        in_specs=[smem(), smem(), vmem(), vmem(), vmem(), vmem()],
        out_specs=vmem(),
        scratch_shapes=pair_scratch(1, 2),
        compiler_params=pltpu.CompilerParams(vmem_limit_bytes=VMEM_LIMIT),
        cost_estimate=pl.CostEstimate(flops=2 * 10**9, bytes_accessed=10**7, transcendentals=0),
        name="near_pairs",
    )(scalars, keep, own, other, rows, cols)


def far_pairs(scalars, keep, own, other, right, left, rows, cols, near):
    return pl.pallas_call(
        far_kernel,
        out_shape=jax.ShapeDtypeStruct((4, 8, LANES), jnp.float32),
        in_specs=[smem(), smem()] + [vmem()] * 7,
        out_specs=vmem(),
        scratch_shapes=pair_scratch(3, 1),
        compiler_params=pltpu.CompilerParams(vmem_limit_bytes=VMEM_LIMIT),
        cost_estimate=pl.CostEstimate(flops=4 * 10**9, bytes_accessed=10**7, transcendentals=0),
        name="far_pairs",
    )(scalars, keep, own, other, right, left, rows, cols, near)


def rank_kernel(place_ref, a_ref, b_ref, c_ref, d_ref, out_ref):
    place_at = place_ref[...]
    lane = place_at & 127
    which = place_at >> 7
    total = jnp.zeros((32, LANES), jnp.float32)
    for s, piece in enumerate((a_ref, b_ref, c_ref, d_ref)):
        for u in range(8):
            row = jnp.broadcast_to(piece[u : u + 1, :], (32, LANES))
            value = jnp.take_along_axis(row, lane, axis=1)
            total = jnp.where(which == s * 8 + u, value, total)
    out_ref[...] = total * (1.0 / TILE)


def to_rank_order(place_at, pieces):
    return pl.pallas_call(
        rank_kernel,
        out_shape=jax.ShapeDtypeStruct((32, LANES), jnp.float32),
        in_specs=[vmem()] * 5,
        out_specs=vmem(),
        name="to_rank_order",
    )(place_at, *pieces)


def on_device(points, rank_source, thresholds, kept_tiles):
    bands = lax.axis_size("band")
    reps = lax.axis_size("rep")
    device = lax.axis_index("band").astype(jnp.int32)
    rep = lax.axis_index("rep").astype(jnp.int32)
    core = device & 1
    own_band = jnp.where(core == 0, device, bands - device)
    other_band = bands - 1 - own_band
    own_offset = jnp.where(own_band < bands // 2, 0, 2)
    other_offset = 2 - own_offset
    cross = (rep >= 2).astype(jnp.int32)
    left_offset = jnp.where(cross == 1, other_offset, own_offset)
    scalars = jnp.stack([
        device, rep * 16, rep, own_band, other_band, device, core,
        own_offset, other_offset, cross, left_offset,
    ]).astype(jnp.int32)
    codes = lax.dynamic_index_in_dim(kept_tiles, jnp.minimum(own_band, other_band), 0, keepdims=False)
    ids = jnp.arange(16, dtype=jnp.int32)
    a, c = ids // 4, ids % 4
    wanted = jnp.minimum(a, c) * 4 + jnp.maximum(a, c)
    keep = jnp.where(jnp.any(codes[:, None] == wanted[None, :], axis=0), 1.0, -1e30).astype(jnp.float32)

    rank2d = rank_source.reshape(2048, LANES)
    thr2d = thresholds.reshape(2048, LANES)

    def joint(move):
        return [
            (d * reps + r, e * reps + q)
            for d in range(bands)
            for r in range(reps)
            for e, q in (move(d, r),)
        ]

    def shift(value, move):
        return lax.ppermute(value, ("band", "rep"), joint(move))

    payload = send_rows(scalars, rank2d, points)
    own = lax.all_to_all(
        payload.reshape(bands, 16, 256), "band", split_axis=0, concat_axis=0, tiled=True
    ).reshape(1024, 256)
    rows, cols, place_at = place(scalars, rank2d, thr2d)

    def to_right(d, r):
        q = (r + 1) % reps
        return (d if q < 2 else d ^ 1), q

    other = shift(own, lambda d, r: (d ^ 1, r))
    right = shift(own, lambda d, r: (d, (r - 1) % reps))
    left = shift(own, to_right)

    near = near_pairs(scalars, keep, own, other, rows, cols)
    sums = far_pairs(scalars, keep, own, other, right, left, rows, cols, near)

    def from_left(d, r):
        return (d if r < 2 else d ^ 1), (r - 1) % reps

    total = sums[0] + shift(sums[1], lambda d, r: (d ^ 1, r))
    total = total + shift(sums[2], from_left)
    total = total + shift(sums[3], lambda d, r: (d, (r + 1) % reps))

    pieces = [
        shift(total, lambda d, r, s=s: (block_band(d), (r + s) % reps)) for s in range(reps)
    ]
    return to_rank_order(place_at, pieces).reshape(points.shape[0])


def solution(mesh):
    in_specs = (P("band", None), P(), P(), P())
    out_specs = P("band")
    return jax.shard_map(
        on_device, mesh=mesh, in_specs=in_specs, out_specs=out_specs, check_vma=False
    )
```

```python
import jax
import jax.numpy as jnp
from jax import lax
from jax.experimental import pallas as pl
from jax.experimental.pallas import tpu as pltpu
from jax.sharding import PartitionSpec as P

TILE = 2048
LANES = 128
VMEM_LIMIT = 48 * 1024 * 1024
NT = (((1,), (1,)), ((), ()))


def prefix_matrix():
    row = lax.broadcasted_iota(jnp.int32, (LANES, 2 * LANES), 0)
    col = lax.broadcasted_iota(jnp.int32, (LANES, 2 * LANES), 1)
    return jnp.where((row <= col) | (col >= LANES), 1.0, 0.0).astype(jnp.bfloat16)


def block_band(device):
    return device if device % 2 == 0 else 64 - device


def smem():
    return pl.BlockSpec(memory_space=pltpu.SMEM)


def vmem():
    return pl.BlockSpec(memory_space=pltpu.VMEM)


def hbm():
    return pl.BlockSpec(memory_space=pltpu.HBM)


def send_kernel(s_ref, rank_hbm, points_hbm, out_ref, rank_ref, points_ref, acc_ref, row_ref,
                hot_a, hot_b, rank_sem, points_sem):
    def fetch_rank(g):
        rows = pl.ds(g * 256, 256)
        return pltpu.make_async_copy(rank_hbm.at[rows, :], rank_ref.at[rows, :], rank_sem.at[g])

    for g in range(8):
        fetch_rank(g).start()
    fetch_points = pltpu.make_async_copy(points_hbm, points_ref, points_sem)
    fetch_points.start()
    shard = s_ref[0]
    prefix = prefix_matrix()
    base = (s_ref[1] + 1).astype(jnp.float32)
    ones = jnp.ones((LANES, LANES), jnp.bfloat16)
    for g in range(8):
        fetch_rank(g).wait()
        source = [rank_ref[pl.ds(g * 256 + j, 8, stride=32), :] for j in range(32)]
        mine = [(source[j] >> 12) == shard for j in range(32)]
        marks = jnp.concatenate([jnp.where(m, 1.0, 0.0) for m in mine], axis=0).astype(jnp.bfloat16)
        counts = jnp.dot(marks, prefix, preferred_element_type=jnp.float32)
        carry = jnp.zeros((8, LANES), jnp.float32) - base
        accs = [jnp.zeros((8, LANES), jnp.int32) for _ in range(16)]
        for j in range(32):
            pos = jnp.where(mine[j], carry + counts[j * 8 : j * 8 + 8, :LANES], -1.0)
            loc = source[j] & 4095
            carry = carry + counts[j * 8 : j * 8 + 8, LANES:]
            for i in range(16):
                accs[i] = jnp.where(pos == float(i), loc, accs[i])
        for i in range(16):
            acc_ref[g * 128 + i * 8 : g * 128 + i * 8 + 8, :] = accs[i]

    acc = acc_ref[...]
    high = (acc >> 6).astype(jnp.float32).astype(jnp.bfloat16)
    low = (acc & 63).astype(jnp.float32).astype(jnp.bfloat16)
    row_ref[...] = 64.0 * jnp.dot(high, ones, preferred_element_type=jnp.float32) + jnp.dot(
        low, ones, preferred_element_type=jnp.float32
    )
    fetch_points.wait()
    lane = lax.broadcasted_iota(jnp.int32, (256, LANES), 1)
    one = jnp.ones((256, LANES), jnp.bfloat16)
    zero = jnp.zeros((256, LANES), jnp.bfloat16)
    for blk in range(4):
        hot_ref = hot_a if blk % 2 == 0 else hot_b
        parts = []
        for i in range(16):
            band = block_band(blk * 16 + i)
            parts.append(row_ref[pl.ds((band // 8) * 128 + band % 8, 16, stride=8), :])
        local = jnp.concatenate(parts, axis=0).astype(jnp.int32)
        chunk = (local >> 7).astype(jnp.float32).astype(jnp.bfloat16)
        hot = jnp.where((local & 127) == lane, 1.0, 0.0).astype(jnp.bfloat16)
        for ch in range(32):
            hot_ref[:, ch * 128 : (ch + 1) * 128] = jnp.where(chunk == one * ch, hot, zero)
        out_ref[blk * 256 : (blk + 1) * 256, :] = jnp.dot(
            hot_ref[...], points_ref[...], preferred_element_type=jnp.float32
        ).astype(jnp.bfloat16)


def send_rows(scalars, rank2d, points):
    return pl.pallas_call(
        send_kernel,
        out_shape=jax.ShapeDtypeStruct((1024, 256), jnp.bfloat16),
        in_specs=[smem(), hbm(), hbm()],
        out_specs=vmem(),
        scratch_shapes=[
            pltpu.VMEM((2048, LANES), jnp.int32),
            pltpu.VMEM((4096, 256), jnp.bfloat16),
            pltpu.VMEM((1024, LANES), jnp.int32),
            pltpu.VMEM((1024, LANES), jnp.float32),
            pltpu.VMEM((256, 4096), jnp.bfloat16),
            pltpu.VMEM((256, 4096), jnp.bfloat16),
            pltpu.SemaphoreType.DMA((8,)),
            pltpu.SemaphoreType.DMA,
        ],
        compiler_params=pltpu.CompilerParams(vmem_limit_bytes=VMEM_LIMIT),
        name="send_rows",
    )(scalars, rank2d, points)


def place_kernel(s_ref, rank_ref, thr_ref, row_ref, col_ref, place_ref, u_ref, v_ref):
    rep = s_ref[2]
    prefix = prefix_matrix()
    shard_iota = lax.broadcasted_iota(jnp.int32, (64, LANES), 0)
    u_iota = lax.broadcasted_iota(jnp.int32, (32, LANES), 0)
    v_iota = lax.broadcasted_iota(jnp.int32, (LANES, LANES), 0)
    for x in range(3):
        start = pl.multiple_of(s_ref[3 + x] * 32, 32)
        carry = jnp.zeros((64, LANES), jnp.float32)
        source = rank_ref[pl.ds(start, 32), :] >> 12
        thr = thr_ref[pl.ds(start, 32), :]
        for j in range(32):
            shard = source[j : j + 1, :]
            hot = shard == shard_iota
            counts = jnp.dot(
                jnp.where(hot, 1.0, 0.0).astype(jnp.bfloat16), prefix, preferred_element_type=jnp.float32
            )
            slot = jnp.sum(jnp.where(hot, carry + counts[:, :LANES], 0.0), axis=0, keepdims=True)
            slot = slot.astype(jnp.int32) - 1
            carry = carry + counts[:, LANES:]
            quarter = slot >> 4
            v = (shard & 7) * 16 + (slot & 15)
            if x == 2:
                place_ref[j : j + 1, :] = (((rep - quarter) & 3) * 8 + (shard >> 3)) * 128 + v
            else:
                u = ((quarter - rep) & 3) * 8 + (shard >> 3)
                u_hot = u == u_iota
                t = thr[j : j + 1, :]
                lanes = slice(j * LANES, (j + 1) * LANES)
                u_ref[0:32, lanes] = jnp.where(u_hot, (t >> 4).astype(jnp.float32), 0.0).astype(jnp.bfloat16)
                u_ref[32:64, lanes] = jnp.where(u_hot, (t & 15).astype(jnp.float32), 0.0).astype(jnp.bfloat16)
                u_ref[64:96, lanes] = jnp.where(u_hot, float(j >= 16), 0.0).astype(jnp.bfloat16)
                v_ref[:, lanes] = jnp.where(v == v_iota, 1.0, 0.0).astype(jnp.bfloat16)
        if x < 2:
            us = u_ref[...]
            vs = v_ref[...]
            rows = lax.dot_general(us, vs, NT, preferred_element_type=jnp.float32)
            cols = lax.dot_general(vs, us, NT, preferred_element_type=jnp.float32)
            row_ref[x, 0:32, :] = 1024.0 / (rows[0:32] * 16.0 + rows[32:64])
            row_ref[x, 32:64, :] = rows[64:96]
            col_ref[x, :, 0:32] = 1024.0 / (cols[:, 0:32] * 16.0 + cols[:, 32:64])
            col_ref[x, :, 32:64] = cols[:, 64:96]


def place(scalars, rank2d, thr2d):
    return pl.pallas_call(
        place_kernel,
        out_shape=(
            jax.ShapeDtypeStruct((2, 64, LANES), jnp.float32),
            jax.ShapeDtypeStruct((2, LANES, 64), jnp.float32),
            jax.ShapeDtypeStruct((32, LANES), jnp.int32),
        ),
        in_specs=[
            pl.BlockSpec(memory_space=pltpu.SMEM),
            pl.BlockSpec(memory_space=pltpu.VMEM),
            pl.BlockSpec(memory_space=pltpu.VMEM),
        ],
        out_specs=(pl.BlockSpec(memory_space=pltpu.VMEM),) * 3,
        scratch_shapes=[
            pltpu.VMEM((96, 4096), jnp.bfloat16),
            pltpu.VMEM((LANES, 4096), jnp.bfloat16),
        ],
        compiler_params=pltpu.CompilerParams(vmem_limit_bytes=VMEM_LIMIT),
        cost_estimate=pl.CostEstimate(flops=2 * 10**9, bytes_accessed=10**7, transcendentals=0),
        name="place",
    )(scalars, rank2d, thr2d)


def square_sums(block):
    values = block.astype(jnp.float32)
    square = values * values
    total = square[:, :LANES] + square[:, LANES:]
    high = total.astype(jnp.bfloat16)
    rest = total - high.astype(jnp.float32)
    middle = rest.astype(jnp.bfloat16)
    low = (rest - middle.astype(jnp.float32)).astype(jnp.bfloat16)
    return high, middle, low


def inverse_column(terms):
    ones = jnp.ones((LANES, LANES), jnp.bfloat16)
    high, middle, low = (jnp.dot(t, ones, preferred_element_type=jnp.float32) for t in terms)
    return lax.rsqrt(high + (middle + low) + 1e-06)


def inverse_row(terms):
    ones = jnp.ones((8, LANES), jnp.bfloat16)
    high, middle, low = (
        lax.dot_general(ones, t, NT, preferred_element_type=jnp.float32) for t in terms
    )
    return lax.rsqrt(high + (middle + low) + 1e-06)


def load_column_meta(at, col_ref, band, quarter, meta):
    for u in range(8):
        rows = slice(at + u * LANES, at + (u + 1) * LANES)
        i = quarter * 8 + u
        meta[1, rows, :] = jnp.broadcast_to(col_ref[band, :, i : i + 1], (LANES, LANES))
        meta[2, rows, :] = jnp.broadcast_to(col_ref[band, :, 32 + i : 33 + i], (LANES, LANES))


def load_row_meta(slot, row_ref, band, quarter, meta):
    for u in range(8):
        lanes = slice(u * LANES, (u + 1) * LANES)
        i = quarter * 8 + u
        meta[slot, 1, :, lanes] = jnp.broadcast_to(row_ref[band, i : i + 1, :], (8, LANES))
        meta[slot, 2, :, lanes] = jnp.broadcast_to(row_ref[band, 32 + i : 33 + i, :], (8, LANES))


def keep_rows(keep_ref, row_offset, col_offset, row_meta, slot, keep, at):
    upper = row_meta[slot, 2] > 0.5
    for t in range(2):
        code = (row_offset + t) * 4 + col_offset
        keep[at, t] = jnp.where(upper, keep_ref[code + 1], keep_ref[code])


def product(left_ref, left_at, right_ref, right_at, prod_ref):
    prod_ref[...] = lax.dot_general(
        left_ref[pl.ds(left_at, 256), :], right_ref[pl.ds(right_at, 512), :], NT,
        preferred_element_type=jnp.float32,
    )


def weigh(prod_ref, left_at, left_meta, right_at, right_meta, slot, keep, keep_at, row_sum, col_sum,
          diagonal):
    sums = [jnp.zeros((8, LANES), jnp.float32) for _ in range(4)]
    lanes = [pl.ds(pl.multiple_of(right_at + ch * LANES, LANES), LANES) for ch in range(4)]
    for i in range(8):
        rows = pl.ds(pl.multiple_of(left_at + i * 32, 32), 32)
        inv_i = left_meta[0, rows, :].reshape(4, 8, LANES)
        rho_i = left_meta[1, rows, :].reshape(4, 8, LANES)
        upper = left_meta[2, rows, :].reshape(4, 8, LANES) > 0.5
        total = row_sum[rows, :].reshape(4, 8, LANES)
        for ch in range(4):
            inv_j = right_meta[slot, 0, :, lanes[ch]][None]
            rho_j = right_meta[slot, 1, :, lanes[ch]][None]
            kept = jnp.where(upper, keep[keep_at, 1, :, lanes[ch]][None], keep[keep_at, 0, :, lanes[ch]][None])
            p = prod_ref[i * 32 : i * 32 + 32, ch * LANES : (ch + 1) * LANES].reshape(4, 8, LANES)
            near = (p * inv_i) * inv_j - 1.0
            w = jnp.maximum(near * jnp.maximum(rho_i, rho_j) + kept, 0.0)
            if diagonal:
                row_ids = lax.broadcasted_iota(jnp.int32, w.shape, 0) * 8 + lax.broadcasted_iota(jnp.int32, w.shape, 1)
                col_ids = lax.broadcasted_iota(jnp.int32, w.shape, 2)
                w = jnp.where(row_ids + (left_at + i * 32) == col_ids + (right_at + ch * LANES), 0.0, w)
            total = total + w
            if not diagonal:
                sums[ch] = sums[ch] + ((w[0] + w[1]) + (w[2] + w[3]))
        row_sum[rows, :] = total.reshape(32, LANES)
    if not diagonal:
        for ch in range(4):
            col_sum[:, lanes[ch]] += sums[ch]


def rows_to_lanes(row_sum, at):
    row = lax.broadcasted_iota(jnp.int32, (LANES, LANES), 0)
    lane = lax.broadcasted_iota(jnp.int32, (LANES, LANES), 1)
    out = []
    for u in range(8):
        total = jnp.sum(row_sum[at + u * LANES : at + (u + 1) * LANES, :], axis=1, keepdims=True)
        out.append(jnp.sum(jnp.where(row == lane, total, 0.0), axis=0, keepdims=True))
    return out


def cols_to_lanes(col_sum):
    return [
        jnp.sum(col_sum[:, u * LANES : (u + 1) * LANES], axis=0, keepdims=True) for u in range(8)
    ]


def near_kernel(s_ref, keep_ref, own_ref, other_ref, row_ref, col_ref, out_ref,
                left_meta, right_meta, keep, prod_a, prod_b, row_sum, col_sum):
    core = s_ref[6]
    own_offset = s_ref[7]
    other_offset = s_ref[8]
    terms = square_sums(own_ref[...])
    left_meta[0] = inverse_column(terms)
    right_meta[0, 0] = inverse_row(terms)
    right_meta[1, 0] = inverse_row(square_sums(other_ref[...]))
    load_column_meta(0, col_ref, 0, 0, left_meta)
    load_row_meta(0, row_ref, 0, 0, right_meta)
    load_row_meta(1, row_ref, 1, 0, right_meta)
    row_sum[...] = jnp.zeros_like(row_sum)
    col_sum[...] = jnp.zeros_like(col_sum)
    keep_rows(keep_ref, own_offset, own_offset, right_meta, 0, keep, 0)
    keep_rows(keep_ref, own_offset, other_offset, right_meta, 1, keep, 1)

    @pl.loop(0, 4)
    def _(i):
        at = pl.multiple_of(i * 256, 256)
        half = pl.multiple_of(((i >> 1) ^ core) * 512, 512)
        product(own_ref, at, own_ref, 0, prod_a)
        product(own_ref, at, own_ref, 512, prod_b)
        weigh(prod_a, at, left_meta, 0, right_meta, 0, keep, 0, row_sum, col_sum, True)
        product(own_ref, at, other_ref, half, prod_a)
        weigh(prod_b, at, left_meta, 512, right_meta, 0, keep, 0, row_sum, col_sum, True)
        weigh(prod_a, at, left_meta, half, right_meta, 1, keep, 1, row_sum, col_sum, False)

    for u, value in enumerate(rows_to_lanes(row_sum, 0)):
        out_ref[0, u : u + 1, :] = value
    for u, value in enumerate(cols_to_lanes(col_sum)):
        out_ref[1, u : u + 1, :] = value


def far_kernel(s_ref, keep_ref, own_hbm, other_hbm, left_hbm, right_ref, row_ref, col_ref, near_ref,
               stay_ref, move_ref, block_ref, left_meta, right_meta, keep, prod_a, prod_b, row_sum,
               col_sum, sems):
    own_offset = s_ref[7]
    other_offset = s_ref[8]
    cross = s_ref[9]
    left_offset = s_ref[10]
    copies = [
        pltpu.make_async_copy(source, block_ref.at[pl.ds(i * 1024, 1024), :], sems.at[i])
        for i, source in enumerate((own_hbm, other_hbm, left_hbm))
    ]
    for copy in copies:
        copy.start()
    right_meta[0, 0] = inverse_row(square_sums(right_ref[...]))
    load_column_meta(0, col_ref, 0, 0, left_meta)
    load_column_meta(1024, col_ref, 1, 0, left_meta)
    load_column_meta(2048, col_ref, cross, 3, left_meta)
    load_row_meta(0, row_ref, 0, 1, right_meta)
    for i, offset in enumerate((own_offset, other_offset, left_offset)):
        keep_rows(keep_ref, offset, own_offset, right_meta, 0, keep, i)
    row_sum[...] = jnp.zeros_like(row_sum)
    col_sum[...] = jnp.zeros_like(col_sum)
    for i, copy in enumerate(copies):
        copy.wait()
        left_meta[0, i * 1024 : (i + 1) * 1024, :] = inverse_column(
            square_sums(block_ref[i * 1024 : (i + 1) * 1024, :])
        )
    product(block_ref, 0, right_ref, 0, prod_a)

    @pl.loop(0, 12)
    def _(i):
        at = pl.multiple_of(i * 256, 256)
        after = pl.multiple_of(jnp.minimum(i + 1, 11) * 256, 256)
        block = i >> 2
        product(block_ref, at, right_ref, 512, prod_b)
        weigh(prod_a, at, left_meta, 0, right_meta, 0, keep, block, row_sum, col_sum, False)
        product(block_ref, after, right_ref, 0, prod_a)
        weigh(prod_b, at, left_meta, 512, right_meta, 0, keep, block, row_sum, col_sum, False)

    own = rows_to_lanes(row_sum, 0)
    other = rows_to_lanes(row_sum, 1024)
    left = rows_to_lanes(row_sum, 2048)
    right = cols_to_lanes(col_sum)
    for u in range(8):
        row = slice(u, u + 1)
        stay_ref[0, row, :] = own[u] + near_ref[0, row, :]
        stay_ref[1, row, :] = right[u]
        stay_ref[2, row, :] = jnp.where(cross == 0, left[u], 0.0)
        move_ref[0, row, :] = other[u] + near_ref[1, row, :]
        move_ref[1, row, :] = jnp.where(cross == 0, 0.0, left[u])


def pair_scratch(lefts, rights, keeps):
    return [
        pltpu.VMEM((3, lefts * 1024, LANES), jnp.float32),
        pltpu.VMEM((rights, 3, 8, 1024), jnp.float32),
        pltpu.VMEM((keeps, 2, 8, 1024), jnp.float32),
        pltpu.VMEM((256, 512), jnp.float32),
        pltpu.VMEM((256, 512), jnp.float32),
        pltpu.VMEM((lefts * 1024, LANES), jnp.float32),
        pltpu.VMEM((8, 1024), jnp.float32),
    ]


def near_pairs(scalars, keep, own, other, rows, cols):
    return pl.pallas_call(
        near_kernel,
        out_shape=jax.ShapeDtypeStruct((2, 8, LANES), jnp.float32),
        in_specs=[smem(), smem(), vmem(), vmem(), vmem(), vmem()],
        out_specs=vmem(),
        scratch_shapes=pair_scratch(1, 2, 2),
        compiler_params=pltpu.CompilerParams(vmem_limit_bytes=VMEM_LIMIT),
        cost_estimate=pl.CostEstimate(flops=2 * 10**9, bytes_accessed=10**7, transcendentals=0),
        name="near_pairs",
    )(scalars, keep, own, other, rows, cols)


def far_pairs(scalars, keep, own, other, left, right, rows, cols, near):
    return pl.pallas_call(
        far_kernel,
        out_shape=(
            jax.ShapeDtypeStruct((3, 8, LANES), jnp.float32),
            jax.ShapeDtypeStruct((2, 8, LANES), jnp.float32),
        ),
        in_specs=[smem(), smem(), hbm(), hbm(), hbm()] + [vmem()] * 4,
        out_specs=(vmem(), vmem()),
        scratch_shapes=[pltpu.VMEM((3072, 256), jnp.bfloat16)]
        + pair_scratch(3, 1, 3)
        + [pltpu.SemaphoreType.DMA((3,))],
        compiler_params=pltpu.CompilerParams(vmem_limit_bytes=VMEM_LIMIT),
        cost_estimate=pl.CostEstimate(flops=4 * 10**9, bytes_accessed=10**7, transcendentals=0),
        name="far_pairs",
    )(scalars, keep, own, other, left, right, rows, cols, near)


def rank_kernel(place_ref, *refs):
    pieces, out_ref = refs[:-1], refs[-1]
    place_at = place_ref[...]
    lane = place_at & 127
    which = place_at >> 7
    total = jnp.zeros((32, LANES), jnp.float32)
    for s in range(4):
        block = pieces[s][0] + pieces[(s + 1) % 4][1] + pieces[(s + 3) % 4][2]
        for u in range(8):
            row = jnp.broadcast_to(block[u : u + 1, :], (32, LANES))
            value = jnp.take_along_axis(row, lane, axis=1)
            total = jnp.where(which == s * 8 + u, value, total)
    out_ref[...] = total * (1.0 / TILE)


def to_rank_order(place_at, pieces):
    return pl.pallas_call(
        rank_kernel,
        out_shape=jax.ShapeDtypeStruct((32, LANES), jnp.float32),
        in_specs=[vmem()] * 5,
        out_specs=vmem(),
        name="to_rank_order",
    )(place_at, *pieces)


def on_device(points, rank_source, thresholds, kept_tiles):
    bands = lax.axis_size("band")
    reps = lax.axis_size("rep")
    device = lax.axis_index("band").astype(jnp.int32)
    rep = lax.axis_index("rep").astype(jnp.int32)
    core = device & 1
    own_band = jnp.where(core == 0, device, bands - device)
    other_band = bands - 1 - own_band
    own_offset = jnp.where(own_band < bands // 2, 0, 2)
    other_offset = 2 - own_offset
    cross = (rep >= 2).astype(jnp.int32)
    left_offset = jnp.where(cross == 1, other_offset, own_offset)
    scalars = jnp.stack([
        device, rep * 16, rep, own_band, other_band, device, core,
        own_offset, other_offset, cross, left_offset,
    ]).astype(jnp.int32)
    codes = lax.dynamic_index_in_dim(kept_tiles, jnp.minimum(own_band, other_band), 0, keepdims=False)
    ids = jnp.arange(16, dtype=jnp.int32)
    a, c = ids // 4, ids % 4
    wanted = jnp.minimum(a, c) * 4 + jnp.maximum(a, c)
    keep = jnp.where(jnp.any(codes[:, None] == wanted[None, :], axis=0), 1.0, -1e30).astype(jnp.float32)

    rank2d = rank_source.reshape(2048, LANES)
    thr2d = thresholds.reshape(2048, LANES)

    def joint(move):
        return [
            (d * reps + r, e * reps + q)
            for d in range(bands)
            for r in range(reps)
            for e, q in (move(d, r),)
        ]

    def shift(value, move):
        return lax.ppermute(value, ("band", "rep"), joint(move))

    payload = send_rows(scalars, rank2d, points)
    own = lax.all_to_all(
        payload.reshape(bands, 16, 256), "band", split_axis=0, concat_axis=0, tiled=True
    ).reshape(1024, 256)
    own, rows, cols, place_at = lax.optimization_barrier((own, *place(scalars, rank2d, thr2d)))

    def to_right(d, r):
        q = (r + 1) % reps
        return (d if q < 2 else d ^ 1), q

    other = shift(own, lambda d, r: (d ^ 1, r))
    right = shift(own, lambda d, r: (d, (r - 1) % reps))
    left = shift(own, to_right)

    near = near_pairs(scalars, keep, own, other, rows, cols)
    stay, move = far_pairs(scalars, keep, own, other, left, right, rows, cols, near)
    moved = shift(move, lambda d, r: (d ^ 1, r))
    sums = stay + jnp.stack([moved[0], jnp.zeros_like(moved[0]), moved[1]])
    home = shift(sums, lambda d, r: (block_band(d), r))
    pieces = [home] + [
        shift(home, lambda d, r, s=s: (d, (r + s) % reps)) for s in range(1, reps)
    ]
    return to_rank_order(place_at, pieces).reshape(points.shape[0])


def solution(mesh):
    in_specs = (P("band", None), P(), P(), P())
    out_specs = P("band")
    return jax.shard_map(
        on_device, mesh=mesh, in_specs=in_specs, out_specs=out_specs, check_vma=False
    )
```

```python
import jax
import jax.numpy as jnp
from jax import lax
from jax.experimental import pallas as pl
from jax.experimental.pallas import tpu as pltpu
from jax.sharding import PartitionSpec as P

TILE = 2048
LANES = 128
VMEM_LIMIT = 60 * 1024 * 1024
NT = (((1,), (1,)), ((), ()))


def prefix_matrix():
    row = lax.broadcasted_iota(jnp.int32, (LANES, 2 * LANES), 0)
    col = lax.broadcasted_iota(jnp.int32, (LANES, 2 * LANES), 1)
    return jnp.where((row <= col) | (col >= LANES), 1.0, 0.0).astype(jnp.bfloat16)


def block_band(device):
    return device if device % 2 == 0 else 64 - device


def smem():
    return pl.BlockSpec(memory_space=pltpu.SMEM)


def vmem():
    return pl.BlockSpec(memory_space=pltpu.VMEM)


def hbm():
    return pl.BlockSpec(memory_space=pltpu.HBM)


def send_kernel(s_ref, rank_hbm, points_hbm, out_ref, rank_ref, points_ref, acc_ref, row_ref,
                hot_a, hot_b, rank_sem, points_sem):
    def fetch_rank(g):
        rows = pl.ds(g * 256, 256)
        return pltpu.make_async_copy(rank_hbm.at[rows, :], rank_ref.at[rows, :], rank_sem.at[g])

    for g in range(8):
        fetch_rank(g).start()
    fetch_points = pltpu.make_async_copy(points_hbm, points_ref, points_sem)
    fetch_points.start()
    shard = s_ref[0]
    prefix = prefix_matrix()
    base = (s_ref[1] + 1).astype(jnp.float32)
    ones = jnp.ones((LANES, LANES), jnp.bfloat16)
    for g in range(8):
        fetch_rank(g).wait()
        source = [rank_ref[pl.ds(g * 256 + j, 8, stride=32), :] for j in range(32)]
        mine = [(source[j] >> 12) == shard for j in range(32)]
        marks = jnp.concatenate([jnp.where(m, 1.0, 0.0) for m in mine], axis=0).astype(jnp.bfloat16)
        counts = jnp.dot(marks, prefix, preferred_element_type=jnp.float32)
        carry = jnp.zeros((8, LANES), jnp.float32) - base
        accs = [jnp.zeros((8, LANES), jnp.int32) for _ in range(16)]
        for j in range(32):
            pos = jnp.where(mine[j], carry + counts[j * 8 : j * 8 + 8, :LANES], -1.0)
            loc = source[j] & 4095
            carry = carry + counts[j * 8 : j * 8 + 8, LANES:]
            for i in range(16):
                accs[i] = jnp.where(pos == float(i), loc, accs[i])
        for i in range(16):
            acc_ref[g * 128 + i * 8 : g * 128 + i * 8 + 8, :] = accs[i]

    acc = acc_ref[...]
    high = (acc >> 6).astype(jnp.float32).astype(jnp.bfloat16)
    low = (acc & 63).astype(jnp.float32).astype(jnp.bfloat16)
    row_ref[...] = 64.0 * jnp.dot(high, ones, preferred_element_type=jnp.float32) + jnp.dot(
        low, ones, preferred_element_type=jnp.float32
    )
    fetch_points.wait()
    lane = lax.broadcasted_iota(jnp.int32, (256, LANES), 1)
    one = jnp.ones((256, LANES), jnp.bfloat16)
    zero = jnp.zeros((256, LANES), jnp.bfloat16)
    for blk in range(4):
        hot_ref = hot_a if blk % 2 == 0 else hot_b
        parts = []
        for i in range(16):
            band = block_band(blk * 16 + i)
            parts.append(row_ref[pl.ds((band // 8) * 128 + band % 8, 16, stride=8), :])
        local = jnp.concatenate(parts, axis=0).astype(jnp.int32)
        chunk = (local >> 7).astype(jnp.float32).astype(jnp.bfloat16)
        hot = jnp.where((local & 127) == lane, 1.0, 0.0).astype(jnp.bfloat16)
        for ch in range(32):
            hot_ref[:, ch * 128 : (ch + 1) * 128] = jnp.where(chunk == one * ch, hot, zero)
        out_ref[blk * 256 : (blk + 1) * 256, :] = jnp.dot(
            hot_ref[...], points_ref[...], preferred_element_type=jnp.float32
        ).astype(jnp.bfloat16)


def send_rows(scalars, rank2d, points):
    return pl.pallas_call(
        send_kernel,
        out_shape=jax.ShapeDtypeStruct((1024, 256), jnp.bfloat16),
        in_specs=[smem(), hbm(), hbm()],
        out_specs=vmem(),
        scratch_shapes=[
            pltpu.VMEM((2048, LANES), jnp.int32),
            pltpu.VMEM((4096, 256), jnp.bfloat16),
            pltpu.VMEM((1024, LANES), jnp.int32),
            pltpu.VMEM((1024, LANES), jnp.float32),
            pltpu.VMEM((256, 4096), jnp.bfloat16),
            pltpu.VMEM((256, 4096), jnp.bfloat16),
            pltpu.SemaphoreType.DMA((8,)),
            pltpu.SemaphoreType.DMA,
        ],
        compiler_params=pltpu.CompilerParams(vmem_limit_bytes=VMEM_LIMIT),
        name="send_rows",
    )(scalars, rank2d, points)


def place_kernel(s_ref, rank_hbm, thr_hbm, row_ref, col_ref, place_ref, u_ref, v_ref, rank_ref, thr_ref, sems):
    copies = []
    for x in range(3):
        start = pl.multiple_of(s_ref[3 + x] * 32, 32)
        copies.append((
            pltpu.make_async_copy(rank_hbm.at[pl.ds(start, 32), :], rank_ref.at[x], sems.at[x, 0]),
            pltpu.make_async_copy(thr_hbm.at[pl.ds(start, 32), :], thr_ref.at[x], sems.at[x, 1]),
        ))
        for copy in copies[x]:
            copy.start()
    rep = s_ref[2]
    prefix = prefix_matrix()
    shard_iota = lax.broadcasted_iota(jnp.int32, (64, LANES), 0)
    u_iota = lax.broadcasted_iota(jnp.int32, (32, LANES), 0)
    v_iota = lax.broadcasted_iota(jnp.int32, (LANES, LANES), 0)
    for x in range(3):
        for copy in copies[x]:
            copy.wait()
        carry = jnp.zeros((64, LANES), jnp.float32)
        source = rank_ref[x] >> 12
        thr = thr_ref[x]
        for j in range(32):
            shard = source[j : j + 1, :]
            hot = shard == shard_iota
            counts = jnp.dot(
                jnp.where(hot, 1.0, 0.0).astype(jnp.bfloat16), prefix, preferred_element_type=jnp.float32
            )
            slot = jnp.sum(jnp.where(hot, carry + counts[:, :LANES], 0.0), axis=0, keepdims=True)
            slot = slot.astype(jnp.int32) - 1
            carry = carry + counts[:, LANES:]
            quarter = slot >> 4
            v = (shard & 7) * 16 + (slot & 15)
            if x == 2:
                place_ref[j : j + 1, :] = (((rep - quarter) & 3) * 8 + (shard >> 3)) * 128 + v
            else:
                u = ((quarter - rep) & 3) * 8 + (shard >> 3)
                u_hot = u == u_iota
                t = thr[j : j + 1, :]
                lanes = slice(j * LANES, (j + 1) * LANES)
                u_ref[0:32, lanes] = jnp.where(u_hot, (t >> 4).astype(jnp.float32), 0.0).astype(jnp.bfloat16)
                u_ref[32:64, lanes] = jnp.where(u_hot, (t & 15).astype(jnp.float32), 0.0).astype(jnp.bfloat16)
                u_ref[64:96, lanes] = jnp.where(u_hot, float(j >= 16), 0.0).astype(jnp.bfloat16)
                v_ref[:, lanes] = jnp.where(v == v_iota, 1.0, 0.0).astype(jnp.bfloat16)
        if x < 2:
            us = u_ref[...]
            vs = v_ref[...]
            rows = lax.dot_general(us, vs, NT, preferred_element_type=jnp.float32)
            cols = lax.dot_general(vs, us, NT, preferred_element_type=jnp.float32)
            row_ref[x, 0:32, :] = 1024.0 / (rows[0:32] * 16.0 + rows[32:64])
            row_ref[x, 32:64, :] = rows[64:96]
            col_ref[x, :, 0:32] = 1024.0 / (cols[:, 0:32] * 16.0 + cols[:, 32:64])
            col_ref[x, :, 32:64] = cols[:, 64:96]


def place(scalars, rank2d, thr2d):
    return pl.pallas_call(
        place_kernel,
        out_shape=(
            jax.ShapeDtypeStruct((2, 64, LANES), jnp.float32),
            jax.ShapeDtypeStruct((2, LANES, 64), jnp.float32),
            jax.ShapeDtypeStruct((32, LANES), jnp.int32),
        ),
        in_specs=[smem(), hbm(), hbm()],
        out_specs=(vmem(),) * 3,
        scratch_shapes=[
            pltpu.VMEM((96, 4096), jnp.bfloat16),
            pltpu.VMEM((LANES, 4096), jnp.bfloat16),
            pltpu.VMEM((3, 32, LANES), jnp.int32),
            pltpu.VMEM((3, 32, LANES), jnp.int32),
            pltpu.SemaphoreType.DMA((3, 2)),
        ],
        compiler_params=pltpu.CompilerParams(vmem_limit_bytes=VMEM_LIMIT),
        cost_estimate=pl.CostEstimate(flops=2 * 10**9, bytes_accessed=10**7, transcendentals=0),
        name="place",
    )(scalars, rank2d, thr2d)


def square_sums(block):
    values = block.astype(jnp.float32)
    square = values * values
    total = square[:, :LANES] + square[:, LANES:]
    high = total.astype(jnp.bfloat16)
    rest = total - high.astype(jnp.float32)
    middle = rest.astype(jnp.bfloat16)
    low = (rest - middle.astype(jnp.float32)).astype(jnp.bfloat16)
    return high, middle, low


def inverse_column(terms):
    ones = jnp.ones((LANES, LANES), jnp.bfloat16)
    high, middle, low = (jnp.dot(t, ones, preferred_element_type=jnp.float32) for t in terms)
    return lax.rsqrt(high + (middle + low) + 1e-06)


def inverse_row(terms):
    ones = jnp.ones((8, LANES), jnp.bfloat16)
    high, middle, low = (
        lax.dot_general(ones, t, NT, preferred_element_type=jnp.float32) for t in terms
    )
    return lax.rsqrt(high + (middle + low) + 1e-06)


def load_column_meta(col_ref, band, quarter, meta):
    for u in range(8):
        rows = slice(u * LANES, (u + 1) * LANES)
        i = quarter * 8 + u
        meta[1, rows, :] = jnp.broadcast_to(col_ref[band, :, i : i + 1], (LANES, LANES))
        meta[2, rows, :] = jnp.broadcast_to(col_ref[band, :, 32 + i : 33 + i], (LANES, LANES))


def load_row_meta(at, row_ref, band, quarter, keep_ref, row_offset, col_offset, meta, keep):
    for u in range(8):
        lanes = slice(at + u * LANES, at + (u + 1) * LANES)
        i = quarter * 8 + u
        meta[1, :, lanes] = jnp.broadcast_to(row_ref[band, i : i + 1, :], (8, LANES))
        upper = jnp.broadcast_to(row_ref[band, 32 + i : 33 + i, :], (8, LANES)) > 0.5
        for t in range(2):
            code = (row_offset + t) * 4 + col_offset
            keep[t, :, lanes] = jnp.where(upper, keep_ref[code + 1], keep_ref[code])


def product(left_ref, left_at, right_ref, right_at, prod_ref):
    rows, cols = prod_ref.shape
    prod_ref[...] = lax.dot_general(
        left_ref[pl.ds(left_at, rows), :], right_ref[pl.ds(right_at, cols), :], NT,
        preferred_element_type=jnp.float32,
    )


def weigh(prod_ref, left_at, left_meta, right_at, right_meta, keep, row_sum, col_sum, diagonal):
    chunks = prod_ref.shape[1] // LANES
    sums = [jnp.zeros((8, LANES), jnp.float32) for _ in range(chunks)]
    lanes = [pl.ds(pl.multiple_of(right_at + ch * LANES, LANES), LANES) for ch in range(chunks)]
    for i in range(prod_ref.shape[0] // 32):
        rows = pl.ds(pl.multiple_of(left_at + i * 32, 32), 32)
        inv_i = left_meta[0, rows, :].reshape(4, 8, LANES)
        rho_i = left_meta[1, rows, :].reshape(4, 8, LANES)
        upper = left_meta[2, rows, :].reshape(4, 8, LANES) > 0.5
        total = row_sum[rows, :].reshape(4, 8, LANES)
        for ch in range(chunks):
            inv_j = right_meta[0, :, lanes[ch]][None]
            rho_j = right_meta[1, :, lanes[ch]][None]
            kept = jnp.where(upper, keep[1, :, lanes[ch]][None], keep[0, :, lanes[ch]][None])
            p = prod_ref[i * 32 : i * 32 + 32, ch * LANES : (ch + 1) * LANES].reshape(4, 8, LANES)
            near = (p * inv_i) * inv_j - 1.0
            w = jnp.maximum(near * jnp.maximum(rho_i, rho_j) + kept, 0.0)
            if diagonal:
                row_ids = lax.broadcasted_iota(jnp.int32, w.shape, 0) * 8 + lax.broadcasted_iota(jnp.int32, w.shape, 1)
                col_ids = lax.broadcasted_iota(jnp.int32, w.shape, 2)
                w = jnp.where(row_ids + (left_at + i * 32) == col_ids + (right_at + ch * LANES), 0.0, w)
            total = total + w
            if not diagonal:
                sums[ch] = sums[ch] + ((w[0] + w[1]) + (w[2] + w[3]))
        row_sum[rows, :] = total.reshape(32, LANES)
    if not diagonal:
        for ch in range(chunks):
            col_sum[:, lanes[ch]] += sums[ch]


def rows_to_lanes(row_sum):
    row = lax.broadcasted_iota(jnp.int32, (LANES, LANES), 0)
    lane = lax.broadcasted_iota(jnp.int32, (LANES, LANES), 1)
    out = []
    for u in range(8):
        total = jnp.sum(row_sum[u * LANES : (u + 1) * LANES, :], axis=1, keepdims=True)
        out.append(jnp.sum(jnp.where(row == lane, total, 0.0), axis=0, keepdims=True))
    return out


def cols_to_lanes(col_sum, at):
    return [
        jnp.sum(col_sum[:, at + u * LANES : at + (u + 1) * LANES], axis=0, keepdims=True)
        for u in range(8)
    ]


def near_kernel(s_ref, keep_ref, own_ref, other_ref, row_ref, col_ref, out_ref, inverse_ref,
                left_meta, right_meta, keep, prod_a, prod_b, row_sum, col_sum):
    core = s_ref[6]
    own_offset = s_ref[7]
    other_offset = s_ref[8]
    terms = square_sums(own_ref[...])
    left_meta[0] = inverse_column(terms)
    right_meta[0, :, 0:1024] = inverse_row(terms)
    right_meta[0, :, 1024:2048] = inverse_row(square_sums(other_ref[...]))
    inverse_ref[...] = right_meta[0]
    load_column_meta(col_ref, 0, 0, left_meta)
    load_row_meta(0, row_ref, 0, 0, keep_ref, own_offset, own_offset, right_meta, keep)
    load_row_meta(1024, row_ref, 1, 0, keep_ref, own_offset, other_offset, right_meta, keep)
    row_sum[...] = jnp.zeros_like(row_sum)
    col_sum[...] = jnp.zeros_like(col_sum)

    @pl.loop(0, 4)
    def _(i):
        at = pl.multiple_of(i * 256, 256)
        half = pl.multiple_of(((i >> 1) ^ core) * 512, 512)
        product(own_ref, at, own_ref, 0, prod_a)
        product(own_ref, at, own_ref, 512, prod_b)
        weigh(prod_a, at, left_meta, 0, right_meta, keep, row_sum, col_sum, True)
        product(own_ref, at, other_ref, half, prod_a)
        weigh(prod_b, at, left_meta, 512, right_meta, keep, row_sum, col_sum, True)
        weigh(prod_a, at, left_meta, 1024 + half, right_meta, keep, row_sum, col_sum, False)

    own = rows_to_lanes(row_sum)
    other = cols_to_lanes(col_sum, 1024)
    for u in range(8):
        out_ref[0, u : u + 1, :] = own[u]
        out_ref[1, u : u + 1, :] = other[u]


def far_kernel(s_ref, keep_ref, own_hbm, other_hbm, left_hbm, right_ref, row_ref, col_ref, near_ref,
               inverse_ref, stay_ref, move_ref, block_ref, left_meta, right_meta, keep, prod_a,
               prod_b, row_sum, col_sum, sems):
    own_offset = s_ref[7]
    other_offset = s_ref[8]
    cross = s_ref[9]
    left_offset = s_ref[10]
    copies = [
        pltpu.make_async_copy(source, block_ref.at[pl.ds(i * 1024, 1024), :], sems.at[i])
        for i, source in enumerate((own_hbm, other_hbm, left_hbm))
    ]
    for copy in copies:
        copy.start()
    left_meta[0] = inverse_column(square_sums(right_ref[...]))
    load_column_meta(col_ref, 0, 1, left_meta)
    load_row_meta(0, row_ref, 0, 0, keep_ref, own_offset, own_offset, right_meta, keep)
    load_row_meta(1024, row_ref, 1, 0, keep_ref, own_offset, other_offset, right_meta, keep)
    load_row_meta(2048, row_ref, cross, 3, keep_ref, own_offset, left_offset, right_meta, keep)
    right_meta[0, :, 0:2048] = inverse_ref[...]
    row_sum[...] = jnp.zeros_like(row_sum)
    col_sum[...] = jnp.zeros_like(col_sum)
    for copy in copies:
        copy.wait()
    right_meta[0, :, 2048:3072] = inverse_row(square_sums(block_ref[2048:3072, :]))
    rows, cols = prod_a.shape
    steps = 1024 // rows
    total = steps * (3072 // cols)
    product(right_ref, 0, block_ref, 0, prod_a)

    def place_of(t):
        return pl.multiple_of((t % steps) * rows, rows), pl.multiple_of((t // steps) * cols, cols)

    @pl.loop(0, total // 2)
    def _(i):
        left_a, right_a = place_of(i * 2)
        left_b, right_b = place_of(i * 2 + 1)
        left_c, right_c = place_of(jnp.minimum(i * 2 + 2, total - 1))
        product(right_ref, left_b, block_ref, right_b, prod_b)
        weigh(prod_a, left_a, left_meta, right_a, right_meta, keep, row_sum, col_sum, False)
        product(right_ref, left_c, block_ref, right_c, prod_a)
        weigh(prod_b, left_b, left_meta, right_b, right_meta, keep, row_sum, col_sum, False)

    right = rows_to_lanes(row_sum)
    own = cols_to_lanes(col_sum, 0)
    other = cols_to_lanes(col_sum, 1024)
    left = cols_to_lanes(col_sum, 2048)
    for u in range(8):
        row = slice(u, u + 1)
        stay_ref[0, row, :] = own[u] + near_ref[0, row, :]
        stay_ref[1, row, :] = right[u]
        stay_ref[2, row, :] = jnp.where(cross == 0, left[u], 0.0)
        move_ref[0, row, :] = other[u] + near_ref[1, row, :]
        move_ref[1, row, :] = jnp.where(cross == 0, 0.0, left[u])


FAR_TILE = (512, 512)


def pair_scratch(columns, tile):
    return [
        pltpu.VMEM((3, 1024, LANES), jnp.float32),
        pltpu.VMEM((2, 8, columns), jnp.float32),
        pltpu.VMEM((2, 8, columns), jnp.float32),
        pltpu.VMEM(tile, jnp.float32),
        pltpu.VMEM(tile, jnp.float32),
        pltpu.VMEM((1024, LANES), jnp.float32),
        pltpu.VMEM((8, columns), jnp.float32),
    ]


def near_pairs(scalars, keep, own, other, rows, cols):
    return pl.pallas_call(
        near_kernel,
        out_shape=(
            jax.ShapeDtypeStruct((2, 8, LANES), jnp.float32),
            jax.ShapeDtypeStruct((8, 2048), jnp.float32),
        ),
        in_specs=[smem(), smem(), vmem(), vmem(), vmem(), vmem()],
        out_specs=(vmem(), vmem()),
        scratch_shapes=pair_scratch(2048, (256, 512)),
        compiler_params=pltpu.CompilerParams(vmem_limit_bytes=VMEM_LIMIT),
        cost_estimate=pl.CostEstimate(flops=2 * 10**9, bytes_accessed=10**7, transcendentals=0),
        name="near_pairs",
    )(scalars, keep, own, other, rows, cols)


def far_pairs(scalars, keep, own, other, left, right, rows, cols, near):
    return pl.pallas_call(
        far_kernel,
        out_shape=(
            jax.ShapeDtypeStruct((3, 8, LANES), jnp.float32),
            jax.ShapeDtypeStruct((2, 8, LANES), jnp.float32),
        ),
        in_specs=[smem(), smem(), hbm(), hbm(), hbm()] + [vmem()] * 5,
        out_specs=(vmem(), vmem()),
        scratch_shapes=[pltpu.VMEM((3072, 256), jnp.bfloat16)]
        + pair_scratch(3072, FAR_TILE)
        + [pltpu.SemaphoreType.DMA((3,))],
        compiler_params=pltpu.CompilerParams(vmem_limit_bytes=VMEM_LIMIT),
        cost_estimate=pl.CostEstimate(flops=4 * 10**9, bytes_accessed=10**7, transcendentals=0),
        name="far_pairs",
    )(scalars, keep, own, other, left, right, rows, cols, *near)


def rank_kernel(place_ref, *refs):
    pieces, out_ref = refs[:-1], refs[-1]
    place_at = place_ref[...]
    lane = place_at & 127
    which = place_at >> 7
    total = jnp.zeros((32, LANES), jnp.float32)
    for s in range(4):
        block = pieces[s][0] + pieces[(s + 1) % 4][1] + pieces[(s + 3) % 4][2]
        for u in range(8):
            row = jnp.broadcast_to(block[u : u + 1, :], (32, LANES))
            value = jnp.take_along_axis(row, lane, axis=1)
            total = jnp.where(which == s * 8 + u, value, total)
    out_ref[...] = total * (1.0 / TILE)


def to_rank_order(place_at, pieces):
    return pl.pallas_call(
        rank_kernel,
        out_shape=jax.ShapeDtypeStruct((32, LANES), jnp.float32),
        in_specs=[vmem()] * 5,
        out_specs=vmem(),
        name="to_rank_order",
    )(place_at, *pieces)


def on_device(points, rank_source, thresholds, kept_tiles):
    bands = lax.axis_size("band")
    reps = lax.axis_size("rep")
    device = lax.axis_index("band").astype(jnp.int32)
    rep = lax.axis_index("rep").astype(jnp.int32)
    core = device & 1
    own_band = jnp.where(core == 0, device, bands - device)
    other_band = bands - 1 - own_band
    own_offset = jnp.where(own_band < bands // 2, 0, 2)
    other_offset = 2 - own_offset
    cross = (rep >= 2).astype(jnp.int32)
    left_offset = jnp.where(cross == 1, other_offset, own_offset)
    scalars = jnp.stack([
        device, rep * 16, rep, own_band, other_band, device, core,
        own_offset, other_offset, cross, left_offset,
    ]).astype(jnp.int32)
    codes = lax.dynamic_index_in_dim(kept_tiles, jnp.minimum(own_band, other_band), 0, keepdims=False)
    ids = jnp.arange(16, dtype=jnp.int32)
    a, c = ids // 4, ids % 4
    wanted = jnp.minimum(a, c) * 4 + jnp.maximum(a, c)
    keep = jnp.where(jnp.any(codes[:, None] == wanted[None, :], axis=0), 1.0, -1e30).astype(jnp.float32)

    rank2d = rank_source.reshape(2048, LANES)
    thr2d = thresholds.reshape(2048, LANES)

    def joint(move):
        return [
            (d * reps + r, e * reps + q)
            for d in range(bands)
            for r in range(reps)
            for e, q in (move(d, r),)
        ]

    def shift(value, move):
        return lax.ppermute(value, ("band", "rep"), joint(move))

    payload = send_rows(scalars, rank2d, points)
    own = lax.all_to_all(
        payload.reshape(bands, 16, 256), "band", split_axis=0, concat_axis=0, tiled=True
    ).reshape(1024, 256)
    own, rows, cols, place_at = lax.optimization_barrier((own, *place(scalars, rank2d, thr2d)))

    def to_right(d, r):
        q = (r + 1) % reps
        return (d if q < 2 else d ^ 1), q

    other = shift(own, lambda d, r: (d ^ 1, r))
    right = shift(own, lambda d, r: (d, (r - 1) % reps))
    left = shift(own, to_right)

    near = near_pairs(scalars, keep, own, other, rows, cols)
    stay, move = far_pairs(scalars, keep, own, other, left, right, rows, cols, near)
    moved = shift(move, lambda d, r: (d ^ 1, r))
    sums = stay + jnp.stack([moved[0], jnp.zeros_like(moved[0]), moved[1]])
    home = shift(sums, lambda d, r: (block_band(d), r))
    pieces = [home] + [
        shift(home, lambda d, r, s=s: (d, (r + s) % reps)) for s in range(1, reps)
    ]
    return to_rank_order(place_at, pieces).reshape(points.shape[0])


def solution(mesh):
    in_specs = (P("band", None), P(), P(), P())
    out_specs = P("band")
    return jax.shard_map(
        on_device, mesh=mesh, in_specs=in_specs, out_specs=out_specs, check_vma=False
    )
```

```python
import jax
import jax.numpy as jnp
from jax import lax
from jax.experimental import pallas as pl
from jax.experimental.pallas import tpu as pltpu
from jax.sharding import PartitionSpec as P

TILE = 2048
LANES = 128
SEND_VMEM = 60 * 1024 * 1024
VMEM = 28 * 1024 * 1024
NT = (((1,), (1,)), ((), ()))


def prefix_matrix():
    row = lax.broadcasted_iota(jnp.int32, (LANES, 2 * LANES), 0)
    col = lax.broadcasted_iota(jnp.int32, (LANES, 2 * LANES), 1)
    return jnp.where((row <= col) | (col >= LANES), 1.0, 0.0).astype(jnp.bfloat16)


def block_band(device):
    return device if device % 2 == 0 else 64 - device


def smem():
    return pl.BlockSpec(memory_space=pltpu.SMEM)


def vmem():
    return pl.BlockSpec(memory_space=pltpu.VMEM)


def hbm():
    return pl.BlockSpec(memory_space=pltpu.HBM)


def send_kernel(rank_hbm, points_hbm, out_ref, rank_ref, points_ref, acc_ref, row_ref,
                hot_ref, rank_sem, points_sem):
    def fetch_rank(g):
        rows = pl.ds(g * 256, 256)
        return pltpu.make_async_copy(rank_hbm.at[rows, :], rank_ref.at[rows, :], rank_sem.at[g])

    for g in range(8):
        fetch_rank(g).start()
    fetch_points = pltpu.make_async_copy(points_hbm, points_ref, points_sem)
    fetch_points.start()
    shard = lax.axis_index("band")
    prefix = prefix_matrix()
    base = (lax.axis_index("rep") * 16 + 1).astype(jnp.float32)
    ones = jnp.ones((LANES, LANES), jnp.bfloat16)
    for g in range(8):
        fetch_rank(g).wait()
        source = [rank_ref[pl.ds(g * 256 + j, 8, stride=32), :] for j in range(32)]
        mine = [(source[j] >> 12) == shard for j in range(32)]
        marks = jnp.concatenate([jnp.where(m, 1.0, 0.0) for m in mine], axis=0).astype(jnp.bfloat16)
        counts = jnp.dot(marks, prefix, preferred_element_type=jnp.float32)
        carry = jnp.zeros((8, LANES), jnp.float32) - base
        accs = [jnp.zeros((8, LANES), jnp.int32) for _ in range(16)]
        for j in range(32):
            pos = jnp.where(mine[j], carry + counts[j * 8 : j * 8 + 8, :LANES], -1.0)
            loc = source[j] & 4095
            carry = carry + counts[j * 8 : j * 8 + 8, LANES:]
            for i in range(16):
                accs[i] = jnp.where(pos == float(i), loc, accs[i])
        for i in range(16):
            acc_ref[g * 128 + i * 8 : g * 128 + i * 8 + 8, :] = accs[i]

    acc = acc_ref[...]
    high = (acc >> 6).astype(jnp.float32).astype(jnp.bfloat16)
    low = (acc & 63).astype(jnp.float32).astype(jnp.bfloat16)
    row_ref[...] = 64.0 * jnp.dot(high, ones, preferred_element_type=jnp.float32) + jnp.dot(
        low, ones, preferred_element_type=jnp.float32
    )
    fetch_points.wait()
    lane = lax.broadcasted_iota(jnp.int32, (1024, LANES), 1)
    one = jnp.ones((1024, LANES), jnp.bfloat16)
    zero = jnp.zeros((1024, LANES), jnp.bfloat16)
    parts = []
    for i in range(64):
        band = block_band(i)
        parts.append(row_ref[pl.ds((band // 8) * 128 + band % 8, 16, stride=8), :])
    local = jnp.concatenate(parts, axis=0).astype(jnp.int32)
    chunk = (local >> 7).astype(jnp.float32).astype(jnp.bfloat16)
    hot = jnp.where((local & 127) == lane, 1.0, 0.0).astype(jnp.bfloat16)
    for ch in range(32):
        hot_ref[:, ch * 128 : (ch + 1) * 128] = jnp.where(chunk == one * ch, hot, zero)
    out_ref[...] = jnp.dot(
        hot_ref[...], points_ref[...], preferred_element_type=jnp.float32
    ).astype(jnp.bfloat16)


def send_rows(rank2d, points):
    return pl.pallas_call(
        send_kernel,
        out_shape=jax.ShapeDtypeStruct((1024, 256), jnp.bfloat16),
        in_specs=[hbm(), hbm()],
        out_specs=vmem(),
        scratch_shapes=[
            pltpu.VMEM((2048, LANES), jnp.int32),
            pltpu.VMEM((4096, 256), jnp.bfloat16),
            pltpu.VMEM((1024, LANES), jnp.int32),
            pltpu.VMEM((1024, LANES), jnp.float32),
            pltpu.VMEM((1024, 4096), jnp.bfloat16),
            pltpu.SemaphoreType.DMA((8,)),
            pltpu.SemaphoreType.DMA,
        ],
        compiler_params=pltpu.CompilerParams(vmem_limit_bytes=SEND_VMEM),
        name="send_rows",
    )(rank2d, points)


def place_kernel(s_ref, rank_hbm, thr_hbm, row_ref, col_ref, place_ref, u_ref, v_ref, rank_ref, thr_ref, sems):
    copies = []
    for x in range(3):
        start = pl.multiple_of(s_ref[3 + x] * 32, 32)
        copies.append((
            pltpu.make_async_copy(rank_hbm.at[pl.ds(start, 32), :], rank_ref.at[x], sems.at[x, 0]),
            pltpu.make_async_copy(thr_hbm.at[pl.ds(start, 32), :], thr_ref.at[x], sems.at[x, 1]),
        ))
        for copy in copies[x]:
            copy.start()
    rep = s_ref[2]
    prefix = prefix_matrix()
    shard_iota = lax.broadcasted_iota(jnp.int32, (64, LANES), 0)
    u_iota = lax.broadcasted_iota(jnp.int32, (32, LANES), 0)
    v_iota = lax.broadcasted_iota(jnp.int32, (LANES, LANES), 0)
    for x in range(3):
        for copy in copies[x]:
            copy.wait()
        carry = jnp.zeros((64, LANES), jnp.float32)
        source = rank_ref[x] >> 12
        thr = thr_ref[x]
        for j in range(32):
            shard = source[j : j + 1, :]
            hot = shard == shard_iota
            counts = jnp.dot(
                jnp.where(hot, 1.0, 0.0).astype(jnp.bfloat16), prefix, preferred_element_type=jnp.float32
            )
            slot = jnp.sum(jnp.where(hot, carry + counts[:, :LANES], 0.0), axis=0, keepdims=True)
            slot = slot.astype(jnp.int32) - 1
            carry = carry + counts[:, LANES:]
            quarter = slot >> 4
            v = (shard & 7) * 16 + (slot & 15)
            if x == 2:
                place_ref[j : j + 1, :] = (((rep - quarter) & 3) * 8 + (shard >> 3)) * 128 + v
            else:
                u = ((quarter - rep) & 3) * 8 + (shard >> 3)
                u_hot = u == u_iota
                t = thr[j : j + 1, :]
                lanes = slice(j * LANES, (j + 1) * LANES)
                u_ref[0:32, lanes] = jnp.where(u_hot, (t >> 4).astype(jnp.float32), 0.0).astype(jnp.bfloat16)
                u_ref[32:64, lanes] = jnp.where(u_hot, (t & 15).astype(jnp.float32), 0.0).astype(jnp.bfloat16)
                u_ref[64:96, lanes] = jnp.where(u_hot, float(j >= 16), 0.0).astype(jnp.bfloat16)
                v_ref[:, lanes] = jnp.where(v == v_iota, 1.0, 0.0).astype(jnp.bfloat16)
        if x < 2:
            us = u_ref[...]
            vs = v_ref[...]
            rows = lax.dot_general(us, vs, NT, preferred_element_type=jnp.float32)
            cols = lax.dot_general(vs, us, NT, preferred_element_type=jnp.float32)
            row_ref[x, 0:32, :] = 1024.0 / (rows[0:32] * 16.0 + rows[32:64])
            row_ref[x, 32:64, :] = rows[64:96]
            col_ref[x, :, 0:32] = 1024.0 / (cols[:, 0:32] * 16.0 + cols[:, 32:64])
            col_ref[x, :, 32:64] = cols[:, 64:96]


def place(scalars, rank2d, thr2d):
    return pl.pallas_call(
        place_kernel,
        out_shape=(
            jax.ShapeDtypeStruct((2, 64, LANES), jnp.float32),
            jax.ShapeDtypeStruct((2, LANES, 64), jnp.float32),
            jax.ShapeDtypeStruct((32, LANES), jnp.int32),
        ),
        in_specs=[smem(), hbm(), hbm()],
        out_specs=(vmem(),) * 3,
        scratch_shapes=[
            pltpu.VMEM((96, 4096), jnp.bfloat16),
            pltpu.VMEM((LANES, 4096), jnp.bfloat16),
            pltpu.VMEM((3, 32, LANES), jnp.int32),
            pltpu.VMEM((3, 32, LANES), jnp.int32),
            pltpu.SemaphoreType.DMA((3, 2)),
        ],
        compiler_params=pltpu.CompilerParams(vmem_limit_bytes=VMEM),
        cost_estimate=pl.CostEstimate(flops=2 * 10**9, bytes_accessed=10**7, transcendentals=0),
        name="place",
    )(scalars, rank2d, thr2d)


def square_sums(block):
    values = block.astype(jnp.float32)
    square = values * values
    total = square[:, :LANES] + square[:, LANES:]
    high = total.astype(jnp.bfloat16)
    rest = total - high.astype(jnp.float32)
    middle = rest.astype(jnp.bfloat16)
    low = (rest - middle.astype(jnp.float32)).astype(jnp.bfloat16)
    return high, middle, low


def inverse_column(terms):
    ones = jnp.ones((LANES, LANES), jnp.bfloat16)
    high, middle, low = (jnp.dot(t, ones, preferred_element_type=jnp.float32) for t in terms)
    return lax.rsqrt(high + (middle + low) + 1e-06)


def inverse_row(terms):
    ones = jnp.ones((8, LANES), jnp.bfloat16)
    high, middle, low = (
        lax.dot_general(ones, t, NT, preferred_element_type=jnp.float32) for t in terms
    )
    return lax.rsqrt(high + (middle + low) + 1e-06)


def load_column_meta(col_ref, band, quarter, meta):
    for u in range(8):
        rows = slice(u * LANES, (u + 1) * LANES)
        i = quarter * 8 + u
        meta[1, rows, :] = jnp.broadcast_to(col_ref[band, :, i : i + 1], (LANES, LANES))
        meta[2, rows, :] = jnp.broadcast_to(col_ref[band, :, 32 + i : 33 + i], (LANES, LANES))


def load_row_meta(at, row_ref, band, quarter, keep_ref, row_offset, col_offset, meta, keep):
    for u in range(8):
        lanes = slice(at + u * LANES, at + (u + 1) * LANES)
        i = quarter * 8 + u
        meta[1, :, lanes] = jnp.broadcast_to(row_ref[band, i : i + 1, :], (8, LANES))
        upper = jnp.broadcast_to(row_ref[band, 32 + i : 33 + i, :], (8, LANES)) > 0.5
        for t in range(2):
            code = (row_offset + t) * 4 + col_offset
            keep[t, :, lanes] = jnp.where(upper, keep_ref[code + 1], keep_ref[code])


def product(left_ref, left_at, right_ref, right_at, prod_ref):
    rows, cols = prod_ref.shape
    prod_ref[...] = lax.dot_general(
        left_ref[pl.ds(left_at, rows), :], right_ref[pl.ds(right_at, cols), :], NT,
        preferred_element_type=jnp.float32,
    )


def weigh(prod_ref, left_at, left_meta, right_at, right_meta, keep, row_sum, col_sum, diagonal):
    chunks = prod_ref.shape[1] // LANES
    sums = [jnp.zeros((8, LANES), jnp.float32) for _ in range(chunks)]
    lanes = [pl.ds(pl.multiple_of(right_at + ch * LANES, LANES), LANES) for ch in range(chunks)]
    for i in range(prod_ref.shape[0] // 32):
        rows = pl.ds(pl.multiple_of(left_at + i * 32, 32), 32)
        inv_i = left_meta[0, rows, :].reshape(4, 8, LANES)
        rho_i = left_meta[1, rows, :].reshape(4, 8, LANES)
        upper = left_meta[2, rows, :].reshape(4, 8, LANES) > 0.5
        total = row_sum[rows, :].reshape(4, 8, LANES)
        for ch in range(chunks):
            inv_j = right_meta[0, :, lanes[ch]][None]
            rho_j = right_meta[1, :, lanes[ch]][None]
            kept = jnp.where(upper, keep[1, :, lanes[ch]][None], keep[0, :, lanes[ch]][None])
            p = prod_ref[i * 32 : i * 32 + 32, ch * LANES : (ch + 1) * LANES].reshape(4, 8, LANES)
            near = (p * inv_i) * inv_j - 1.0
            w = jnp.maximum(near * jnp.maximum(rho_i, rho_j) + kept, 0.0)
            if diagonal:
                row_ids = lax.broadcasted_iota(jnp.int32, w.shape, 0) * 8 + lax.broadcasted_iota(jnp.int32, w.shape, 1)
                col_ids = lax.broadcasted_iota(jnp.int32, w.shape, 2)
                w = jnp.where(row_ids + (left_at + i * 32) == col_ids + (right_at + ch * LANES), 0.0, w)
            total = total + w
            if not diagonal:
                sums[ch] = sums[ch] + ((w[0] + w[1]) + (w[2] + w[3]))
        row_sum[rows, :] = total.reshape(32, LANES)
    if not diagonal:
        for ch in range(chunks):
            col_sum[:, lanes[ch]] += sums[ch]


def rows_to_lanes(row_sum):
    row = lax.broadcasted_iota(jnp.int32, (LANES, LANES), 0)
    lane = lax.broadcasted_iota(jnp.int32, (LANES, LANES), 1)
    out = []
    for u in range(8):
        total = jnp.sum(row_sum[u * LANES : (u + 1) * LANES, :], axis=1, keepdims=True)
        out.append(jnp.sum(jnp.where(row == lane, total, 0.0), axis=0, keepdims=True))
    return out


def cols_to_lanes(col_sum, at):
    return [
        jnp.sum(col_sum[:, at + u * LANES : at + (u + 1) * LANES], axis=0, keepdims=True)
        for u in range(8)
    ]


def near_kernel(s_ref, keep_ref, own_ref, other_ref, row_ref, col_ref, out_ref, inverse_ref,
                left_meta, right_meta, keep, prod_a, prod_b, row_sum, col_sum):
    core = s_ref[6]
    own_offset = s_ref[7]
    other_offset = s_ref[8]
    terms = square_sums(own_ref[...])
    left_meta[0] = inverse_column(terms)
    right_meta[0, :, 0:1024] = inverse_row(terms)
    right_meta[0, :, 1024:2048] = inverse_row(square_sums(other_ref[...]))
    inverse_ref[...] = right_meta[0]
    load_column_meta(col_ref, 0, 0, left_meta)
    load_row_meta(0, row_ref, 0, 0, keep_ref, own_offset, own_offset, right_meta, keep)
    load_row_meta(1024, row_ref, 1, 0, keep_ref, own_offset, other_offset, right_meta, keep)
    row_sum[...] = jnp.zeros_like(row_sum)
    col_sum[...] = jnp.zeros_like(col_sum)

    @pl.loop(0, 4)
    def _(i):
        at = pl.multiple_of(i * 256, 256)
        half = pl.multiple_of(((i >> 1) ^ core) * 512, 512)
        product(own_ref, at, own_ref, 0, prod_a)
        product(own_ref, at, own_ref, 512, prod_b)
        weigh(prod_a, at, left_meta, 0, right_meta, keep, row_sum, col_sum, True)
        product(own_ref, at, other_ref, half, prod_a)
        weigh(prod_b, at, left_meta, 512, right_meta, keep, row_sum, col_sum, True)
        weigh(prod_a, at, left_meta, 1024 + half, right_meta, keep, row_sum, col_sum, False)

    own = rows_to_lanes(row_sum)
    other = cols_to_lanes(col_sum, 1024)
    for u in range(8):
        out_ref[0, u : u + 1, :] = own[u]
        out_ref[1, u : u + 1, :] = other[u]


def far_kernel(s_ref, keep_ref, own_hbm, other_hbm, left_hbm, right_ref, row_ref, col_ref, near_ref,
               inverse_ref, stay_ref, move_ref, block_ref, left_meta, right_meta, keep, prod_a,
               prod_b, row_sum, col_sum, sems):
    own_offset = s_ref[7]
    other_offset = s_ref[8]
    cross = s_ref[9]
    left_offset = s_ref[10]
    copies = [
        pltpu.make_async_copy(source, block_ref.at[pl.ds(i * 1024, 1024), :], sems.at[i])
        for i, source in enumerate((own_hbm, other_hbm, left_hbm))
    ]
    for copy in copies:
        copy.start()
    left_meta[0] = inverse_column(square_sums(right_ref[...]))
    load_column_meta(col_ref, 0, 1, left_meta)
    load_row_meta(0, row_ref, 0, 0, keep_ref, own_offset, own_offset, right_meta, keep)
    load_row_meta(1024, row_ref, 1, 0, keep_ref, own_offset, other_offset, right_meta, keep)
    load_row_meta(2048, row_ref, cross, 3, keep_ref, own_offset, left_offset, right_meta, keep)
    right_meta[0, :, 0:2048] = inverse_ref[...]
    row_sum[...] = jnp.zeros_like(row_sum)
    col_sum[...] = jnp.zeros_like(col_sum)
    for copy in copies:
        copy.wait()
    right_meta[0, :, 2048:3072] = inverse_row(square_sums(block_ref[2048:3072, :]))
    rows, cols = prod_a.shape
    steps = 1024 // rows
    total = steps * (3072 // cols)
    product(right_ref, 0, block_ref, 0, prod_a)

    def place_of(t):
        return pl.multiple_of((t % steps) * rows, rows), pl.multiple_of((t // steps) * cols, cols)

    @pl.loop(0, total // 2)
    def _(i):
        left_a, right_a = place_of(i * 2)
        left_b, right_b = place_of(i * 2 + 1)
        left_c, right_c = place_of(jnp.minimum(i * 2 + 2, total - 1))
        product(right_ref, left_b, block_ref, right_b, prod_b)
        weigh(prod_a, left_a, left_meta, right_a, right_meta, keep, row_sum, col_sum, False)
        product(right_ref, left_c, block_ref, right_c, prod_a)
        weigh(prod_b, left_b, left_meta, right_b, right_meta, keep, row_sum, col_sum, False)

    right = rows_to_lanes(row_sum)
    own = cols_to_lanes(col_sum, 0)
    other = cols_to_lanes(col_sum, 1024)
    left = cols_to_lanes(col_sum, 2048)
    for u in range(8):
        row = slice(u, u + 1)
        stay_ref[0, row, :] = own[u] + near_ref[0, row, :]
        stay_ref[1, row, :] = right[u]
        stay_ref[2, row, :] = jnp.where(cross == 0, left[u], 0.0)
        move_ref[0, row, :] = other[u] + near_ref[1, row, :]
        move_ref[1, row, :] = jnp.where(cross == 0, 0.0, left[u])


FAR_TILE = (512, 512)


def pair_scratch(columns, tile):
    return [
        pltpu.VMEM((3, 1024, LANES), jnp.float32),
        pltpu.VMEM((2, 8, columns), jnp.float32),
        pltpu.VMEM((2, 8, columns), jnp.float32),
        pltpu.VMEM(tile, jnp.float32),
        pltpu.VMEM(tile, jnp.float32),
        pltpu.VMEM((1024, LANES), jnp.float32),
        pltpu.VMEM((8, columns), jnp.float32),
    ]


def near_pairs(scalars, keep, own, other, rows, cols):
    return pl.pallas_call(
        near_kernel,
        out_shape=(
            jax.ShapeDtypeStruct((2, 8, LANES), jnp.float32),
            jax.ShapeDtypeStruct((8, 2048), jnp.float32),
        ),
        in_specs=[smem(), smem(), vmem(), vmem(), vmem(), vmem()],
        out_specs=(vmem(), vmem()),
        scratch_shapes=pair_scratch(2048, (256, 512)),
        compiler_params=pltpu.CompilerParams(vmem_limit_bytes=VMEM),
        cost_estimate=pl.CostEstimate(flops=2 * 10**9, bytes_accessed=10**7, transcendentals=0),
        name="near_pairs",
    )(scalars, keep, own, other, rows, cols)


def far_pairs(scalars, keep, own, other, left, right, rows, cols, near):
    return pl.pallas_call(
        far_kernel,
        out_shape=(
            jax.ShapeDtypeStruct((3, 8, LANES), jnp.float32),
            jax.ShapeDtypeStruct((2, 8, LANES), jnp.float32),
        ),
        in_specs=[smem(), smem(), hbm(), hbm(), hbm()] + [vmem()] * 5,
        out_specs=(vmem(), vmem()),
        scratch_shapes=[pltpu.VMEM((3072, 256), jnp.bfloat16)]
        + pair_scratch(3072, FAR_TILE)
        + [pltpu.SemaphoreType.DMA((3,))],
        compiler_params=pltpu.CompilerParams(vmem_limit_bytes=VMEM),
        cost_estimate=pl.CostEstimate(flops=4 * 10**9, bytes_accessed=10**7, transcendentals=0),
        name="far_pairs",
    )(scalars, keep, own, other, left, right, rows, cols, *near)


def rank_kernel(place_ref, *refs):
    pieces, out_ref = refs[:-1], refs[-1]
    place_at = place_ref[...]
    lane = place_at & 127
    which = place_at >> 7
    total = jnp.zeros((32, LANES), jnp.float32)
    for s in range(4):
        block = pieces[s][0] + pieces[(s + 1) % 4][1] + pieces[(s + 3) % 4][2]
        for u in range(8):
            row = jnp.broadcast_to(block[u : u + 1, :], (32, LANES))
            value = jnp.take_along_axis(row, lane, axis=1)
            total = jnp.where(which == s * 8 + u, value, total)
    out_ref[...] = total * (1.0 / TILE)


def to_rank_order(place_at, pieces):
    return pl.pallas_call(
        rank_kernel,
        out_shape=jax.ShapeDtypeStruct((32, LANES), jnp.float32),
        in_specs=[vmem()] * 5,
        out_specs=vmem(),
        compiler_params=pltpu.CompilerParams(vmem_limit_bytes=VMEM),
        name="to_rank_order",
    )(place_at, *pieces)


def on_device(points, rank_source, thresholds, kept_tiles):
    bands = lax.axis_size("band")
    reps = lax.axis_size("rep")
    device = lax.axis_index("band").astype(jnp.int32)
    rep = lax.axis_index("rep").astype(jnp.int32)
    core = device & 1
    own_band = jnp.where(core == 0, device, bands - device)
    other_band = bands - 1 - own_band
    own_offset = jnp.where(own_band < bands // 2, 0, 2)
    other_offset = 2 - own_offset
    cross = (rep >= 2).astype(jnp.int32)
    left_offset = jnp.where(cross == 1, other_offset, own_offset)
    scalars = jnp.stack([
        device, rep * 16, rep, own_band, other_band, device, core,
        own_offset, other_offset, cross, left_offset,
    ]).astype(jnp.int32)
    codes = lax.dynamic_index_in_dim(kept_tiles, jnp.minimum(own_band, other_band), 0, keepdims=False)
    ids = jnp.arange(16, dtype=jnp.int32)
    a, c = ids // 4, ids % 4
    wanted = jnp.minimum(a, c) * 4 + jnp.maximum(a, c)
    keep = jnp.where(jnp.any(codes[:, None] == wanted[None, :], axis=0), 1.0, -1e30).astype(jnp.float32)

    rank2d = rank_source.reshape(2048, LANES)
    thr2d = thresholds.reshape(2048, LANES)

    def joint(move):
        return [
            (d * reps + r, e * reps + q)
            for d in range(bands)
            for r in range(reps)
            for e, q in (move(d, r),)
        ]

    def shift(value, move):
        return lax.ppermute(value, ("band", "rep"), joint(move))

    payload = send_rows(rank2d, points)
    own = lax.all_to_all(
        payload.reshape(bands, 16, 256), "band", split_axis=0, concat_axis=0, tiled=True
    ).reshape(1024, 256)
    own, rows, cols, place_at = lax.optimization_barrier((own, *place(scalars, rank2d, thr2d)))

    def to_right(d, r):
        q = (r + 1) % reps
        return (d if q < 2 else d ^ 1), q

    other = shift(own, lambda d, r: (d ^ 1, r))
    right = shift(own, lambda d, r: (d, (r - 1) % reps))
    left = shift(own, to_right)

    near = near_pairs(scalars, keep, own, other, rows, cols)
    stay, move = far_pairs(scalars, keep, own, other, left, right, rows, cols, near)
    moved = shift(move, lambda d, r: (d ^ 1, r))
    sums = stay + jnp.stack([moved[0], jnp.zeros_like(moved[0]), moved[1]])
    home = shift(sums, lambda d, r: (block_band(d), r))
    pieces = [home] + [
        shift(home, lambda d, r, s=s: (d, (r + s) % reps)) for s in range(1, reps)
    ]
    return to_rank_order(place_at, pieces).reshape(points.shape[0])


def solution(mesh):
    in_specs = (P("band", None), P(), P(), P())
    out_specs = P("band")
    return jax.shard_map(
        on_device, mesh=mesh, in_specs=in_specs, out_specs=out_specs, check_vma=False
    )
```

```python
import jax
import jax.numpy as jnp
from jax import lax
from jax.experimental import pallas as pl
from jax.experimental.pallas import tpu as pltpu
from jax.sharding import PartitionSpec as P

TILE = 2048
LANES = 128
SEND_VMEM = 60 * 1024 * 1024
VMEM = 28 * 1024 * 1024
NT = (((1,), (1,)), ((), ()))


def prefix_matrix():
    row = lax.broadcasted_iota(jnp.int32, (LANES, 2 * LANES), 0)
    col = lax.broadcasted_iota(jnp.int32, (LANES, 2 * LANES), 1)
    return jnp.where((row <= col) | (col >= LANES), 1.0, 0.0).astype(jnp.bfloat16)


def block_band(device):
    host = device ^ 8
    return host if host % 2 == 0 else 64 - host


def smem():
    return pl.BlockSpec(memory_space=pltpu.SMEM)


def vmem():
    return pl.BlockSpec(memory_space=pltpu.VMEM)


def hbm():
    return pl.BlockSpec(memory_space=pltpu.HBM)


def send_kernel(rank_hbm, points_hbm, out_ref, rank_ref, points_ref, acc_ref, row_ref,
                hot_ref, rank_sem, points_sem):
    def fetch_rank(g):
        rows = pl.ds(g * 256, 256)
        return pltpu.make_async_copy(rank_hbm.at[rows, :], rank_ref.at[rows, :], rank_sem.at[g])

    for g in range(8):
        fetch_rank(g).start()
    fetch_points = pltpu.make_async_copy(points_hbm, points_ref, points_sem)
    fetch_points.start()
    shard = lax.axis_index("band")
    prefix = prefix_matrix()
    base = (lax.axis_index("rep") * 16 + 1).astype(jnp.float32)
    ones = jnp.ones((LANES, LANES), jnp.bfloat16)
    for g in range(8):
        fetch_rank(g).wait()
        source = [rank_ref[pl.ds(g * 256 + j, 8, stride=32), :] for j in range(32)]
        mine = [(source[j] >> 12) == shard for j in range(32)]
        marks = jnp.concatenate([jnp.where(m, 1.0, 0.0) for m in mine], axis=0).astype(jnp.bfloat16)
        counts = jnp.dot(marks, prefix, preferred_element_type=jnp.float32)
        carry = jnp.zeros((8, LANES), jnp.float32) - base
        accs = [jnp.zeros((8, LANES), jnp.int32) for _ in range(16)]
        for j in range(32):
            pos = jnp.where(mine[j], carry + counts[j * 8 : j * 8 + 8, :LANES], -1.0)
            loc = source[j] & 4095
            carry = carry + counts[j * 8 : j * 8 + 8, LANES:]
            for i in range(16):
                accs[i] = jnp.where(pos == float(i), loc, accs[i])
        for i in range(16):
            acc_ref[g * 128 + i * 8 : g * 128 + i * 8 + 8, :] = accs[i]

    acc = acc_ref[...]
    high = (acc >> 6).astype(jnp.float32).astype(jnp.bfloat16)
    low = (acc & 63).astype(jnp.float32).astype(jnp.bfloat16)
    row_ref[...] = 64.0 * jnp.dot(high, ones, preferred_element_type=jnp.float32) + jnp.dot(
        low, ones, preferred_element_type=jnp.float32
    )
    fetch_points.wait()
    lane = lax.broadcasted_iota(jnp.int32, (1024, LANES), 1)
    one = jnp.ones((1024, LANES), jnp.bfloat16)
    zero = jnp.zeros((1024, LANES), jnp.bfloat16)
    parts = []
    for i in range(64):
        band = block_band(i)
        parts.append(row_ref[pl.ds((band // 8) * 128 + band % 8, 16, stride=8), :])
    local = jnp.concatenate(parts, axis=0).astype(jnp.int32)
    chunk = (local >> 7).astype(jnp.float32).astype(jnp.bfloat16)
    hot = jnp.where((local & 127) == lane, 1.0, 0.0).astype(jnp.bfloat16)
    for ch in range(32):
        hot_ref[:, ch * 128 : (ch + 1) * 128] = jnp.where(chunk == one * ch, hot, zero)
    out_ref[...] = jnp.dot(
        hot_ref[...], points_ref[...], preferred_element_type=jnp.float32
    ).astype(jnp.bfloat16)


def send_rows(rank2d, points):
    return pl.pallas_call(
        send_kernel,
        out_shape=jax.ShapeDtypeStruct((1024, 256), jnp.bfloat16),
        in_specs=[hbm(), hbm()],
        out_specs=vmem(),
        scratch_shapes=[
            pltpu.VMEM((2048, LANES), jnp.int32),
            pltpu.VMEM((4096, 256), jnp.bfloat16),
            pltpu.VMEM((1024, LANES), jnp.int32),
            pltpu.VMEM((1024, LANES), jnp.float32),
            pltpu.VMEM((1024, 4096), jnp.bfloat16),
            pltpu.SemaphoreType.DMA((8,)),
            pltpu.SemaphoreType.DMA,
        ],
        compiler_params=pltpu.CompilerParams(vmem_limit_bytes=SEND_VMEM),
        name="send_rows",
    )(rank2d, points)


def place_kernel(s_ref, rank_hbm, thr_hbm, row_ref, col_ref, place_ref, u_ref, v_ref, rank_ref, thr_ref, sems):
    copies = []
    for x in range(3):
        start = pl.multiple_of(s_ref[3 + x] * 32, 32)
        copies.append((
            pltpu.make_async_copy(rank_hbm.at[pl.ds(start, 32), :], rank_ref.at[x], sems.at[x, 0]),
            pltpu.make_async_copy(thr_hbm.at[pl.ds(start, 32), :], thr_ref.at[x], sems.at[x, 1]),
        ))
        for copy in copies[x]:
            copy.start()
    rep = s_ref[2]
    prefix = prefix_matrix()
    shard_iota = lax.broadcasted_iota(jnp.int32, (64, LANES), 0)
    u_iota = lax.broadcasted_iota(jnp.int32, (32, LANES), 0)
    v_iota = lax.broadcasted_iota(jnp.int32, (LANES, LANES), 0)
    for x in range(3):
        for copy in copies[x]:
            copy.wait()
        carry = jnp.zeros((64, LANES), jnp.float32)
        source = rank_ref[x] >> 12
        thr = thr_ref[x]
        for j in range(32):
            shard = source[j : j + 1, :]
            hot = shard == shard_iota
            counts = jnp.dot(
                jnp.where(hot, 1.0, 0.0).astype(jnp.bfloat16), prefix, preferred_element_type=jnp.float32
            )
            slot = jnp.sum(jnp.where(hot, carry + counts[:, :LANES], 0.0), axis=0, keepdims=True)
            slot = slot.astype(jnp.int32) - 1
            carry = carry + counts[:, LANES:]
            quarter = slot >> 4
            v = (shard & 7) * 16 + (slot & 15)
            if x == 2:
                place_ref[j : j + 1, :] = (((rep - quarter) & 3) * 8 + (shard >> 3)) * 128 + v
            else:
                u = ((quarter - rep) & 3) * 8 + (shard >> 3)
                u_hot = u == u_iota
                t = thr[j : j + 1, :]
                lanes = slice(j * LANES, (j + 1) * LANES)
                u_ref[0:32, lanes] = jnp.where(u_hot, (t >> 4).astype(jnp.float32), 0.0).astype(jnp.bfloat16)
                u_ref[32:64, lanes] = jnp.where(u_hot, (t & 15).astype(jnp.float32), 0.0).astype(jnp.bfloat16)
                u_ref[64:96, lanes] = jnp.where(u_hot, float(j >= 16), 0.0).astype(jnp.bfloat16)
                v_ref[:, lanes] = jnp.where(v == v_iota, 1.0, 0.0).astype(jnp.bfloat16)
        if x < 2:
            us = u_ref[...]
            vs = v_ref[...]
            rows = lax.dot_general(us, vs, NT, preferred_element_type=jnp.float32)
            cols = lax.dot_general(vs, us, NT, preferred_element_type=jnp.float32)
            row_ref[x, 0:32, :] = 1024.0 / (rows[0:32] * 16.0 + rows[32:64])
            row_ref[x, 32:64, :] = rows[64:96]
            col_ref[x, :, 0:32] = 1024.0 / (cols[:, 0:32] * 16.0 + cols[:, 32:64])
            col_ref[x, :, 32:64] = cols[:, 64:96]


def place(scalars, rank2d, thr2d):
    return pl.pallas_call(
        place_kernel,
        out_shape=(
            jax.ShapeDtypeStruct((2, 64, LANES), jnp.float32),
            jax.ShapeDtypeStruct((2, LANES, 64), jnp.float32),
            jax.ShapeDtypeStruct((32, LANES), jnp.int32),
        ),
        in_specs=[smem(), hbm(), hbm()],
        out_specs=(vmem(),) * 3,
        scratch_shapes=[
            pltpu.VMEM((96, 4096), jnp.bfloat16),
            pltpu.VMEM((LANES, 4096), jnp.bfloat16),
            pltpu.VMEM((3, 32, LANES), jnp.int32),
            pltpu.VMEM((3, 32, LANES), jnp.int32),
            pltpu.SemaphoreType.DMA((3, 2)),
        ],
        compiler_params=pltpu.CompilerParams(vmem_limit_bytes=VMEM),
        cost_estimate=pl.CostEstimate(flops=2 * 10**9, bytes_accessed=10**7, transcendentals=0),
        name="place",
    )(scalars, rank2d, thr2d)


def square_sums(block):
    values = block.astype(jnp.float32)
    square = values * values
    total = square[:, :LANES] + square[:, LANES:]
    high = total.astype(jnp.bfloat16)
    rest = total - high.astype(jnp.float32)
    middle = rest.astype(jnp.bfloat16)
    low = (rest - middle.astype(jnp.float32)).astype(jnp.bfloat16)
    return high, middle, low


def inverse_column(terms):
    ones = jnp.ones((LANES, LANES), jnp.bfloat16)
    high, middle, low = (jnp.dot(t, ones, preferred_element_type=jnp.float32) for t in terms)
    return lax.rsqrt(high + (middle + low) + 1e-06)


def inverse_row(terms):
    ones = jnp.ones((8, LANES), jnp.bfloat16)
    high, middle, low = (
        lax.dot_general(ones, t, NT, preferred_element_type=jnp.float32) for t in terms
    )
    return lax.rsqrt(high + (middle + low) + 1e-06)


def load_column_meta(col_ref, band, quarter, meta):
    for u in range(8):
        rows = slice(u * LANES, (u + 1) * LANES)
        i = quarter * 8 + u
        meta[1, rows, :] = jnp.broadcast_to(col_ref[band, :, i : i + 1], (LANES, LANES))
        meta[2, rows, :] = jnp.broadcast_to(col_ref[band, :, 32 + i : 33 + i], (LANES, LANES))


def load_row_meta(at, row_ref, band, quarter, keep_ref, row_offset, col_offset, meta, keep):
    for u in range(8):
        lanes = slice(at + u * LANES, at + (u + 1) * LANES)
        i = quarter * 8 + u
        meta[1, :, lanes] = jnp.broadcast_to(row_ref[band, i : i + 1, :], (8, LANES))
        upper = jnp.broadcast_to(row_ref[band, 32 + i : 33 + i, :], (8, LANES)) > 0.5
        for t in range(2):
            code = (row_offset + t) * 4 + col_offset
            keep[t, :, lanes] = jnp.where(upper, keep_ref[code + 1], keep_ref[code])


def product(left_ref, left_at, right_ref, right_at, prod_ref):
    rows, cols = prod_ref.shape
    prod_ref[...] = lax.dot_general(
        left_ref[pl.ds(left_at, rows), :], right_ref[pl.ds(right_at, cols), :], NT,
        preferred_element_type=jnp.float32,
    )


def weigh(prod_ref, left_at, left_meta, right_at, right_meta, keep, row_sum, col_sum, diagonal):
    chunks = prod_ref.shape[1] // LANES
    sums = [jnp.zeros((8, LANES), jnp.float32) for _ in range(chunks)]
    lanes = [pl.ds(pl.multiple_of(right_at + ch * LANES, LANES), LANES) for ch in range(chunks)]
    for i in range(prod_ref.shape[0] // 32):
        rows = pl.ds(pl.multiple_of(left_at + i * 32, 32), 32)
        inv_i = left_meta[0, rows, :].reshape(4, 8, LANES)
        rho_i = left_meta[1, rows, :].reshape(4, 8, LANES)
        upper = left_meta[2, rows, :].reshape(4, 8, LANES) > 0.5
        total = row_sum[rows, :].reshape(4, 8, LANES)
        for ch in range(chunks):
            inv_j = right_meta[0, :, lanes[ch]][None]
            rho_j = right_meta[1, :, lanes[ch]][None]
            kept = jnp.where(upper, keep[1, :, lanes[ch]][None], keep[0, :, lanes[ch]][None])
            p = prod_ref[i * 32 : i * 32 + 32, ch * LANES : (ch + 1) * LANES].reshape(4, 8, LANES)
            near = (p * inv_i) * inv_j - 1.0
            w = jnp.maximum(near * jnp.maximum(rho_i, rho_j) + kept, 0.0)
            if diagonal:
                row_ids = lax.broadcasted_iota(jnp.int32, w.shape, 0) * 8 + lax.broadcasted_iota(jnp.int32, w.shape, 1)
                col_ids = lax.broadcasted_iota(jnp.int32, w.shape, 2)
                w = jnp.where(row_ids + (left_at + i * 32) == col_ids + (right_at + ch * LANES), 0.0, w)
            total = total + w
            if not diagonal:
                sums[ch] = sums[ch] + ((w[0] + w[1]) + (w[2] + w[3]))
        row_sum[rows, :] = total.reshape(32, LANES)
    if not diagonal:
        for ch in range(chunks):
            col_sum[:, lanes[ch]] += sums[ch]


def rows_to_lanes(row_sum):
    row = lax.broadcasted_iota(jnp.int32, (LANES, LANES), 0)
    lane = lax.broadcasted_iota(jnp.int32, (LANES, LANES), 1)
    out = []
    for u in range(8):
        total = jnp.sum(row_sum[u * LANES : (u + 1) * LANES, :], axis=1, keepdims=True)
        out.append(jnp.sum(jnp.where(row == lane, total, 0.0), axis=0, keepdims=True))
    return out


def cols_to_lanes(col_sum, at):
    return [
        jnp.sum(col_sum[:, at + u * LANES : at + (u + 1) * LANES], axis=0, keepdims=True)
        for u in range(8)
    ]


def near_kernel(s_ref, keep_ref, own_ref, other_ref, row_ref, col_ref, out_ref, inverse_ref,
                left_meta, right_meta, keep, prod_a, prod_b, row_sum, col_sum):
    core = s_ref[6]
    own_offset = s_ref[7]
    other_offset = s_ref[8]
    terms = square_sums(own_ref[...])
    left_meta[0] = inverse_column(terms)
    right_meta[0, :, 0:1024] = inverse_row(terms)
    right_meta[0, :, 1024:2048] = inverse_row(square_sums(other_ref[...]))
    inverse_ref[...] = right_meta[0]
    load_column_meta(col_ref, 0, 0, left_meta)
    load_row_meta(0, row_ref, 0, 0, keep_ref, own_offset, own_offset, right_meta, keep)
    load_row_meta(1024, row_ref, 1, 0, keep_ref, own_offset, other_offset, right_meta, keep)
    row_sum[...] = jnp.zeros_like(row_sum)
    col_sum[...] = jnp.zeros_like(col_sum)

    @pl.loop(0, 4)
    def _(i):
        at = pl.multiple_of(i * 256, 256)
        half = pl.multiple_of(((i >> 1) ^ core) * 512, 512)
        product(own_ref, at, own_ref, 0, prod_a)
        product(own_ref, at, own_ref, 512, prod_b)
        weigh(prod_a, at, left_meta, 0, right_meta, keep, row_sum, col_sum, True)
        product(own_ref, at, other_ref, half, prod_a)
        weigh(prod_b, at, left_meta, 512, right_meta, keep, row_sum, col_sum, True)
        weigh(prod_a, at, left_meta, 1024 + half, right_meta, keep, row_sum, col_sum, False)

    own = rows_to_lanes(row_sum)
    other = cols_to_lanes(col_sum, 1024)
    for u in range(8):
        out_ref[0, u : u + 1, :] = own[u]
        out_ref[1, u : u + 1, :] = other[u]


def far_kernel(s_ref, keep_ref, own_hbm, other_hbm, left_hbm, right_ref, row_ref, col_ref, near_ref,
               inverse_ref, stay_ref, move_ref, block_ref, left_meta, right_meta, keep, prod_a,
               prod_b, row_sum, col_sum, sems):
    own_offset = s_ref[7]
    other_offset = s_ref[8]
    cross = s_ref[9]
    left_offset = s_ref[10]
    copies = [
        pltpu.make_async_copy(source, block_ref.at[pl.ds(i * 1024, 1024), :], sems.at[i])
        for i, source in enumerate((own_hbm, other_hbm, left_hbm))
    ]
    for copy in copies:
        copy.start()
    left_meta[0] = inverse_column(square_sums(right_ref[...]))
    load_column_meta(col_ref, 0, 1, left_meta)
    load_row_meta(0, row_ref, 0, 0, keep_ref, own_offset, own_offset, right_meta, keep)
    load_row_meta(1024, row_ref, 1, 0, keep_ref, own_offset, other_offset, right_meta, keep)
    load_row_meta(2048, row_ref, cross, 3, keep_ref, own_offset, left_offset, right_meta, keep)
    right_meta[0, :, 0:2048] = inverse_ref[...]
    row_sum[...] = jnp.zeros_like(row_sum)
    col_sum[...] = jnp.zeros_like(col_sum)
    for copy in copies:
        copy.wait()
    right_meta[0, :, 2048:3072] = inverse_row(square_sums(block_ref[2048:3072, :]))
    rows, cols = prod_a.shape
    steps = 1024 // rows
    total = steps * (3072 // cols)
    product(right_ref, 0, block_ref, 0, prod_a)

    def place_of(t):
        return pl.multiple_of((t % steps) * rows, rows), pl.multiple_of((t // steps) * cols, cols)

    @pl.loop(0, total // 2)
    def _(i):
        left_a, right_a = place_of(i * 2)
        left_b, right_b = place_of(i * 2 + 1)
        left_c, right_c = place_of(jnp.minimum(i * 2 + 2, total - 1))
        product(right_ref, left_b, block_ref, right_b, prod_b)
        weigh(prod_a, left_a, left_meta, right_a, right_meta, keep, row_sum, col_sum, False)
        product(right_ref, left_c, block_ref, right_c, prod_a)
        weigh(prod_b, left_b, left_meta, right_b, right_meta, keep, row_sum, col_sum, False)

    right = rows_to_lanes(row_sum)
    own = cols_to_lanes(col_sum, 0)
    other = cols_to_lanes(col_sum, 1024)
    left = cols_to_lanes(col_sum, 2048)
    for u in range(8):
        row = slice(u, u + 1)
        stay_ref[0, row, :] = own[u] + near_ref[0, row, :]
        stay_ref[1, row, :] = right[u]
        stay_ref[2, row, :] = jnp.where(cross == 0, left[u], 0.0)
        move_ref[0, row, :] = other[u] + near_ref[1, row, :]
        move_ref[1, row, :] = jnp.where(cross == 0, 0.0, left[u])


FAR_TILE = (512, 512)


def pair_scratch(columns, tile):
    return [
        pltpu.VMEM((3, 1024, LANES), jnp.float32),
        pltpu.VMEM((2, 8, columns), jnp.float32),
        pltpu.VMEM((2, 8, columns), jnp.float32),
        pltpu.VMEM(tile, jnp.float32),
        pltpu.VMEM(tile, jnp.float32),
        pltpu.VMEM((1024, LANES), jnp.float32),
        pltpu.VMEM((8, columns), jnp.float32),
    ]


def near_pairs(scalars, keep, own, other, rows, cols):
    return pl.pallas_call(
        near_kernel,
        out_shape=(
            jax.ShapeDtypeStruct((2, 8, LANES), jnp.float32),
            jax.ShapeDtypeStruct((8, 2048), jnp.float32),
        ),
        in_specs=[smem(), smem(), vmem(), vmem(), vmem(), vmem()],
        out_specs=(vmem(), vmem()),
        scratch_shapes=pair_scratch(2048, (256, 512)),
        compiler_params=pltpu.CompilerParams(vmem_limit_bytes=VMEM),
        cost_estimate=pl.CostEstimate(flops=2 * 10**9, bytes_accessed=10**7, transcendentals=0),
        name="near_pairs",
    )(scalars, keep, own, other, rows, cols)


def far_pairs(scalars, keep, own, other, left, right, rows, cols, near):
    return pl.pallas_call(
        far_kernel,
        out_shape=(
            jax.ShapeDtypeStruct((3, 8, LANES), jnp.float32),
            jax.ShapeDtypeStruct((2, 8, LANES), jnp.float32),
        ),
        in_specs=[smem(), smem(), hbm(), hbm(), hbm()] + [vmem()] * 5,
        out_specs=(vmem(), vmem()),
        scratch_shapes=[pltpu.VMEM((3072, 256), jnp.bfloat16)]
        + pair_scratch(3072, FAR_TILE)
        + [pltpu.SemaphoreType.DMA((3,))],
        compiler_params=pltpu.CompilerParams(vmem_limit_bytes=VMEM),
        cost_estimate=pl.CostEstimate(flops=4 * 10**9, bytes_accessed=10**7, transcendentals=0),
        name="far_pairs",
    )(scalars, keep, own, other, left, right, rows, cols, *near)


def rank_kernel(place_ref, *refs):
    pieces, out_ref = refs[:-1], refs[-1]
    place_at = place_ref[...]
    lane = place_at & 127
    which = place_at >> 7
    total = jnp.zeros((32, LANES), jnp.float32)
    for s in range(4):
        block = pieces[s][0] + pieces[(s + 1) % 4][1] + pieces[(s + 3) % 4][2]
        for u in range(8):
            row = jnp.broadcast_to(block[u : u + 1, :], (32, LANES))
            value = jnp.take_along_axis(row, lane, axis=1)
            total = jnp.where(which == s * 8 + u, value, total)
    out_ref[...] = total * (1.0 / TILE)


def to_rank_order(place_at, pieces):
    return pl.pallas_call(
        rank_kernel,
        out_shape=jax.ShapeDtypeStruct((32, LANES), jnp.float32),
        in_specs=[vmem()] * 5,
        out_specs=vmem(),
        compiler_params=pltpu.CompilerParams(vmem_limit_bytes=VMEM),
        name="to_rank_order",
    )(place_at, *pieces)


def on_device(points, rank_source, thresholds, kept_tiles):
    bands = lax.axis_size("band")
    reps = lax.axis_size("rep")
    device = lax.axis_index("band").astype(jnp.int32)
    rep = lax.axis_index("rep").astype(jnp.int32)
    core = device & 1
    host = device ^ 8
    own_band = jnp.where(core == 0, host, bands - host)
    other_band = bands - 1 - own_band
    own_offset = jnp.where(own_band < bands // 2, 0, 2)
    other_offset = 2 - own_offset
    cross = (rep >= 2).astype(jnp.int32)
    left_offset = jnp.where(cross == 1, other_offset, own_offset)
    scalars = jnp.stack([
        device, rep * 16, rep, own_band, other_band, device, core,
        own_offset, other_offset, cross, left_offset,
    ]).astype(jnp.int32)
    codes = lax.dynamic_index_in_dim(kept_tiles, jnp.minimum(own_band, other_band), 0, keepdims=False)
    ids = jnp.arange(16, dtype=jnp.int32)
    a, c = ids // 4, ids % 4
    wanted = jnp.minimum(a, c) * 4 + jnp.maximum(a, c)
    keep = jnp.where(jnp.any(codes[:, None] == wanted[None, :], axis=0), 1.0, -1e30).astype(jnp.float32)

    rank2d = rank_source.reshape(2048, LANES)
    thr2d = thresholds.reshape(2048, LANES)

    def joint(move):
        return [
            (d * reps + r, e * reps + q)
            for d in range(bands)
            for r in range(reps)
            for e, q in (move(d, r),)
        ]

    def shift(value, move):
        return lax.ppermute(value, ("band", "rep"), joint(move))

    payload = send_rows(rank2d, points)
    own = lax.all_to_all(
        payload.reshape(bands, 16, 256), "band", split_axis=0, concat_axis=0, tiled=True
    ).reshape(1024, 256)
    own, rows, cols, place_at = lax.optimization_barrier((own, *place(scalars, rank2d, thr2d)))

    def to_right(d, r):
        q = (r + 1) % reps
        return (d if q < 2 else d ^ 1), q

    other = shift(own, lambda d, r: (d ^ 1, r))
    right = shift(own, lambda d, r: (d, (r - 1) % reps))
    left = shift(own, to_right)

    near = near_pairs(scalars, keep, own, other, rows, cols)
    stay, move = far_pairs(scalars, keep, own, other, left, right, rows, cols, near)
    moved = shift(move, lambda d, r: (d ^ 1, r))
    sums = stay + jnp.stack([moved[0], jnp.zeros_like(moved[0]), moved[1]])
    home = shift(sums, lambda d, r: (block_band(d), r))
    pieces = [home] + [
        shift(home, lambda d, r, s=s: (d, (r + s) % reps)) for s in range(1, reps)
    ]
    return to_rank_order(place_at, pieces).reshape(points.shape[0])


def solution(mesh):
    in_specs = (P("band", None), P(), P(), P())
    out_specs = P("band")
    return jax.shard_map(
        on_device, mesh=mesh, in_specs=in_specs, out_specs=out_specs, check_vma=False
    )
```

```python
import jax
import jax.numpy as jnp
from jax import lax
from jax.experimental import pallas as pl
from jax.experimental.pallas import tpu as pltpu
from jax.sharding import PartitionSpec as P

TILE = 2048
LANES = 128
SEND_VMEM = 60 * 1024 * 1024
VMEM = 28 * 1024 * 1024
NT = (((1,), (1,)), ((), ()))


def prefix_matrix():
    row = lax.broadcasted_iota(jnp.int32, (LANES, 2 * LANES), 0)
    col = lax.broadcasted_iota(jnp.int32, (LANES, 2 * LANES), 1)
    return jnp.where((row <= col) | (col >= LANES), 1.0, 0.0).astype(jnp.bfloat16)


def block_band(device):
    host = device ^ 8
    return host if host % 2 == 0 else 64 - host


def smem():
    return pl.BlockSpec(memory_space=pltpu.SMEM)


def vmem():
    return pl.BlockSpec(memory_space=pltpu.VMEM)


def hbm():
    return pl.BlockSpec(memory_space=pltpu.HBM)


def send_kernel(rank_hbm, points_hbm, out_ref, rank_ref, points_ref, acc_ref, row_ref,
                hot_ref, rank_sem, points_sem):
    def fetch_rank(g):
        rows = pl.ds(g * 256, 256)
        return pltpu.make_async_copy(rank_hbm.at[rows, :], rank_ref.at[rows, :], rank_sem.at[g])

    for g in range(8):
        fetch_rank(g).start()
    fetch_points = pltpu.make_async_copy(points_hbm, points_ref, points_sem)
    fetch_points.start()
    shard = lax.axis_index("band")
    prefix = prefix_matrix()
    base = (lax.axis_index("rep") * 16 + 1).astype(jnp.float32)
    ones = jnp.ones((LANES, LANES), jnp.bfloat16)
    for g in range(8):
        fetch_rank(g).wait()
        source = [rank_ref[pl.ds(g * 256 + j, 8, stride=32), :] for j in range(32)]
        mine = [(source[j] >> 12) == shard for j in range(32)]
        marks = jnp.concatenate([jnp.where(m, 1.0, 0.0) for m in mine], axis=0).astype(jnp.bfloat16)
        counts = jnp.dot(marks, prefix, preferred_element_type=jnp.float32)
        carry = jnp.zeros((8, LANES), jnp.float32) - base
        accs = [jnp.zeros((8, LANES), jnp.int32) for _ in range(16)]
        for j in range(32):
            pos = jnp.where(mine[j], carry + counts[j * 8 : j * 8 + 8, :LANES], -1.0)
            loc = source[j] & 4095
            carry = carry + counts[j * 8 : j * 8 + 8, LANES:]
            for i in range(16):
                accs[i] = jnp.where(pos == float(i), loc, accs[i])
        for i in range(16):
            acc_ref[g * 128 + i * 8 : g * 128 + i * 8 + 8, :] = accs[i]

    acc = acc_ref[...]
    high = (acc >> 6).astype(jnp.float32).astype(jnp.bfloat16)
    low = (acc & 63).astype(jnp.float32).astype(jnp.bfloat16)
    row_ref[...] = 64.0 * jnp.dot(high, ones, preferred_element_type=jnp.float32) + jnp.dot(
        low, ones, preferred_element_type=jnp.float32
    )
    fetch_points.wait()
    lane = lax.broadcasted_iota(jnp.int32, (1024, LANES), 1)
    one = jnp.ones((1024, LANES), jnp.bfloat16)
    zero = jnp.zeros((1024, LANES), jnp.bfloat16)
    parts = []
    for i in range(64):
        band = block_band(i)
        parts.append(row_ref[pl.ds((band // 8) * 128 + band % 8, 16, stride=8), :])
    local = jnp.concatenate(parts, axis=0).astype(jnp.int32)
    chunk = (local >> 7).astype(jnp.float32).astype(jnp.bfloat16)
    hot = jnp.where((local & 127) == lane, 1.0, 0.0).astype(jnp.bfloat16)
    for ch in range(32):
        hot_ref[:, ch * 128 : (ch + 1) * 128] = jnp.where(chunk == one * ch, hot, zero)
    out_ref[...] = jnp.dot(
        hot_ref[...], points_ref[...], preferred_element_type=jnp.float32
    ).astype(jnp.bfloat16)


def send_rows(rank2d, points):
    return pl.pallas_call(
        send_kernel,
        out_shape=jax.ShapeDtypeStruct((1024, 256), jnp.bfloat16),
        in_specs=[hbm(), hbm()],
        out_specs=vmem(),
        scratch_shapes=[
            pltpu.VMEM((2048, LANES), jnp.int32),
            pltpu.VMEM((4096, 256), jnp.bfloat16),
            pltpu.VMEM((1024, LANES), jnp.int32),
            pltpu.VMEM((1024, LANES), jnp.float32),
            pltpu.VMEM((1024, 4096), jnp.bfloat16),
            pltpu.SemaphoreType.DMA((8,)),
            pltpu.SemaphoreType.DMA,
        ],
        compiler_params=pltpu.CompilerParams(vmem_limit_bytes=SEND_VMEM),
        name="send_rows",
    )(rank2d, points)


def place_kernel(s_ref, rank_hbm, thr_hbm, row_ref, col_ref, place_ref, u_ref, v_ref, rank_ref, thr_ref, sems):
    copies = []
    for x in range(3):
        start = pl.multiple_of(s_ref[3 + x] * 32, 32)
        copies.append((
            pltpu.make_async_copy(rank_hbm.at[pl.ds(start, 32), :], rank_ref.at[x], sems.at[x, 0]),
            pltpu.make_async_copy(thr_hbm.at[pl.ds(start, 32), :], thr_ref.at[x], sems.at[x, 1]),
        ))
        for copy in copies[x]:
            copy.start()
    rep = s_ref[2]
    prefix = prefix_matrix()
    shard_iota = lax.broadcasted_iota(jnp.int32, (64, LANES), 0)
    u_iota = lax.broadcasted_iota(jnp.int32, (32, LANES), 0)
    v_iota = lax.broadcasted_iota(jnp.int32, (LANES, LANES), 0)
    for x in range(3):
        for copy in copies[x]:
            copy.wait()
        carry = jnp.zeros((64, LANES), jnp.float32)
        source = rank_ref[x] >> 12
        thr = thr_ref[x]
        for j in range(32):
            shard = source[j : j + 1, :]
            hot = shard == shard_iota
            counts = jnp.dot(
                jnp.where(hot, 1.0, 0.0).astype(jnp.bfloat16), prefix, preferred_element_type=jnp.float32
            )
            slot = jnp.sum(jnp.where(hot, carry + counts[:, :LANES], 0.0), axis=0, keepdims=True)
            slot = slot.astype(jnp.int32) - 1
            carry = carry + counts[:, LANES:]
            quarter = slot >> 4
            v = (shard & 7) * 16 + (slot & 15)
            if x == 2:
                place_ref[j : j + 1, :] = (((rep - quarter) & 3) * 8 + (shard >> 3)) * 128 + v
            else:
                u = ((quarter - rep) & 3) * 8 + (shard >> 3)
                u_hot = u == u_iota
                t = thr[j : j + 1, :]
                lanes = slice(j * LANES, (j + 1) * LANES)
                u_ref[0:32, lanes] = jnp.where(u_hot, (t >> 4).astype(jnp.float32), 0.0).astype(jnp.bfloat16)
                u_ref[32:64, lanes] = jnp.where(u_hot, (t & 15).astype(jnp.float32), 0.0).astype(jnp.bfloat16)
                u_ref[64:96, lanes] = jnp.where(u_hot, float(j >= 16), 0.0).astype(jnp.bfloat16)
                v_ref[:, lanes] = jnp.where(v == v_iota, 1.0, 0.0).astype(jnp.bfloat16)
        if x < 2:
            us = u_ref[...]
            vs = v_ref[...]
            rows = lax.dot_general(us, vs, NT, preferred_element_type=jnp.float32)
            cols = lax.dot_general(vs, us, NT, preferred_element_type=jnp.float32)
            row_ref[x, 0:32, :] = 1024.0 / (rows[0:32] * 16.0 + rows[32:64])
            row_ref[x, 32:64, :] = rows[64:96]
            col_ref[x, :, 0:32] = 1024.0 / (cols[:, 0:32] * 16.0 + cols[:, 32:64])
            col_ref[x, :, 32:64] = cols[:, 64:96]


def place(scalars, rank2d, thr2d):
    return pl.pallas_call(
        place_kernel,
        out_shape=(
            jax.ShapeDtypeStruct((2, 64, LANES), jnp.float32),
            jax.ShapeDtypeStruct((2, LANES, 64), jnp.float32),
            jax.ShapeDtypeStruct((32, LANES), jnp.int32),
        ),
        in_specs=[smem(), hbm(), hbm()],
        out_specs=(vmem(),) * 3,
        scratch_shapes=[
            pltpu.VMEM((96, 4096), jnp.bfloat16),
            pltpu.VMEM((LANES, 4096), jnp.bfloat16),
            pltpu.VMEM((3, 32, LANES), jnp.int32),
            pltpu.VMEM((3, 32, LANES), jnp.int32),
            pltpu.SemaphoreType.DMA((3, 2)),
        ],
        compiler_params=pltpu.CompilerParams(vmem_limit_bytes=VMEM),
        cost_estimate=pl.CostEstimate(flops=2 * 10**9, bytes_accessed=10**7, transcendentals=0),
        name="place",
    )(scalars, rank2d, thr2d)


def square_sums(block):
    values = block.astype(jnp.float32)
    square = values * values
    total = square[:, :LANES] + square[:, LANES:]
    high = total.astype(jnp.bfloat16)
    rest = total - high.astype(jnp.float32)
    middle = rest.astype(jnp.bfloat16)
    low = (rest - middle.astype(jnp.float32)).astype(jnp.bfloat16)
    return high, middle, low


def inverse_column(terms):
    ones = jnp.ones((LANES, LANES), jnp.bfloat16)
    high, middle, low = (jnp.dot(t, ones, preferred_element_type=jnp.float32) for t in terms)
    return lax.rsqrt(high + (middle + low) + 1e-06)


def inverse_row(terms):
    ones = jnp.ones((8, LANES), jnp.bfloat16)
    high, middle, low = (
        lax.dot_general(ones, t, NT, preferred_element_type=jnp.float32) for t in terms
    )
    return lax.rsqrt(high + (middle + low) + 1e-06)


def load_column_meta(col_ref, band, quarter, meta):
    for u in range(8):
        rows = slice(u * LANES, (u + 1) * LANES)
        i = quarter * 8 + u
        meta[1, rows, :] = jnp.broadcast_to(col_ref[band, :, i : i + 1], (LANES, LANES))
        meta[2, rows, :] = jnp.broadcast_to(col_ref[band, :, 32 + i : 33 + i], (LANES, LANES))


def load_row_meta(at, row_ref, band, quarter, keep_ref, row_offset, col_offset, meta, keep):
    for u in range(8):
        lanes = slice(at + u * LANES, at + (u + 1) * LANES)
        i = quarter * 8 + u
        meta[1, :, lanes] = jnp.broadcast_to(row_ref[band, i : i + 1, :], (8, LANES))
        upper = jnp.broadcast_to(row_ref[band, 32 + i : 33 + i, :], (8, LANES)) > 0.5
        for t in range(2):
            code = (row_offset + t) * 4 + col_offset
            keep[t, :, lanes] = jnp.where(upper, keep_ref[code + 1], keep_ref[code])


def product(left_ref, left_at, right_ref, right_at, prod_ref):
    rows, cols = prod_ref.shape
    prod_ref[...] = lax.dot_general(
        left_ref[pl.ds(left_at, rows), :], right_ref[pl.ds(right_at, cols), :], NT,
        preferred_element_type=jnp.float32,
    )


def weigh(prod_ref, left_at, left_meta, right_at, right_meta, keep, row_sum, col_sum, diagonal):
    chunks = prod_ref.shape[1] // LANES
    sums = [jnp.zeros((8, LANES), jnp.float32) for _ in range(chunks)]
    lanes = [pl.ds(pl.multiple_of(right_at + ch * LANES, LANES), LANES) for ch in range(chunks)]
    for i in range(prod_ref.shape[0] // 32):
        rows = pl.ds(pl.multiple_of(left_at + i * 32, 32), 32)
        inv_i = left_meta[0, rows, :].reshape(4, 8, LANES)
        rho_i = left_meta[1, rows, :].reshape(4, 8, LANES)
        upper = left_meta[2, rows, :].reshape(4, 8, LANES) > 0.5
        total = row_sum[rows, :].reshape(4, 8, LANES)
        for ch in range(chunks):
            inv_j = right_meta[0, :, lanes[ch]][None]
            rho_j = right_meta[1, :, lanes[ch]][None]
            kept = jnp.where(upper, keep[1, :, lanes[ch]][None], keep[0, :, lanes[ch]][None])
            p = prod_ref[i * 32 : i * 32 + 32, ch * LANES : (ch + 1) * LANES].reshape(4, 8, LANES)
            near = (p * inv_i) * inv_j - 1.0
            w = jnp.maximum(near * jnp.maximum(rho_i, rho_j) + kept, 0.0)
            if diagonal:
                row_ids = lax.broadcasted_iota(jnp.int32, w.shape, 0) * 8 + lax.broadcasted_iota(jnp.int32, w.shape, 1)
                col_ids = lax.broadcasted_iota(jnp.int32, w.shape, 2)
                w = jnp.where(row_ids + (left_at + i * 32) == col_ids + (right_at + ch * LANES), 0.0, w)
            total = total + w
            if not diagonal:
                sums[ch] = sums[ch] + ((w[0] + w[1]) + (w[2] + w[3]))
        row_sum[rows, :] = total.reshape(32, LANES)
    if not diagonal:
        for ch in range(chunks):
            col_sum[:, lanes[ch]] += sums[ch]


def rows_to_lanes(row_sum):
    row = lax.broadcasted_iota(jnp.int32, (LANES, LANES), 0)
    lane = lax.broadcasted_iota(jnp.int32, (LANES, LANES), 1)
    out = []
    for u in range(8):
        total = jnp.sum(row_sum[u * LANES : (u + 1) * LANES, :], axis=1, keepdims=True)
        out.append(jnp.sum(jnp.where(row == lane, total, 0.0), axis=0, keepdims=True))
    return out


def cols_to_lanes(col_sum, at):
    return [
        jnp.sum(col_sum[:, at + u * LANES : at + (u + 1) * LANES], axis=0, keepdims=True)
        for u in range(8)
    ]


def near_kernel(s_ref, keep_ref, own_ref, other_ref, row_ref, col_ref, out_ref, inverse_ref,
                left_meta, right_meta, keep, prod_a, prod_b, row_sum, col_sum):
    core = s_ref[6]
    own_offset = s_ref[7]
    other_offset = s_ref[8]
    terms = square_sums(own_ref[...])
    left_meta[0] = inverse_column(terms)
    right_meta[0, :, 0:1024] = inverse_row(terms)
    right_meta[0, :, 1024:2048] = inverse_row(square_sums(other_ref[...]))
    inverse_ref[...] = right_meta[0]
    load_column_meta(col_ref, 0, 0, left_meta)
    load_row_meta(0, row_ref, 0, 0, keep_ref, own_offset, own_offset, right_meta, keep)
    load_row_meta(1024, row_ref, 1, 0, keep_ref, own_offset, other_offset, right_meta, keep)
    row_sum[...] = jnp.zeros_like(row_sum)
    col_sum[...] = jnp.zeros_like(col_sum)

    @pl.loop(0, 4)
    def _(i):
        at = pl.multiple_of(i * 256, 256)
        half = pl.multiple_of(((i >> 1) ^ core) * 512, 512)
        product(own_ref, at, own_ref, 0, prod_a)
        product(own_ref, at, own_ref, 512, prod_b)
        weigh(prod_a, at, left_meta, 0, right_meta, keep, row_sum, col_sum, True)
        product(own_ref, at, other_ref, half, prod_a)
        weigh(prod_b, at, left_meta, 512, right_meta, keep, row_sum, col_sum, True)
        weigh(prod_a, at, left_meta, 1024 + half, right_meta, keep, row_sum, col_sum, False)

    own = rows_to_lanes(row_sum)
    other = cols_to_lanes(col_sum, 1024)
    for u in range(8):
        out_ref[0, u : u + 1, :] = own[u]
        out_ref[1, u : u + 1, :] = other[u]


def far_kernel(s_ref, keep_ref, own_hbm, other_hbm, left_hbm, right_ref, row_ref, col_ref, near_ref,
               inverse_ref, stay_ref, move_ref, block_ref, left_meta, right_meta, keep, prod_a,
               prod_b, row_sum, col_sum, sems):
    own_offset = s_ref[7]
    other_offset = s_ref[8]
    cross = s_ref[9]
    left_offset = s_ref[10]
    copies = [
        pltpu.make_async_copy(source, block_ref.at[pl.ds(i * 1024, 1024), :], sems.at[i])
        for i, source in enumerate((own_hbm, other_hbm, left_hbm))
    ]
    for copy in copies:
        copy.start()
    left_meta[0] = inverse_column(square_sums(right_ref[...]))
    load_column_meta(col_ref, 0, 1, left_meta)
    load_row_meta(0, row_ref, 0, 0, keep_ref, own_offset, own_offset, right_meta, keep)
    load_row_meta(1024, row_ref, 1, 0, keep_ref, own_offset, other_offset, right_meta, keep)
    load_row_meta(2048, row_ref, cross, 3, keep_ref, own_offset, left_offset, right_meta, keep)
    right_meta[0, :, 0:2048] = inverse_ref[...]
    row_sum[...] = jnp.zeros_like(row_sum)
    col_sum[...] = jnp.zeros_like(col_sum)
    for copy in copies:
        copy.wait()
    right_meta[0, :, 2048:3072] = inverse_row(square_sums(block_ref[2048:3072, :]))
    rows, cols = prod_a.shape
    steps = 1024 // rows
    total = steps * (3072 // cols)
    product(right_ref, 0, block_ref, 0, prod_a)

    def place_of(t):
        return pl.multiple_of((t % steps) * rows, rows), pl.multiple_of((t // steps) * cols, cols)

    @pl.loop(0, total // 2)
    def _(i):
        left_a, right_a = place_of(i * 2)
        left_b, right_b = place_of(i * 2 + 1)
        left_c, right_c = place_of(jnp.minimum(i * 2 + 2, total - 1))
        product(right_ref, left_b, block_ref, right_b, prod_b)
        weigh(prod_a, left_a, left_meta, right_a, right_meta, keep, row_sum, col_sum, False)
        product(right_ref, left_c, block_ref, right_c, prod_a)
        weigh(prod_b, left_b, left_meta, right_b, right_meta, keep, row_sum, col_sum, False)

    right = rows_to_lanes(row_sum)
    own = cols_to_lanes(col_sum, 0)
    other = cols_to_lanes(col_sum, 1024)
    left = cols_to_lanes(col_sum, 2048)
    for u in range(8):
        row = slice(u, u + 1)
        stay_ref[0, row, :] = own[u] + near_ref[0, row, :]
        stay_ref[1, row, :] = right[u]
        stay_ref[2, row, :] = jnp.where(cross == 0, left[u], 0.0)
        move_ref[0, row, :] = other[u] + near_ref[1, row, :]
        move_ref[1, row, :] = jnp.where(cross == 0, 0.0, left[u])


FAR_TILE = (1024, 256)


def pair_scratch(columns, tile):
    return [
        pltpu.VMEM((3, 1024, LANES), jnp.float32),
        pltpu.VMEM((2, 8, columns), jnp.float32),
        pltpu.VMEM((2, 8, columns), jnp.float32),
        pltpu.VMEM(tile, jnp.float32),
        pltpu.VMEM(tile, jnp.float32),
        pltpu.VMEM((1024, LANES), jnp.float32),
        pltpu.VMEM((8, columns), jnp.float32),
    ]


def near_pairs(scalars, keep, own, other, rows, cols):
    return pl.pallas_call(
        near_kernel,
        out_shape=(
            jax.ShapeDtypeStruct((2, 8, LANES), jnp.float32),
            jax.ShapeDtypeStruct((8, 2048), jnp.float32),
        ),
        in_specs=[smem(), smem(), vmem(), vmem(), vmem(), vmem()],
        out_specs=(vmem(), vmem()),
        scratch_shapes=pair_scratch(2048, (256, 512)),
        compiler_params=pltpu.CompilerParams(vmem_limit_bytes=VMEM),
        cost_estimate=pl.CostEstimate(flops=2 * 10**9, bytes_accessed=10**7, transcendentals=0),
        name="near_pairs",
    )(scalars, keep, own, other, rows, cols)


def far_pairs(scalars, keep, own, other, left, right, rows, cols, near):
    return pl.pallas_call(
        far_kernel,
        out_shape=(
            jax.ShapeDtypeStruct((3, 8, LANES), jnp.float32),
            jax.ShapeDtypeStruct((2, 8, LANES), jnp.float32),
        ),
        in_specs=[smem(), smem(), hbm(), hbm(), hbm()] + [vmem()] * 5,
        out_specs=(vmem(), vmem()),
        scratch_shapes=[pltpu.VMEM((3072, 256), jnp.bfloat16)]
        + pair_scratch(3072, FAR_TILE)
        + [pltpu.SemaphoreType.DMA((3,))],
        compiler_params=pltpu.CompilerParams(vmem_limit_bytes=VMEM),
        cost_estimate=pl.CostEstimate(flops=4 * 10**9, bytes_accessed=10**7, transcendentals=0),
        name="far_pairs",
    )(scalars, keep, own, other, left, right, rows, cols, *near)


def rank_kernel(place_ref, *refs):
    pieces, out_ref = refs[:-1], refs[-1]
    place_at = place_ref[...]
    lane = place_at & 127
    which = place_at >> 7
    total = jnp.zeros((32, LANES), jnp.float32)
    for s in range(4):
        block = pieces[s][0] + pieces[(s + 1) % 4][1] + pieces[(s + 3) % 4][2]
        for u in range(8):
            row = jnp.broadcast_to(block[u : u + 1, :], (32, LANES))
            value = jnp.take_along_axis(row, lane, axis=1)
            total = jnp.where(which == s * 8 + u, value, total)
    out_ref[...] = total * (1.0 / TILE)


def to_rank_order(place_at, pieces):
    return pl.pallas_call(
        rank_kernel,
        out_shape=jax.ShapeDtypeStruct((32, LANES), jnp.float32),
        in_specs=[vmem()] * 5,
        out_specs=vmem(),
        compiler_params=pltpu.CompilerParams(vmem_limit_bytes=VMEM),
        name="to_rank_order",
    )(place_at, *pieces)


def on_device(points, rank_source, thresholds, kept_tiles):
    bands = lax.axis_size("band")
    reps = lax.axis_size("rep")
    device = lax.axis_index("band").astype(jnp.int32)
    rep = lax.axis_index("rep").astype(jnp.int32)
    core = device & 1
    host = device ^ 8
    own_band = jnp.where(core == 0, host, bands - host)
    other_band = bands - 1 - own_band
    own_offset = jnp.where(own_band < bands // 2, 0, 2)
    other_offset = 2 - own_offset
    cross = (rep >= 2).astype(jnp.int32)
    left_offset = jnp.where(cross == 1, other_offset, own_offset)
    scalars = jnp.stack([
        device, rep * 16, rep, own_band, other_band, device, core,
        own_offset, other_offset, cross, left_offset,
    ]).astype(jnp.int32)
    codes = lax.dynamic_index_in_dim(kept_tiles, jnp.minimum(own_band, other_band), 0, keepdims=False)
    ids = jnp.arange(16, dtype=jnp.int32)
    a, c = ids // 4, ids % 4
    wanted = jnp.minimum(a, c) * 4 + jnp.maximum(a, c)
    keep = jnp.where(jnp.any(codes[:, None] == wanted[None, :], axis=0), 1.0, -1e30).astype(jnp.float32)

    rank2d = rank_source.reshape(2048, LANES)
    thr2d = thresholds.reshape(2048, LANES)

    def joint(move):
        return [
            (d * reps + r, e * reps + q)
            for d in range(bands)
            for r in range(reps)
            for e, q in (move(d, r),)
        ]

    def shift(value, move):
        return lax.ppermute(value, ("band", "rep"), joint(move))

    payload = send_rows(rank2d, points)
    own = lax.all_to_all(
        payload.reshape(bands, 16, 256), "band", split_axis=0, concat_axis=0, tiled=True
    ).reshape(1024, 256)
    own, rows, cols, place_at = lax.optimization_barrier((own, *place(scalars, rank2d, thr2d)))

    def to_right(d, r):
        q = (r + 1) % reps
        return (d if q < 2 else d ^ 1), q

    other = shift(own, lambda d, r: (d ^ 1, r))
    right = shift(own, lambda d, r: (d, (r - 1) % reps))
    left = shift(own, to_right)

    near = near_pairs(scalars, keep, own, other, rows, cols)
    stay, move = far_pairs(scalars, keep, own, other, left, right, rows, cols, near)
    moved = shift(move, lambda d, r: (d ^ 1, r))
    sums = stay + jnp.stack([moved[0], jnp.zeros_like(moved[0]), moved[1]])
    home = shift(sums, lambda d, r: (block_band(d), r))
    pieces = [home] + [
        shift(home, lambda d, r, s=s: (d, (r + s) % reps)) for s in range(1, reps)
    ]
    return to_rank_order(place_at, pieces).reshape(points.shape[0])


def solution(mesh):
    in_specs = (P("band", None), P(), P(), P())
    out_specs = P("band")
    return jax.shard_map(
        on_device, mesh=mesh, in_specs=in_specs, out_specs=out_specs, check_vma=False
    )
```

```python
import jax
import jax.numpy as jnp
from jax import lax
from jax.experimental import pallas as pl
from jax.experimental.pallas import tpu as pltpu
from jax.sharding import PartitionSpec as P

TILE = 2048
LANES = 128
SEND_VMEM = 60 * 1024 * 1024
VMEM = 28 * 1024 * 1024
NT = (((1,), (1,)), ((), ()))


def prefix_matrix():
    row = lax.broadcasted_iota(jnp.int32, (LANES, 2 * LANES), 0)
    col = lax.broadcasted_iota(jnp.int32, (LANES, 2 * LANES), 1)
    return jnp.where((row <= col) | (col >= LANES), 1.0, 0.0).astype(jnp.bfloat16)


def block_band(device):
    host = device ^ 8
    return host if host % 2 == 0 else 64 - host


def smem():
    return pl.BlockSpec(memory_space=pltpu.SMEM)


def vmem():
    return pl.BlockSpec(memory_space=pltpu.VMEM)


def hbm():
    return pl.BlockSpec(memory_space=pltpu.HBM)


def send_kernel(rank_hbm, points_hbm, out_ref, rank_ref, points_ref, acc_ref, row_ref,
                hot_ref, rank_sem, points_sem):
    def fetch_rank(g):
        rows = pl.ds(g * 256, 256)
        return pltpu.make_async_copy(rank_hbm.at[rows, :], rank_ref.at[rows, :], rank_sem.at[g])

    for g in range(8):
        fetch_rank(g).start()
    fetch_points = pltpu.make_async_copy(points_hbm, points_ref, points_sem)
    fetch_points.start()
    shard = lax.axis_index("band")
    prefix = prefix_matrix()
    base = (lax.axis_index("rep") * 16 + 1).astype(jnp.float32)
    ones = jnp.ones((LANES, LANES), jnp.bfloat16)
    for g in range(8):
        fetch_rank(g).wait()
        source = [rank_ref[pl.ds(g * 256 + j, 8, stride=32), :] for j in range(32)]
        mine = [(source[j] >> 12) == shard for j in range(32)]
        marks = jnp.concatenate([jnp.where(m, 1.0, 0.0) for m in mine], axis=0).astype(jnp.bfloat16)
        counts = jnp.dot(marks, prefix, preferred_element_type=jnp.float32)
        carry = jnp.zeros((8, LANES), jnp.float32) - base
        accs = [jnp.zeros((8, LANES), jnp.int32) for _ in range(16)]
        for j in range(32):
            pos = jnp.where(mine[j], carry + counts[j * 8 : j * 8 + 8, :LANES], -1.0)
            loc = source[j] & 4095
            carry = carry + counts[j * 8 : j * 8 + 8, LANES:]
            for i in range(16):
                accs[i] = jnp.where(pos == float(i), loc, accs[i])
        for i in range(16):
            acc_ref[g * 128 + i * 8 : g * 128 + i * 8 + 8, :] = accs[i]

    acc = acc_ref[...]
    high = (acc >> 6).astype(jnp.float32).astype(jnp.bfloat16)
    low = (acc & 63).astype(jnp.float32).astype(jnp.bfloat16)
    row_ref[...] = 64.0 * jnp.dot(high, ones, preferred_element_type=jnp.float32) + jnp.dot(
        low, ones, preferred_element_type=jnp.float32
    )
    fetch_points.wait()
    lane = lax.broadcasted_iota(jnp.int32, (1024, LANES), 1)
    one = jnp.ones((1024, LANES), jnp.bfloat16)
    zero = jnp.zeros((1024, LANES), jnp.bfloat16)
    parts = []
    for i in range(64):
        band = block_band(i)
        parts.append(row_ref[pl.ds((band // 8) * 128 + band % 8, 16, stride=8), :])
    local = jnp.concatenate(parts, axis=0).astype(jnp.int32)
    chunk = (local >> 7).astype(jnp.float32).astype(jnp.bfloat16)
    hot = jnp.where((local & 127) == lane, 1.0, 0.0).astype(jnp.bfloat16)
    for ch in range(32):
        hot_ref[:, ch * 128 : (ch + 1) * 128] = jnp.where(chunk == one * ch, hot, zero)
    out_ref[...] = jnp.dot(
        hot_ref[...], points_ref[...], preferred_element_type=jnp.float32
    ).astype(jnp.bfloat16)


def send_rows(rank2d, points):
    return pl.pallas_call(
        send_kernel,
        out_shape=jax.ShapeDtypeStruct((1024, 256), jnp.bfloat16),
        in_specs=[hbm(), hbm()],
        out_specs=vmem(),
        scratch_shapes=[
            pltpu.VMEM((2048, LANES), jnp.int32),
            pltpu.VMEM((4096, 256), jnp.bfloat16),
            pltpu.VMEM((1024, LANES), jnp.int32),
            pltpu.VMEM((1024, LANES), jnp.float32),
            pltpu.VMEM((1024, 4096), jnp.bfloat16),
            pltpu.SemaphoreType.DMA((8,)),
            pltpu.SemaphoreType.DMA,
        ],
        compiler_params=pltpu.CompilerParams(vmem_limit_bytes=SEND_VMEM),
        name="send_rows",
    )(rank2d, points)


def place_kernel(s_ref, rank_hbm, thr_hbm, row_ref, col_ref, place_ref, u_ref, v_ref, rank_ref, thr_ref, sems):
    copies = []
    for x in range(3):
        start = pl.multiple_of(s_ref[3 + x] * 32, 32)
        copies.append((
            pltpu.make_async_copy(rank_hbm.at[pl.ds(start, 32), :], rank_ref.at[x], sems.at[x, 0]),
            pltpu.make_async_copy(thr_hbm.at[pl.ds(start, 32), :], thr_ref.at[x], sems.at[x, 1]),
        ))
        for copy in copies[x]:
            copy.start()
    rep = s_ref[2]
    prefix = prefix_matrix()
    shard_iota = lax.broadcasted_iota(jnp.int32, (64, LANES), 0)
    u_iota = lax.broadcasted_iota(jnp.int32, (32, LANES), 0)
    v_iota = lax.broadcasted_iota(jnp.int32, (LANES, LANES), 0)
    for x in range(3):
        for copy in copies[x]:
            copy.wait()
        carry = jnp.zeros((64, LANES), jnp.float32)
        source = rank_ref[x] >> 12
        thr = thr_ref[x]
        for j in range(32):
            shard = source[j : j + 1, :]
            hot = shard == shard_iota
            counts = jnp.dot(
                jnp.where(hot, 1.0, 0.0).astype(jnp.bfloat16), prefix, preferred_element_type=jnp.float32
            )
            slot = jnp.sum(jnp.where(hot, carry + counts[:, :LANES], 0.0), axis=0, keepdims=True)
            slot = slot.astype(jnp.int32) - 1
            carry = carry + counts[:, LANES:]
            quarter = slot >> 4
            v = (shard & 7) * 16 + (slot & 15)
            if x == 2:
                place_ref[j : j + 1, :] = (((rep - quarter) & 3) * 8 + (shard >> 3)) * 128 + v
            else:
                u = ((quarter - rep) & 3) * 8 + (shard >> 3)
                u_hot = u == u_iota
                t = thr[j : j + 1, :]
                lanes = slice(j * LANES, (j + 1) * LANES)
                u_ref[0:32, lanes] = jnp.where(u_hot, (t >> 4).astype(jnp.float32), 0.0).astype(jnp.bfloat16)
                u_ref[32:64, lanes] = jnp.where(u_hot, (t & 15).astype(jnp.float32), 0.0).astype(jnp.bfloat16)
                u_ref[64:96, lanes] = jnp.where(u_hot, float(j >= 16), 0.0).astype(jnp.bfloat16)
                v_ref[:, lanes] = jnp.where(v == v_iota, 1.0, 0.0).astype(jnp.bfloat16)
        if x < 2:
            us = u_ref[...]
            vs = v_ref[...]
            rows = lax.dot_general(us, vs, NT, preferred_element_type=jnp.float32)
            cols = lax.dot_general(vs, us, NT, preferred_element_type=jnp.float32)
            row_ref[x, 0:32, :] = 1024.0 / (rows[0:32] * 16.0 + rows[32:64])
            row_ref[x, 32:64, :] = rows[64:96]
            col_ref[x, :, 0:32] = 1024.0 / (cols[:, 0:32] * 16.0 + cols[:, 32:64])
            col_ref[x, :, 32:64] = cols[:, 64:96]


def place(scalars, rank2d, thr2d):
    return pl.pallas_call(
        place_kernel,
        out_shape=(
            jax.ShapeDtypeStruct((2, 64, LANES), jnp.float32),
            jax.ShapeDtypeStruct((2, LANES, 64), jnp.float32),
            jax.ShapeDtypeStruct((32, LANES), jnp.int32),
        ),
        in_specs=[smem(), hbm(), hbm()],
        out_specs=(vmem(),) * 3,
        scratch_shapes=[
            pltpu.VMEM((96, 4096), jnp.bfloat16),
            pltpu.VMEM((LANES, 4096), jnp.bfloat16),
            pltpu.VMEM((3, 32, LANES), jnp.int32),
            pltpu.VMEM((3, 32, LANES), jnp.int32),
            pltpu.SemaphoreType.DMA((3, 2)),
        ],
        compiler_params=pltpu.CompilerParams(vmem_limit_bytes=VMEM),
        cost_estimate=pl.CostEstimate(flops=2 * 10**9, bytes_accessed=10**7, transcendentals=0),
        name="place",
    )(scalars, rank2d, thr2d)


def square_sums(block):
    values = block.astype(jnp.float32)
    square = values * values
    total = square[:, :LANES] + square[:, LANES:]
    high = total.astype(jnp.bfloat16)
    rest = total - high.astype(jnp.float32)
    middle = rest.astype(jnp.bfloat16)
    low = (rest - middle.astype(jnp.float32)).astype(jnp.bfloat16)
    return high, middle, low


def inverse_column(terms):
    ones = jnp.ones((LANES, LANES), jnp.bfloat16)
    high, middle, low = (jnp.dot(t, ones, preferred_element_type=jnp.float32) for t in terms)
    return lax.rsqrt(high + (middle + low) + 1e-06)


def inverse_row(terms):
    ones = jnp.ones((8, LANES), jnp.bfloat16)
    high, middle, low = (
        lax.dot_general(ones, t, NT, preferred_element_type=jnp.float32) for t in terms
    )
    return lax.rsqrt(high + (middle + low) + 1e-06)


def load_column_meta(col_ref, band, quarter, meta):
    for u in range(8):
        rows = slice(u * LANES, (u + 1) * LANES)
        i = quarter * 8 + u
        meta[1, rows, :] = jnp.broadcast_to(col_ref[band, :, i : i + 1], (LANES, LANES))
        meta[2, rows, :] = jnp.broadcast_to(col_ref[band, :, 32 + i : 33 + i], (LANES, LANES))


def load_row_meta(at, row_ref, band, quarter, keep_ref, row_offset, col_offset, meta, keep):
    for u in range(8):
        lanes = slice(at + u * LANES, at + (u + 1) * LANES)
        i = quarter * 8 + u
        meta[1, :, lanes] = jnp.broadcast_to(row_ref[band, i : i + 1, :], (8, LANES))
        upper = jnp.broadcast_to(row_ref[band, 32 + i : 33 + i, :], (8, LANES)) > 0.5
        for t in range(2):
            code = (row_offset + t) * 4 + col_offset
            keep[t, :, lanes] = jnp.where(upper, keep_ref[code + 1], keep_ref[code])


def product(left_ref, left_at, right_ref, right_at, prod_ref):
    rows, cols = prod_ref.shape
    prod_ref[...] = lax.dot_general(
        left_ref[pl.ds(left_at, rows), :], right_ref[pl.ds(right_at, cols), :], NT,
        preferred_element_type=jnp.float32,
    )


def weigh(prod_ref, left_at, left_meta, right_at, right_meta, keep, row_sum, col_sum, diagonal):
    chunks = prod_ref.shape[1] // LANES
    sums = [jnp.zeros((8, LANES), jnp.float32) for _ in range(chunks)]
    lanes = [pl.ds(pl.multiple_of(right_at + ch * LANES, LANES), LANES) for ch in range(chunks)]
    for i in range(prod_ref.shape[0] // 32):
        rows = pl.ds(pl.multiple_of(left_at + i * 32, 32), 32)
        inv_i = left_meta[0, rows, :].reshape(4, 8, LANES)
        rho_i = left_meta[1, rows, :].reshape(4, 8, LANES)
        upper = left_meta[2, rows, :].reshape(4, 8, LANES) > 0.5
        total = row_sum[rows, :].reshape(4, 8, LANES)
        for ch in range(chunks):
            inv_j = right_meta[0, :, lanes[ch]][None]
            rho_j = right_meta[1, :, lanes[ch]][None]
            kept = jnp.where(upper, keep[1, :, lanes[ch]][None], keep[0, :, lanes[ch]][None])
            p = prod_ref[i * 32 : i * 32 + 32, ch * LANES : (ch + 1) * LANES].reshape(4, 8, LANES)
            near = (p * inv_i) * inv_j - 1.0
            w = jnp.maximum(near * jnp.maximum(rho_i, rho_j) + kept, 0.0)
            if diagonal:
                row_ids = lax.broadcasted_iota(jnp.int32, w.shape, 0) * 8 + lax.broadcasted_iota(jnp.int32, w.shape, 1)
                col_ids = lax.broadcasted_iota(jnp.int32, w.shape, 2)
                w = jnp.where(row_ids + (left_at + i * 32) == col_ids + (right_at + ch * LANES), 0.0, w)
            total = total + w
            if not diagonal:
                sums[ch] = sums[ch] + ((w[0] + w[1]) + (w[2] + w[3]))
        row_sum[rows, :] = total.reshape(32, LANES)
    if not diagonal:
        for ch in range(chunks):
            col_sum[:, lanes[ch]] += sums[ch]


def rows_to_lanes(row_sum):
    row = lax.broadcasted_iota(jnp.int32, (LANES, LANES), 0)
    lane = lax.broadcasted_iota(jnp.int32, (LANES, LANES), 1)
    out = []
    for u in range(8):
        total = jnp.sum(row_sum[u * LANES : (u + 1) * LANES, :], axis=1, keepdims=True)
        out.append(jnp.sum(jnp.where(row == lane, total, 0.0), axis=0, keepdims=True))
    return out


def cols_to_lanes(col_sum, at):
    return [
        jnp.sum(col_sum[:, at + u * LANES : at + (u + 1) * LANES], axis=0, keepdims=True)
        for u in range(8)
    ]


def near_kernel(s_ref, keep_ref, own_ref, other_ref, row_ref, col_ref, out_ref, inverse_ref,
                left_meta, right_meta, keep, prod_a, prod_b, row_sum, col_sum):
    core = s_ref[6]
    own_offset = s_ref[7]
    other_offset = s_ref[8]
    terms = square_sums(own_ref[...])
    left_meta[0] = inverse_column(terms)
    right_meta[0, :, 0:1024] = inverse_row(terms)
    right_meta[0, :, 1024:2048] = inverse_row(square_sums(other_ref[...]))
    inverse_ref[...] = right_meta[0]
    load_column_meta(col_ref, 0, 0, left_meta)
    load_row_meta(0, row_ref, 0, 0, keep_ref, own_offset, own_offset, right_meta, keep)
    load_row_meta(1024, row_ref, 1, 0, keep_ref, own_offset, other_offset, right_meta, keep)
    row_sum[...] = jnp.zeros_like(row_sum)
    col_sum[...] = jnp.zeros_like(col_sum)

    @pl.loop(0, 4)
    def _(i):
        at = pl.multiple_of(i * 256, 256)
        half = pl.multiple_of(((i >> 1) ^ core) * 512, 512)
        product(own_ref, at, own_ref, 0, prod_a)
        product(own_ref, at, own_ref, 512, prod_b)
        weigh(prod_a, at, left_meta, 0, right_meta, keep, row_sum, col_sum, True)
        product(own_ref, at, other_ref, half, prod_a)
        weigh(prod_b, at, left_meta, 512, right_meta, keep, row_sum, col_sum, True)
        weigh(prod_a, at, left_meta, 1024 + half, right_meta, keep, row_sum, col_sum, False)

    own = rows_to_lanes(row_sum)
    other = cols_to_lanes(col_sum, 1024)
    for u in range(8):
        out_ref[0, u : u + 1, :] = own[u]
        out_ref[1, u : u + 1, :] = other[u]


def right_pairs(s_ref, keep_ref, sources, columns, right_ref, row_ref, col_ref, inverse_ref, block_ref,
                left_meta, right_meta, keep, prod_a, prod_b, row_sum, col_sum, sems):
    own_offset = s_ref[7]
    copies = [
        pltpu.make_async_copy(source, block_ref.at[pl.ds(i * 1024, 1024), :], sems.at[i])
        for i, source in enumerate(sources)
    ]
    for copy in copies:
        copy.start()
    left_meta[0] = inverse_column(square_sums(right_ref[...]))
    load_column_meta(col_ref, 0, 1, left_meta)
    for i, (band, quarter, offset, known) in enumerate(columns):
        load_row_meta(i * 1024, row_ref, band, quarter, keep_ref, own_offset, offset, right_meta, keep)
        if known is not None:
            right_meta[0, :, i * 1024 : (i + 1) * 1024] = inverse_ref[:, known * 1024 : (known + 1) * 1024]
    row_sum[...] = jnp.zeros_like(row_sum)
    col_sum[...] = jnp.zeros_like(col_sum)
    for copy in copies:
        copy.wait()
    for i, column in enumerate(columns):
        if column[3] is None:
            at = slice(i * 1024, (i + 1) * 1024)
            right_meta[0, :, at] = inverse_row(square_sums(block_ref[at, :]))
    cols = prod_a.shape[1]
    total = len(columns) * 1024 // cols
    product(right_ref, 0, block_ref, 0, prod_a)

    @pl.loop(0, total // 2)
    def _(i):
        at_a = pl.multiple_of(i * 2 * cols, cols)
        at_b = pl.multiple_of((i * 2 + 1) * cols, cols)
        at_c = pl.multiple_of(jnp.minimum(i * 2 + 2, total - 1) * cols, cols)
        product(right_ref, 0, block_ref, at_b, prod_b)
        weigh(prod_a, 0, left_meta, at_a, right_meta, keep, row_sum, col_sum, False)
        product(right_ref, 0, block_ref, at_c, prod_a)
        weigh(prod_b, 0, left_meta, at_b, right_meta, keep, row_sum, col_sum, False)


def guest_kernel(s_ref, keep_ref, other_hbm, left_hbm, right_ref, row_ref, col_ref, near_ref,
                 inverse_ref, stay_ref, move_ref, *scratch):
    cross = s_ref[9]
    right_pairs(
        s_ref, keep_ref, (other_hbm, left_hbm), ((1, 0, s_ref[8], 1), (cross, 3, s_ref[10], None)),
        right_ref, row_ref, col_ref, inverse_ref, *scratch,
    )
    row_sum, col_sum = scratch[6:8]
    right = rows_to_lanes(row_sum)
    other = cols_to_lanes(col_sum, 0)
    left = cols_to_lanes(col_sum, 1024)
    for u in range(8):
        row = slice(u, u + 1)
        stay_ref[0, row, :] = right[u]
        stay_ref[1, row, :] = jnp.where(cross == 0, left[u], 0.0)
        move_ref[0, row, :] = other[u] + near_ref[1, row, :]
        move_ref[1, row, :] = jnp.where(cross == 0, 0.0, left[u])


def own_kernel(s_ref, keep_ref, own_hbm, right_ref, row_ref, col_ref, near_ref, inverse_ref,
               guest_ref, stay_ref, *scratch):
    right_pairs(
        s_ref, keep_ref, (own_hbm,), ((0, 0, s_ref[7], 0),),
        right_ref, row_ref, col_ref, inverse_ref, *scratch,
    )
    row_sum, col_sum = scratch[6:8]
    right = rows_to_lanes(row_sum)
    own = cols_to_lanes(col_sum, 0)
    for u in range(8):
        row = slice(u, u + 1)
        stay_ref[0, row, :] = own[u] + near_ref[0, row, :]
        stay_ref[1, row, :] = right[u] + guest_ref[0, row, :]
        stay_ref[2, row, :] = guest_ref[1, row, :]


FAR_TILE = (1024, 256)


def pair_scratch(columns, tile):
    return [
        pltpu.VMEM((3, 1024, LANES), jnp.float32),
        pltpu.VMEM((2, 8, columns), jnp.float32),
        pltpu.VMEM((2, 8, columns), jnp.float32),
        pltpu.VMEM(tile, jnp.float32),
        pltpu.VMEM(tile, jnp.float32),
        pltpu.VMEM((1024, LANES), jnp.float32),
        pltpu.VMEM((8, columns), jnp.float32),
    ]


def near_pairs(scalars, keep, own, other, rows, cols):
    return pl.pallas_call(
        near_kernel,
        out_shape=(
            jax.ShapeDtypeStruct((2, 8, LANES), jnp.float32),
            jax.ShapeDtypeStruct((8, 2048), jnp.float32),
        ),
        in_specs=[smem(), smem(), vmem(), vmem(), vmem(), vmem()],
        out_specs=(vmem(), vmem()),
        scratch_shapes=pair_scratch(2048, (256, 512)),
        compiler_params=pltpu.CompilerParams(vmem_limit_bytes=VMEM),
        cost_estimate=pl.CostEstimate(flops=2 * 10**9, bytes_accessed=10**7, transcendentals=0),
        name="near_pairs",
    )(scalars, keep, own, other, rows, cols)


def far_scratch(blocks):
    return (
        [pltpu.VMEM((blocks * 1024, 256), jnp.bfloat16)]
        + pair_scratch(blocks * 1024, FAR_TILE)
        + [pltpu.SemaphoreType.DMA((blocks,))]
    )


def guest_pairs(scalars, keep, other, left, right, rows, cols, near):
    return pl.pallas_call(
        guest_kernel,
        out_shape=(
            jax.ShapeDtypeStruct((2, 8, LANES), jnp.float32),
            jax.ShapeDtypeStruct((2, 8, LANES), jnp.float32),
        ),
        in_specs=[smem(), smem(), hbm(), hbm()] + [vmem()] * 5,
        out_specs=(vmem(), vmem()),
        scratch_shapes=far_scratch(2),
        compiler_params=pltpu.CompilerParams(vmem_limit_bytes=VMEM),
        cost_estimate=pl.CostEstimate(flops=3 * 10**9, bytes_accessed=10**7, transcendentals=0),
        name="guest_pairs",
    )(scalars, keep, other, left, right, rows, cols, *near)


def own_pairs(scalars, keep, own, right, rows, cols, near, guests):
    return pl.pallas_call(
        own_kernel,
        out_shape=jax.ShapeDtypeStruct((3, 8, LANES), jnp.float32),
        in_specs=[smem(), smem(), hbm()] + [vmem()] * 6,
        out_specs=vmem(),
        scratch_shapes=far_scratch(1),
        compiler_params=pltpu.CompilerParams(vmem_limit_bytes=VMEM),
        cost_estimate=pl.CostEstimate(flops=2 * 10**9, bytes_accessed=10**7, transcendentals=0),
        name="own_pairs",
    )(scalars, keep, own, right, rows, cols, *near, guests)


def rank_kernel(place_ref, *refs):
    pieces, out_ref = refs[:-1], refs[-1]
    place_at = place_ref[...]
    lane = place_at & 127
    which = place_at >> 7
    total = jnp.zeros((32, LANES), jnp.float32)
    for s in range(4):
        block = pieces[s][0] + pieces[(s + 1) % 4][1] + pieces[(s + 3) % 4][2]
        for u in range(8):
            row = jnp.broadcast_to(block[u : u + 1, :], (32, LANES))
            value = jnp.take_along_axis(row, lane, axis=1)
            total = jnp.where(which == s * 8 + u, value, total)
    out_ref[...] = total * (1.0 / TILE)


def to_rank_order(place_at, pieces):
    return pl.pallas_call(
        rank_kernel,
        out_shape=jax.ShapeDtypeStruct((32, LANES), jnp.float32),
        in_specs=[vmem()] * 5,
        out_specs=vmem(),
        compiler_params=pltpu.CompilerParams(vmem_limit_bytes=VMEM),
        name="to_rank_order",
    )(place_at, *pieces)


def on_device(points, rank_source, thresholds, kept_tiles):
    bands = lax.axis_size("band")
    reps = lax.axis_size("rep")
    device = lax.axis_index("band").astype(jnp.int32)
    rep = lax.axis_index("rep").astype(jnp.int32)
    core = device & 1
    host = device ^ 8
    own_band = jnp.where(core == 0, host, bands - host)
    other_band = bands - 1 - own_band
    own_offset = jnp.where(own_band < bands // 2, 0, 2)
    other_offset = 2 - own_offset
    cross = (rep >= 2).astype(jnp.int32)
    left_offset = jnp.where(cross == 1, other_offset, own_offset)
    scalars = jnp.stack([
        device, rep * 16, rep, own_band, other_band, device, core,
        own_offset, other_offset, cross, left_offset,
    ]).astype(jnp.int32)
    codes = lax.dynamic_index_in_dim(kept_tiles, jnp.minimum(own_band, other_band), 0, keepdims=False)
    ids = jnp.arange(16, dtype=jnp.int32)
    a, c = ids // 4, ids % 4
    wanted = jnp.minimum(a, c) * 4 + jnp.maximum(a, c)
    keep = jnp.where(jnp.any(codes[:, None] == wanted[None, :], axis=0), 1.0, -1e30).astype(jnp.float32)

    rank2d = rank_source.reshape(2048, LANES)
    thr2d = thresholds.reshape(2048, LANES)

    def joint(move):
        return [
            (d * reps + r, e * reps + q)
            for d in range(bands)
            for r in range(reps)
            for e, q in (move(d, r),)
        ]

    def shift(value, move):
        return lax.ppermute(value, ("band", "rep"), joint(move))

    payload = send_rows(rank2d, points)
    own = lax.all_to_all(
        payload.reshape(bands, 16, 256), "band", split_axis=0, concat_axis=0, tiled=True
    ).reshape(1024, 256)
    own, rows, cols, place_at = lax.optimization_barrier((own, *place(scalars, rank2d, thr2d)))

    def to_right(d, r):
        q = (r + 1) % reps
        return (d if q < 2 else d ^ 1), q

    other = shift(own, lambda d, r: (d ^ 1, r))
    right = shift(own, lambda d, r: (d, (r - 1) % reps))
    left = shift(own, to_right)

    near = near_pairs(scalars, keep, own, other, rows, cols)
    guests, move = guest_pairs(scalars, keep, other, left, right, rows, cols, near)
    moved = shift(move, lambda d, r: (d ^ 1, r))
    stay = own_pairs(scalars, keep, own, right, rows, cols, near, guests)
    sums = stay + jnp.stack([moved[0], jnp.zeros_like(moved[0]), moved[1]])
    home = shift(sums, lambda d, r: (block_band(d), r))
    pieces = [home] + [
        shift(home, lambda d, r, s=s: (d, (r + s) % reps)) for s in range(1, reps)
    ]
    return to_rank_order(place_at, pieces).reshape(points.shape[0])


def solution(mesh):
    in_specs = (P("band", None), P(), P(), P())
    out_specs = P("band")
    return jax.shard_map(
        on_device, mesh=mesh, in_specs=in_specs, out_specs=out_specs, check_vma=False
    )
```

```python
import jax
import jax.numpy as jnp
from jax import lax
from jax.experimental import pallas as pl
from jax.experimental.pallas import tpu as pltpu
from jax.sharding import PartitionSpec as P

TILE = 2048
LANES = 128
SEND_VMEM = 60 * 1024 * 1024
VMEM = 28 * 1024 * 1024
NT = (((1,), (1,)), ((), ()))


def prefix_matrix():
    row = lax.broadcasted_iota(jnp.int32, (LANES, 2 * LANES), 0)
    col = lax.broadcasted_iota(jnp.int32, (LANES, 2 * LANES), 1)
    return jnp.where((row <= col) | (col >= LANES), 1.0, 0.0).astype(jnp.bfloat16)


def block_band(device):
    host = device ^ 8
    return host if host % 2 == 0 else 64 - host


def smem():
    return pl.BlockSpec(memory_space=pltpu.SMEM)


def vmem():
    return pl.BlockSpec(memory_space=pltpu.VMEM)


def hbm():
    return pl.BlockSpec(memory_space=pltpu.HBM)


def send_kernel(rank_hbm, points_hbm, out_ref, rank_ref, points_ref, acc_ref, row_ref,
                hot_ref, rank_sem, points_sem):
    def fetch_rank(g):
        rows = pl.ds(g * 256, 256)
        return pltpu.make_async_copy(rank_hbm.at[rows, :], rank_ref.at[rows, :], rank_sem.at[g])

    for g in range(8):
        fetch_rank(g).start()
    fetch_points = pltpu.make_async_copy(points_hbm, points_ref, points_sem)
    fetch_points.start()
    shard = lax.axis_index("band")
    prefix = prefix_matrix()
    base = (lax.axis_index("rep") * 16 + 1).astype(jnp.float32)
    ones = jnp.ones((LANES, LANES), jnp.bfloat16)
    for g in range(8):
        fetch_rank(g).wait()
        source = [rank_ref[pl.ds(g * 256 + j, 8, stride=32), :] for j in range(32)]
        mine = [(source[j] >> 12) == shard for j in range(32)]
        marks = jnp.concatenate([jnp.where(m, 1.0, 0.0) for m in mine], axis=0).astype(jnp.bfloat16)
        counts = jnp.dot(marks, prefix, preferred_element_type=jnp.float32)
        carry = jnp.zeros((8, LANES), jnp.float32) - base
        accs = [jnp.zeros((8, LANES), jnp.int32) for _ in range(16)]
        for j in range(32):
            pos = jnp.where(mine[j], carry + counts[j * 8 : j * 8 + 8, :LANES], -1.0)
            loc = source[j] & 4095
            carry = carry + counts[j * 8 : j * 8 + 8, LANES:]
            for i in range(16):
                accs[i] = jnp.where(pos == float(i), loc, accs[i])
        for i in range(16):
            acc_ref[g * 128 + i * 8 : g * 128 + i * 8 + 8, :] = accs[i]

    acc = acc_ref[...]
    high = (acc >> 6).astype(jnp.float32).astype(jnp.bfloat16)
    low = (acc & 63).astype(jnp.float32).astype(jnp.bfloat16)
    row_ref[...] = 64.0 * jnp.dot(high, ones, preferred_element_type=jnp.float32) + jnp.dot(
        low, ones, preferred_element_type=jnp.float32
    )
    fetch_points.wait()
    lane = lax.broadcasted_iota(jnp.int32, (1024, LANES), 1)
    one = jnp.ones((1024, LANES), jnp.bfloat16)
    zero = jnp.zeros((1024, LANES), jnp.bfloat16)
    parts = []
    for i in range(64):
        band = block_band(i)
        parts.append(row_ref[pl.ds((band // 8) * 128 + band % 8, 16, stride=8), :])
    local = jnp.concatenate(parts, axis=0).astype(jnp.int32)
    chunk = (local >> 7).astype(jnp.float32).astype(jnp.bfloat16)
    hot = jnp.where((local & 127) == lane, 1.0, 0.0).astype(jnp.bfloat16)
    for ch in range(32):
        hot_ref[:, ch * 128 : (ch + 1) * 128] = jnp.where(chunk == one * ch, hot, zero)
    out_ref[...] = jnp.dot(
        hot_ref[...], points_ref[...], preferred_element_type=jnp.float32
    ).astype(jnp.bfloat16)


def send_rows(rank2d, points):
    return pl.pallas_call(
        send_kernel,
        out_shape=jax.ShapeDtypeStruct((1024, 256), jnp.bfloat16),
        in_specs=[hbm(), hbm()],
        out_specs=vmem(),
        scratch_shapes=[
            pltpu.VMEM((2048, LANES), jnp.int32),
            pltpu.VMEM((4096, 256), jnp.bfloat16),
            pltpu.VMEM((1024, LANES), jnp.int32),
            pltpu.VMEM((1024, LANES), jnp.float32),
            pltpu.VMEM((1024, 4096), jnp.bfloat16),
            pltpu.SemaphoreType.DMA((8,)),
            pltpu.SemaphoreType.DMA,
        ],
        compiler_params=pltpu.CompilerParams(vmem_limit_bytes=SEND_VMEM),
        name="send_rows",
    )(rank2d, points)


def place_kernel(s_ref, rank_hbm, thr_hbm, row_ref, col_ref, place_ref, u_ref, v_ref, rank_ref, thr_ref, sems):
    copies = []
    for x in range(3):
        start = pl.multiple_of(s_ref[3 + x] * 32, 32)
        copies.append((
            pltpu.make_async_copy(rank_hbm.at[pl.ds(start, 32), :], rank_ref.at[x], sems.at[x, 0]),
            pltpu.make_async_copy(thr_hbm.at[pl.ds(start, 32), :], thr_ref.at[x], sems.at[x, 1]),
        ))
        for copy in copies[x]:
            copy.start()
    rep = s_ref[2]
    core = s_ref[6]
    row_sums = []
    col_sums = []
    prefix = prefix_matrix()
    shard_iota = lax.broadcasted_iota(jnp.int32, (64, LANES), 0)
    u_iota = lax.broadcasted_iota(jnp.int32, (64, LANES), 0)
    v_iota = lax.broadcasted_iota(jnp.int32, (LANES, LANES), 0)
    for x in range(3):
        for copy in copies[x]:
            copy.wait()
        carry = jnp.zeros((64, LANES), jnp.float32)
        source = rank_ref[x] >> 12
        thr = thr_ref[x]
        for j in range(32):
            shard = source[j : j + 1, :]
            hot = shard == shard_iota
            counts = jnp.dot(
                jnp.where(hot, 1.0, 0.0).astype(jnp.bfloat16), prefix, preferred_element_type=jnp.float32
            )
            slot = jnp.sum(jnp.where(hot, carry + counts[:, :LANES], 0.0), axis=0, keepdims=True)
            slot = slot.astype(jnp.int32) - 1
            carry = carry + counts[:, LANES:]
            quarter = slot >> 4
            chip = shard >> 1
            parity = (shard & 1) ^ core
            side = core if x == 2 else x
            v = (chip & 3) * 32 + side * 16 + (slot & 15)
            if x == 2:
                u = (parity * 4 + ((rep - quarter) & 3)) * 8 + (chip >> 2)
                place_ref[j : j + 1, :] = u * 128 + v
            else:
                u = parity * 32 + ((quarter - rep) & 3) * 8 + (chip >> 2)
                u_hot = u == u_iota
                t = thr[j : j + 1, :]
                lanes = slice(j * LANES, (j + 1) * LANES)
                u_ref[0:64, lanes] = jnp.where(u_hot, (t >> 4).astype(jnp.float32), 0.0).astype(jnp.bfloat16)
                u_ref[64:128, lanes] = jnp.where(u_hot, (t & 15).astype(jnp.float32), 0.0).astype(jnp.bfloat16)
                u_ref[128:192, lanes] = jnp.where(u_hot, float(j >= 16), 0.0).astype(jnp.bfloat16)
                v_ref[:, lanes] = jnp.where(v == v_iota, 1.0, 0.0).astype(jnp.bfloat16)
        if x < 2:
            us = u_ref[...]
            vs = v_ref[...]
            row_sums.append(lax.dot_general(us, vs, NT, preferred_element_type=jnp.float32))
            col_sums.append(lax.dot_general(vs, us, NT, preferred_element_type=jnp.float32))
        if x == 1:
            rows = row_sums[0] + row_sums[1]
            cols = col_sums[0] + col_sums[1]
            row_rho = 1024.0 / (rows[0:64] * 16.0 + rows[64:128])
            col_rho = 1024.0 / (cols[:, 0:64] * 16.0 + cols[:, 64:128])
            for p in range(2):
                at = slice(p * 32, p * 32 + 32)
                up = slice(128 + p * 32, 160 + p * 32)
                row_ref[p, 0:32, :] = row_rho[at]
                row_ref[p, 32:64, :] = rows[up]
                col_ref[p, :, 0:32] = col_rho[:, at]
                col_ref[p, :, 32:64] = cols[:, up]


def place(scalars, rank2d, thr2d):
    return pl.pallas_call(
        place_kernel,
        out_shape=(
            jax.ShapeDtypeStruct((2, 64, LANES), jnp.float32),
            jax.ShapeDtypeStruct((2, LANES, 64), jnp.float32),
            jax.ShapeDtypeStruct((32, LANES), jnp.int32),
        ),
        in_specs=[smem(), hbm(), hbm()],
        out_specs=(vmem(),) * 3,
        scratch_shapes=[
            pltpu.VMEM((192, 4096), jnp.bfloat16),
            pltpu.VMEM((LANES, 4096), jnp.bfloat16),
            pltpu.VMEM((3, 32, LANES), jnp.int32),
            pltpu.VMEM((3, 32, LANES), jnp.int32),
            pltpu.SemaphoreType.DMA((3, 2)),
        ],
        compiler_params=pltpu.CompilerParams(vmem_limit_bytes=VMEM),
        cost_estimate=pl.CostEstimate(flops=2 * 10**9, bytes_accessed=10**7, transcendentals=0),
        name="place",
    )(scalars, rank2d, thr2d)


def square_sums(block):
    values = block.astype(jnp.float32)
    square = values * values
    total = square[:, :LANES] + square[:, LANES:]
    high = total.astype(jnp.bfloat16)
    rest = total - high.astype(jnp.float32)
    middle = rest.astype(jnp.bfloat16)
    low = (rest - middle.astype(jnp.float32)).astype(jnp.bfloat16)
    return high, middle, low


def inverse_column(terms):
    ones = jnp.ones((LANES, LANES), jnp.bfloat16)
    high, middle, low = (jnp.dot(t, ones, preferred_element_type=jnp.float32) for t in terms)
    return lax.rsqrt(high + (middle + low) + 1e-06)


def inverse_row(terms):
    ones = jnp.ones((8, LANES), jnp.bfloat16)
    high, middle, low = (
        lax.dot_general(ones, t, NT, preferred_element_type=jnp.float32) for t in terms
    )
    return lax.rsqrt(high + (middle + low) + 1e-06)


def load_column_meta(col_ref, band, quarter, meta):
    for u in range(8):
        rows = slice(u * LANES, (u + 1) * LANES)
        i = quarter * 8 + u
        meta[1, rows, :] = jnp.broadcast_to(col_ref[band, :, i : i + 1], (LANES, LANES))
        meta[2, rows, :] = jnp.broadcast_to(col_ref[band, :, 32 + i : 33 + i], (LANES, LANES))


def load_row_meta(at, row_ref, parity, quarter, keep_ref, offsets, meta, keep):
    second = ((lax.broadcasted_iota(jnp.int32, (8, LANES), 1) >> 4) & 1) == 1
    for u in range(8):
        lanes = slice(at + u * LANES, at + (u + 1) * LANES)
        i = quarter * 8 + u
        meta[1, :, lanes] = jnp.broadcast_to(row_ref[parity, i : i + 1, :], (8, LANES))
        upper = jnp.broadcast_to(row_ref[parity, 32 + i : 33 + i, :], (8, LANES)) > 0.5
        for t in range(4):
            code = (offsets[t // 2] + t % 2) * 4
            one, two = (
                jnp.where(upper, keep_ref[code + offset + 1], keep_ref[code + offset])
                for offset in offsets
            )
            keep[t, :, lanes] = jnp.where(second, two, one)


def product(left_ref, left_at, right_ref, right_at, prod_ref):
    rows, cols = prod_ref.shape
    prod_ref[...] = lax.dot_general(
        left_ref[pl.ds(left_at, rows), :], right_ref[pl.ds(right_at, cols), :], NT,
        preferred_element_type=jnp.float32,
    )


def weigh(prod_ref, left_at, left_meta, right_at, right_meta, keep, row_sum, col_sum, diagonal):
    chunks = prod_ref.shape[1] // LANES
    sums = [jnp.zeros((8, LANES), jnp.float32) for _ in range(chunks)]
    lanes = [pl.ds(pl.multiple_of(right_at + ch * LANES, LANES), LANES) for ch in range(chunks)]
    for i in range(prod_ref.shape[0] // 32):
        rows = pl.ds(pl.multiple_of(left_at + i * 32, 32), 32)
        inv_i = left_meta[0, rows, :].reshape(4, 8, LANES)
        rho_i = left_meta[1, rows, :].reshape(4, 8, LANES)
        upper = left_meta[2, rows, :].reshape(4, 8, LANES) > 0.5
        total = row_sum[rows, :].reshape(4, 8, LANES)
        for ch in range(chunks):
            inv_j = right_meta[0, :, lanes[ch]][None]
            rho_j = right_meta[1, :, lanes[ch]][None]
            k = [keep[t, :, lanes[ch]][None] for t in range(4)]
            kept = jnp.concatenate(
                [jnp.where(upper[:2], k[1], k[0]), jnp.where(upper[2:], k[3], k[2])], axis=0
            )
            p = prod_ref[i * 32 : i * 32 + 32, ch * LANES : (ch + 1) * LANES].reshape(4, 8, LANES)
            near = (p * inv_i) * inv_j - 1.0
            w = jnp.maximum(near * jnp.maximum(rho_i, rho_j) + kept, 0.0)
            if diagonal:
                row_ids = lax.broadcasted_iota(jnp.int32, w.shape, 0) * 8 + lax.broadcasted_iota(jnp.int32, w.shape, 1)
                col_ids = lax.broadcasted_iota(jnp.int32, w.shape, 2)
                w = jnp.where(row_ids + (left_at + i * 32) == col_ids + (right_at + ch * LANES), 0.0, w)
            total = total + w
            if not diagonal:
                sums[ch] = sums[ch] + ((w[0] + w[1]) + (w[2] + w[3]))
        row_sum[rows, :] = total.reshape(32, LANES)
    if not diagonal:
        for ch in range(chunks):
            col_sum[:, lanes[ch]] += sums[ch]


def rows_to_lanes(row_sum):
    row = lax.broadcasted_iota(jnp.int32, (LANES, LANES), 0)
    lane = lax.broadcasted_iota(jnp.int32, (LANES, LANES), 1)
    out = []
    for u in range(8):
        total = jnp.sum(row_sum[u * LANES : (u + 1) * LANES, :], axis=1, keepdims=True)
        out.append(jnp.sum(jnp.where(row == lane, total, 0.0), axis=0, keepdims=True))
    return out


def cols_to_lanes(col_sum, at):
    return [
        jnp.sum(col_sum[:, at + u * LANES : at + (u + 1) * LANES], axis=0, keepdims=True)
        for u in range(8)
    ]


def near_kernel(s_ref, keep_ref, own_ref, other_ref, row_ref, col_ref, out_ref, inverse_ref,
                left_meta, right_meta, keep, prod_a, prod_b, row_sum, col_sum):
    core = s_ref[6]
    offsets = (s_ref[7], s_ref[8])
    terms = square_sums(own_ref[...])
    left_meta[0] = inverse_column(terms)
    right_meta[0, :, 0:1024] = inverse_row(terms)
    right_meta[0, :, 1024:2048] = inverse_row(square_sums(other_ref[...]))
    inverse_ref[...] = right_meta[0]
    load_column_meta(col_ref, 0, 0, left_meta)
    load_row_meta(0, row_ref, 0, 0, keep_ref, offsets, right_meta, keep)
    load_row_meta(1024, row_ref, 1, 0, keep_ref, offsets, right_meta, keep)
    row_sum[...] = jnp.zeros_like(row_sum)
    col_sum[...] = jnp.zeros_like(col_sum)

    @pl.loop(0, 4)
    def _(i):
        at = pl.multiple_of(i * 256, 256)
        half = pl.multiple_of(((i >> 1) ^ core) * 512, 512)
        product(own_ref, at, own_ref, 0, prod_a)
        product(own_ref, at, own_ref, 512, prod_b)
        weigh(prod_a, at, left_meta, 0, right_meta, keep, row_sum, col_sum, True)
        product(own_ref, at, other_ref, half, prod_a)
        weigh(prod_b, at, left_meta, 512, right_meta, keep, row_sum, col_sum, True)
        weigh(prod_a, at, left_meta, 1024 + half, right_meta, keep, row_sum, col_sum, False)

    own = rows_to_lanes(row_sum)
    other = cols_to_lanes(col_sum, 1024)
    for u in range(8):
        out_ref[0, u : u + 1, :] = own[u]
        out_ref[1, u : u + 1, :] = other[u]


def far_kernel(s_ref, keep_ref, own_hbm, other_hbm, right_ref, left_hbm, row_ref, col_ref, near_ref,
               inverse_ref, out_ref, block_ref, left_meta, right_meta, keep, prod_a,
               prod_b, row_sum, col_sum, sems):
    offsets = (s_ref[7], s_ref[8])
    cross = s_ref[9]
    copies = [
        pltpu.make_async_copy(source, block_ref.at[pl.ds(i * 1024, 1024), :], sems.at[i])
        for i, source in enumerate((own_hbm, other_hbm, left_hbm))
    ]
    for copy in copies:
        copy.start()
    left_meta[0] = inverse_column(square_sums(right_ref[...]))
    load_column_meta(col_ref, 0, 1, left_meta)
    load_row_meta(0, row_ref, 0, 0, keep_ref, offsets, right_meta, keep)
    load_row_meta(1024, row_ref, 1, 0, keep_ref, offsets, right_meta, keep)
    load_row_meta(2048, row_ref, cross, 3, keep_ref, offsets, right_meta, keep)
    right_meta[0, :, 0:2048] = inverse_ref[...]
    row_sum[...] = jnp.zeros_like(row_sum)
    col_sum[...] = jnp.zeros_like(col_sum)
    for copy in copies:
        copy.wait()
    right_meta[0, :, 2048:3072] = inverse_row(square_sums(block_ref[2048:3072, :]))
    rows, cols = prod_a.shape
    steps = 1024 // rows
    total = steps * (3072 // cols)
    product(right_ref, 0, block_ref, 0, prod_a)

    def place_of(t):
        return pl.multiple_of((t % steps) * rows, rows), pl.multiple_of((t // steps) * cols, cols)

    @pl.loop(0, total // 2)
    def _(i):
        left_a, right_a = place_of(i * 2)
        left_b, right_b = place_of(i * 2 + 1)
        left_c, right_c = place_of(jnp.minimum(i * 2 + 2, total - 1))
        product(right_ref, left_b, block_ref, right_b, prod_b)
        weigh(prod_a, left_a, left_meta, right_a, right_meta, keep, row_sum, col_sum, False)
        product(right_ref, left_c, block_ref, right_c, prod_a)
        weigh(prod_b, left_b, left_meta, right_b, right_meta, keep, row_sum, col_sum, False)

    right = rows_to_lanes(row_sum)
    own = cols_to_lanes(col_sum, 0)
    other = cols_to_lanes(col_sum, 1024)
    left = cols_to_lanes(col_sum, 2048)
    for u in range(8):
        row = slice(u, u + 1)
        out_ref[0, row, :] = own[u] + near_ref[0, row, :]
        out_ref[1, row, :] = other[u] + near_ref[1, row, :]
        out_ref[2, row, :] = right[u]
        out_ref[3, row, :] = left[u]


FAR_TILE = (1024, 256)


def pair_scratch(columns, tile):
    return [
        pltpu.VMEM((3, 1024, LANES), jnp.float32),
        pltpu.VMEM((2, 8, columns), jnp.float32),
        pltpu.VMEM((4, 8, columns), jnp.float32),
        pltpu.VMEM(tile, jnp.float32),
        pltpu.VMEM(tile, jnp.float32),
        pltpu.VMEM((1024, LANES), jnp.float32),
        pltpu.VMEM((8, columns), jnp.float32),
    ]


def near_pairs(scalars, keep, own, other, rows, cols):
    return pl.pallas_call(
        near_kernel,
        out_shape=(
            jax.ShapeDtypeStruct((2, 8, LANES), jnp.float32),
            jax.ShapeDtypeStruct((8, 2048), jnp.float32),
        ),
        in_specs=[smem(), smem(), vmem(), vmem(), vmem(), vmem()],
        out_specs=(vmem(), vmem()),
        scratch_shapes=pair_scratch(2048, (256, 512)),
        compiler_params=pltpu.CompilerParams(vmem_limit_bytes=VMEM),
        cost_estimate=pl.CostEstimate(flops=2 * 10**9, bytes_accessed=10**7, transcendentals=0),
        name="near_pairs",
    )(scalars, keep, own, other, rows, cols)


def far_pairs(scalars, keep, own, other, right, left, rows, cols, near):
    return pl.pallas_call(
        far_kernel,
        out_shape=jax.ShapeDtypeStruct((4, 8, LANES), jnp.float32),
        in_specs=[smem(), smem(), hbm(), hbm(), vmem(), hbm()] + [vmem()] * 4,
        out_specs=vmem(),
        scratch_shapes=[pltpu.VMEM((3072, 256), jnp.bfloat16)]
        + pair_scratch(3072, FAR_TILE)
        + [pltpu.SemaphoreType.DMA((3,))],
        compiler_params=pltpu.CompilerParams(vmem_limit_bytes=VMEM),
        cost_estimate=pl.CostEstimate(flops=4 * 10**9, bytes_accessed=10**7, transcendentals=0),
        name="far_pairs",
    )(scalars, keep, own, other, right, left, rows, cols, *near)


def rank_kernel(place_ref, *refs):
    pieces, out_ref = refs[:-1], refs[-1]
    place_at = place_ref[...]
    lane = place_at & 127
    which = place_at >> 7
    total = jnp.zeros((32, LANES), jnp.float32)
    for i in range(8):
        p, s = i // 4, i % 4
        block = pieces[s][p] + pieces[(s + 1) % 4][2 + p] + pieces[(s + 3) % 4][4 + p]
        for u in range(8):
            row = jnp.broadcast_to(block[u : u + 1, :], (32, LANES))
            value = jnp.take_along_axis(row, lane, axis=1)
            total = jnp.where(which == i * 8 + u, value, total)
    out_ref[...] = total * (1.0 / TILE)


def to_rank_order(place_at, pieces):
    return pl.pallas_call(
        rank_kernel,
        out_shape=jax.ShapeDtypeStruct((32, LANES), jnp.float32),
        in_specs=[vmem()] * 5,
        out_specs=vmem(),
        compiler_params=pltpu.CompilerParams(vmem_limit_bytes=VMEM),
        name="to_rank_order",
    )(place_at, *pieces)


def on_device(points, rank_source, thresholds, kept_tiles):
    bands = lax.axis_size("band")
    reps = lax.axis_size("rep")
    device = lax.axis_index("band").astype(jnp.int32)
    rep = lax.axis_index("rep").astype(jnp.int32)
    core = device & 1
    host = device ^ 8
    own_band = jnp.where(core == 0, host, bands - host)
    other_band = bands - 1 - own_band
    first_band = jnp.where(core == 0, own_band, other_band)
    second_band = bands - 1 - first_band
    first_offset = jnp.where(first_band < bands // 2, 0, 2)
    cross = (rep >= 2).astype(jnp.int32)
    scalars = jnp.stack([
        device, rep * 16, rep, first_band, second_band, device, core,
        first_offset, 2 - first_offset, cross,
    ]).astype(jnp.int32)
    codes = lax.dynamic_index_in_dim(kept_tiles, jnp.minimum(own_band, other_band), 0, keepdims=False)
    ids = jnp.arange(16, dtype=jnp.int32)
    a, c = ids // 4, ids % 4
    wanted = jnp.minimum(a, c) * 4 + jnp.maximum(a, c)
    keep = jnp.where(jnp.any(codes[:, None] == wanted[None, :], axis=0), 1.0, -1e30).astype(jnp.float32)

    rank2d = rank_source.reshape(2048, LANES)
    thr2d = thresholds.reshape(2048, LANES)

    def joint(move):
        return [
            (d * reps + r, e * reps + q)
            for d in range(bands)
            for r in range(reps)
            for e, q in (move(d, r),)
        ]

    def shift(value, move):
        return lax.ppermute(value, ("band", "rep"), joint(move))

    payload = send_rows(rank2d, points)
    own = lax.all_to_all(
        payload.reshape(bands // 2, 32, 256), "band", split_axis=0, concat_axis=0, tiled=True,
        axis_index_groups=[list(range(k, bands, 2)) for k in range(2)],
    ).reshape(1024, 256)
    own, rows, cols, place_at = lax.optimization_barrier((own, *place(scalars, rank2d, thr2d)))

    def to_right(d, r):
        q = (r + 1) % reps
        return (d if q < 2 else d ^ 1), q

    other = shift(own, lambda d, r: (d ^ 1, r))
    left = shift(own, to_right)
    right = shift(own, lambda d, r: (d, (r - 1) % reps))

    near = near_pairs(scalars, keep, own, other, rows, cols)
    sums = far_pairs(scalars, keep, own, other, right, left, rows, cols, near)
    theirs = shift(sums, lambda d, r: (d ^ 1, r))
    swap = cross == 1
    sums = jnp.stack([
        sums[0] + theirs[1], sums[1] + theirs[0], sums[2], theirs[2],
        jnp.where(swap, theirs[3], sums[3]), jnp.where(swap, sums[3], theirs[3]),
    ])
    home = shift(sums, lambda d, r: (block_band(d), r))
    pieces = [home] + [
        shift(home, lambda d, r, s=s: (d, (r + s) % reps)) for s in range(1, reps)
    ]
    return to_rank_order(place_at, pieces).reshape(points.shape[0])


def solution(mesh):
    in_specs = (P("band", None), P(), P(), P())
    out_specs = P("band")
    return jax.shard_map(
        on_device, mesh=mesh, in_specs=in_specs, out_specs=out_specs, check_vma=False
    )
```

```python
import jax
import jax.numpy as jnp
from jax import lax
from jax.experimental import pallas as pl
from jax.experimental.pallas import tpu as pltpu
from jax.sharding import PartitionSpec as P

TILE = 2048
LANES = 128
SEND_VMEM = 60 * 1024 * 1024
VMEM = 28 * 1024 * 1024
NT = (((1,), (1,)), ((), ()))


def prefix_matrix():
    row = lax.broadcasted_iota(jnp.int32, (LANES, 2 * LANES), 0)
    col = lax.broadcasted_iota(jnp.int32, (LANES, 2 * LANES), 1)
    return jnp.where((row <= col) | (col >= LANES), 1.0, 0.0).astype(jnp.bfloat16)


def block_band(device):
    host = device ^ 8
    return host if host % 2 == 0 else 64 - host


def smem():
    return pl.BlockSpec(memory_space=pltpu.SMEM)


def vmem():
    return pl.BlockSpec(memory_space=pltpu.VMEM)


def hbm():
    return pl.BlockSpec(memory_space=pltpu.HBM)


def send_kernel(rank_hbm, points_hbm, out_ref, rank_ref, points_ref, acc_ref, row_ref,
                hot_ref, rank_sem, points_sem):
    def fetch_rank(g):
        rows = pl.ds(g * 256, 256)
        return pltpu.make_async_copy(rank_hbm.at[rows, :], rank_ref.at[rows, :], rank_sem.at[g])

    for g in range(8):
        fetch_rank(g).start()
    fetch_points = pltpu.make_async_copy(points_hbm, points_ref, points_sem)
    fetch_points.start()
    shard = lax.axis_index("band")
    prefix = prefix_matrix()
    base = (lax.axis_index("rep") * 16 + 1).astype(jnp.float32)
    ones = jnp.ones((LANES, LANES), jnp.bfloat16)
    for g in range(8):
        fetch_rank(g).wait()
        source = [rank_ref[pl.ds(g * 256 + j, 8, stride=32), :] for j in range(32)]
        mine = [(source[j] >> 12) == shard for j in range(32)]
        marks = jnp.concatenate([jnp.where(m, 1.0, 0.0) for m in mine], axis=0).astype(jnp.bfloat16)
        counts = jnp.dot(marks, prefix, preferred_element_type=jnp.float32)
        carry = jnp.zeros((8, LANES), jnp.float32) - base
        accs = [jnp.zeros((8, LANES), jnp.int32) for _ in range(16)]
        for j in range(32):
            pos = jnp.where(mine[j], carry + counts[j * 8 : j * 8 + 8, :LANES], -1.0)
            loc = source[j] & 4095
            carry = carry + counts[j * 8 : j * 8 + 8, LANES:]
            for i in range(16):
                accs[i] = jnp.where(pos == float(i), loc, accs[i])
        for i in range(16):
            acc_ref[g * 128 + i * 8 : g * 128 + i * 8 + 8, :] = accs[i]

    acc = acc_ref[...]
    high = (acc >> 6).astype(jnp.float32).astype(jnp.bfloat16)
    low = (acc & 63).astype(jnp.float32).astype(jnp.bfloat16)
    row_ref[...] = 64.0 * jnp.dot(high, ones, preferred_element_type=jnp.float32) + jnp.dot(
        low, ones, preferred_element_type=jnp.float32
    )
    fetch_points.wait()
    lane = lax.broadcasted_iota(jnp.int32, (1024, LANES), 1)
    one = jnp.ones((1024, LANES), jnp.bfloat16)
    zero = jnp.zeros((1024, LANES), jnp.bfloat16)
    parts = []
    for i in range(64):
        band = block_band(i)
        parts.append(row_ref[pl.ds((band // 8) * 128 + band % 8, 16, stride=8), :])
    local = jnp.concatenate(parts, axis=0).astype(jnp.int32)
    chunk = (local >> 7).astype(jnp.float32).astype(jnp.bfloat16)
    hot = jnp.where((local & 127) == lane, 1.0, 0.0).astype(jnp.bfloat16)
    for ch in range(32):
        hot_ref[:, ch * 128 : (ch + 1) * 128] = jnp.where(chunk == one * ch, hot, zero)
    out_ref[...] = jnp.dot(
        hot_ref[...], points_ref[...], preferred_element_type=jnp.float32
    ).astype(jnp.bfloat16)


def send_rows(rank2d, points):
    return pl.pallas_call(
        send_kernel,
        out_shape=jax.ShapeDtypeStruct((1024, 256), jnp.bfloat16),
        in_specs=[hbm(), hbm()],
        out_specs=vmem(),
        scratch_shapes=[
            pltpu.VMEM((2048, LANES), jnp.int32),
            pltpu.VMEM((4096, 256), jnp.bfloat16),
            pltpu.VMEM((1024, LANES), jnp.int32),
            pltpu.VMEM((1024, LANES), jnp.float32),
            pltpu.VMEM((1024, 4096), jnp.bfloat16),
            pltpu.SemaphoreType.DMA((8,)),
            pltpu.SemaphoreType.DMA,
        ],
        compiler_params=pltpu.CompilerParams(vmem_limit_bytes=SEND_VMEM),
        name="send_rows",
    )(rank2d, points)


def place_kernel(s_ref, rank_hbm, thr_hbm, row_ref, col_ref, place_ref, u_ref, v_ref, rank_ref, thr_ref, sems):
    copies = []
    for x in range(3):
        start = pl.multiple_of(s_ref[3 + x] * 32, 32)
        copies.append((
            pltpu.make_async_copy(rank_hbm.at[pl.ds(start, 32), :], rank_ref.at[x], sems.at[x, 0]),
            pltpu.make_async_copy(thr_hbm.at[pl.ds(start, 32), :], thr_ref.at[x], sems.at[x, 1]),
        ))
        for copy in copies[x]:
            copy.start()
    rep = s_ref[2]
    prefix = prefix_matrix()
    shard_iota = lax.broadcasted_iota(jnp.int32, (64, LANES), 0)
    u_iota = lax.broadcasted_iota(jnp.int32, (32, LANES), 0)
    v_iota = lax.broadcasted_iota(jnp.int32, (LANES, LANES), 0)
    for x in range(3):
        for copy in copies[x]:
            copy.wait()
        carry = jnp.zeros((64, LANES), jnp.float32)
        source = rank_ref[x] >> 12
        thr = thr_ref[x]
        for j in range(32):
            shard = source[j : j + 1, :]
            hot = shard == shard_iota
            counts = jnp.dot(
                jnp.where(hot, 1.0, 0.0).astype(jnp.bfloat16), prefix, preferred_element_type=jnp.float32
            )
            slot = jnp.sum(jnp.where(hot, carry + counts[:, :LANES], 0.0), axis=0, keepdims=True)
            slot = slot.astype(jnp.int32) - 1
            carry = carry + counts[:, LANES:]
            quarter = slot >> 4
            v = (shard & 7) * 16 + (slot & 15)
            if x == 2:
                place_ref[j : j + 1, :] = (((rep - quarter) & 3) * 8 + (shard >> 3)) * 128 + v
            else:
                u = ((quarter - rep) & 3) * 8 + (shard >> 3)
                u_hot = u == u_iota
                t = thr[j : j + 1, :]
                lanes = slice(j * LANES, (j + 1) * LANES)
                u_ref[0:32, lanes] = jnp.where(u_hot, (t >> 4).astype(jnp.float32), 0.0).astype(jnp.bfloat16)
                u_ref[32:64, lanes] = jnp.where(u_hot, (t & 15).astype(jnp.float32), 0.0).astype(jnp.bfloat16)
                u_ref[64:96, lanes] = jnp.where(u_hot, float(j >= 16), 0.0).astype(jnp.bfloat16)
                v_ref[:, lanes] = jnp.where(v == v_iota, 1.0, 0.0).astype(jnp.bfloat16)
        if x < 2:
            us = u_ref[...]
            vs = v_ref[...]
            rows = lax.dot_general(us, vs, NT, preferred_element_type=jnp.float32)
            cols = lax.dot_general(vs, us, NT, preferred_element_type=jnp.float32)
            row_ref[x, 0:32, :] = 1024.0 / (rows[0:32] * 16.0 + rows[32:64])
            row_ref[x, 32:64, :] = rows[64:96]
            col_ref[x, :, 0:32] = 1024.0 / (cols[:, 0:32] * 16.0 + cols[:, 32:64])
            col_ref[x, :, 32:64] = cols[:, 64:96]


def place(scalars, rank2d, thr2d):
    return pl.pallas_call(
        place_kernel,
        out_shape=(
            jax.ShapeDtypeStruct((2, 64, LANES), jnp.float32),
            jax.ShapeDtypeStruct((2, LANES, 64), jnp.float32),
            jax.ShapeDtypeStruct((32, LANES), jnp.int32),
        ),
        in_specs=[smem(), hbm(), hbm()],
        out_specs=(vmem(),) * 3,
        scratch_shapes=[
            pltpu.VMEM((96, 4096), jnp.bfloat16),
            pltpu.VMEM((LANES, 4096), jnp.bfloat16),
            pltpu.VMEM((3, 32, LANES), jnp.int32),
            pltpu.VMEM((3, 32, LANES), jnp.int32),
            pltpu.SemaphoreType.DMA((3, 2)),
        ],
        compiler_params=pltpu.CompilerParams(vmem_limit_bytes=VMEM),
        cost_estimate=pl.CostEstimate(flops=2 * 10**9, bytes_accessed=10**7, transcendentals=0),
        name="place",
    )(scalars, rank2d, thr2d)


def square_sums(block):
    values = block.astype(jnp.float32)
    square = values * values
    total = square[:, :LANES] + square[:, LANES:]
    high = total.astype(jnp.bfloat16)
    rest = total - high.astype(jnp.float32)
    middle = rest.astype(jnp.bfloat16)
    low = (rest - middle.astype(jnp.float32)).astype(jnp.bfloat16)
    return high, middle, low


def inverse_column(terms):
    ones = jnp.ones((LANES, LANES), jnp.bfloat16)
    high, middle, low = (jnp.dot(t, ones, preferred_element_type=jnp.float32) for t in terms)
    return lax.rsqrt(high + (middle + low) + 1e-06)


def inverse_row(terms):
    ones = jnp.ones((8, LANES), jnp.bfloat16)
    high, middle, low = (
        lax.dot_general(ones, t, NT, preferred_element_type=jnp.float32) for t in terms
    )
    return lax.rsqrt(high + (middle + low) + 1e-06)


def load_column_meta(col_ref, band, quarter, meta):
    for u in range(8):
        rows = slice(u * LANES, (u + 1) * LANES)
        i = quarter * 8 + u
        meta[1, rows, :] = jnp.broadcast_to(col_ref[band, :, i : i + 1], (LANES, LANES))
        meta[2, rows, :] = jnp.broadcast_to(col_ref[band, :, 32 + i : 33 + i], (LANES, LANES))


def load_row_meta(at, row_ref, band, quarter, keep_ref, row_offset, col_offset, meta, keep):
    for u in range(8):
        lanes = slice(at + u * LANES, at + (u + 1) * LANES)
        i = quarter * 8 + u
        meta[1, :, lanes] = jnp.broadcast_to(row_ref[band, i : i + 1, :], (8, LANES))
        upper = jnp.broadcast_to(row_ref[band, 32 + i : 33 + i, :], (8, LANES)) > 0.5
        for t in range(2):
            code = (row_offset + t) * 4 + col_offset
            keep[t, :, lanes] = jnp.where(upper, keep_ref[code + 1], keep_ref[code])


def product(left_ref, left_at, right_ref, right_at, prod_ref):
    rows, cols = prod_ref.shape
    prod_ref[...] = lax.dot_general(
        left_ref[pl.ds(left_at, rows), :], right_ref[pl.ds(right_at, cols), :], NT,
        preferred_element_type=jnp.float32,
    )


def weigh(prod_ref, left_at, left_meta, right_at, right_meta, keep, row_sum, col_sum, diagonal):
    chunks = prod_ref.shape[1] // LANES
    sums = [jnp.zeros((8, LANES), jnp.float32) for _ in range(chunks)]
    lanes = [pl.ds(pl.multiple_of(right_at + ch * LANES, LANES), LANES) for ch in range(chunks)]
    for i in range(prod_ref.shape[0] // 32):
        rows = pl.ds(pl.multiple_of(left_at + i * 32, 32), 32)
        inv_i = left_meta[0, rows, :].reshape(4, 8, LANES)
        rho_i = left_meta[1, rows, :].reshape(4, 8, LANES)
        upper = left_meta[2, rows, :].reshape(4, 8, LANES) > 0.5
        total = row_sum[rows, :].reshape(4, 8, LANES)
        for ch in range(chunks):
            inv_j = right_meta[0, :, lanes[ch]][None]
            rho_j = right_meta[1, :, lanes[ch]][None]
            kept = jnp.where(upper, keep[1, :, lanes[ch]][None], keep[0, :, lanes[ch]][None])
            p = prod_ref[i * 32 : i * 32 + 32, ch * LANES : (ch + 1) * LANES].reshape(4, 8, LANES)
            near = (p * inv_i) * inv_j - 1.0
            w = jnp.maximum(near * jnp.maximum(rho_i, rho_j) + kept, 0.0)
            if diagonal:
                row_ids = lax.broadcasted_iota(jnp.int32, w.shape, 0) * 8 + lax.broadcasted_iota(jnp.int32, w.shape, 1)
                col_ids = lax.broadcasted_iota(jnp.int32, w.shape, 2)
                w = jnp.where(row_ids + (left_at + i * 32) == col_ids + (right_at + ch * LANES), 0.0, w)
            total = total + w
            if not diagonal:
                sums[ch] = sums[ch] + ((w[0] + w[1]) + (w[2] + w[3]))
        row_sum[rows, :] = total.reshape(32, LANES)
    if not diagonal:
        for ch in range(chunks):
            col_sum[:, lanes[ch]] += sums[ch]


def rows_to_lanes(row_sum):
    row = lax.broadcasted_iota(jnp.int32, (LANES, LANES), 0)
    lane = lax.broadcasted_iota(jnp.int32, (LANES, LANES), 1)
    out = []
    for u in range(8):
        total = jnp.sum(row_sum[u * LANES : (u + 1) * LANES, :], axis=1, keepdims=True)
        out.append(jnp.sum(jnp.where(row == lane, total, 0.0), axis=0, keepdims=True))
    return out


def cols_to_lanes(col_sum, at):
    return [
        jnp.sum(col_sum[:, at + u * LANES : at + (u + 1) * LANES], axis=0, keepdims=True)
        for u in range(8)
    ]


def near_kernel(s_ref, keep_ref, own_ref, other_ref, row_ref, col_ref, out_ref, inverse_ref,
                left_meta, right_meta, keep, prod_a, prod_b, row_sum, col_sum):
    core = s_ref[6]
    own_offset = s_ref[7]
    other_offset = s_ref[8]
    terms = square_sums(own_ref[...])
    left_meta[0] = inverse_column(terms)
    right_meta[0, :, 0:1024] = inverse_row(terms)
    right_meta[0, :, 1024:2048] = inverse_row(square_sums(other_ref[...]))
    inverse_ref[...] = right_meta[0]
    load_column_meta(col_ref, 0, 0, left_meta)
    load_row_meta(0, row_ref, 0, 0, keep_ref, own_offset, own_offset, right_meta, keep)
    load_row_meta(1024, row_ref, 1, 0, keep_ref, own_offset, other_offset, right_meta, keep)
    row_sum[...] = jnp.zeros_like(row_sum)
    col_sum[...] = jnp.zeros_like(col_sum)

    @pl.loop(0, 4)
    def _(i):
        at = pl.multiple_of(i * 256, 256)
        half = pl.multiple_of(((i >> 1) ^ core) * 512, 512)
        product(own_ref, at, own_ref, 0, prod_a)
        product(own_ref, at, own_ref, 512, prod_b)
        weigh(prod_a, at, left_meta, 0, right_meta, keep, row_sum, col_sum, True)
        product(own_ref, at, other_ref, half, prod_a)
        weigh(prod_b, at, left_meta, 512, right_meta, keep, row_sum, col_sum, True)
        weigh(prod_a, at, left_meta, 1024 + half, right_meta, keep, row_sum, col_sum, False)

    own = rows_to_lanes(row_sum)
    other = cols_to_lanes(col_sum, 1024)
    for u in range(8):
        out_ref[0, u : u + 1, :] = own[u]
        out_ref[1, u : u + 1, :] = other[u]


def far_kernel(s_ref, keep_ref, own_hbm, other_hbm, left_hbm, right_ref, row_ref, col_ref, near_ref,
               inverse_ref, stay_ref, move_ref, block_ref, left_meta, right_meta, keep, prod_a,
               prod_b, row_sum, col_sum, sems):
    own_offset = s_ref[7]
    other_offset = s_ref[8]
    cross = s_ref[9]
    left_offset = s_ref[10]
    copies = [
        pltpu.make_async_copy(source, block_ref.at[pl.ds(i * 1024, 1024), :], sems.at[i])
        for i, source in enumerate((own_hbm, other_hbm, left_hbm))
    ]
    for copy in copies:
        copy.start()
    left_meta[0] = inverse_column(square_sums(right_ref[...]))
    load_column_meta(col_ref, 0, 1, left_meta)
    load_row_meta(0, row_ref, 0, 0, keep_ref, own_offset, own_offset, right_meta, keep)
    load_row_meta(1024, row_ref, 1, 0, keep_ref, own_offset, other_offset, right_meta, keep)
    load_row_meta(2048, row_ref, cross, 3, keep_ref, own_offset, left_offset, right_meta, keep)
    right_meta[0, :, 0:2048] = inverse_ref[...]
    row_sum[...] = jnp.zeros_like(row_sum)
    col_sum[...] = jnp.zeros_like(col_sum)
    for copy in copies:
        copy.wait()
    right_meta[0, :, 2048:3072] = inverse_row(square_sums(block_ref[2048:3072, :]))
    rows, cols = prod_a.shape
    steps = 1024 // rows
    total = steps * (3072 // cols)
    product(right_ref, 0, block_ref, 0, prod_a)

    def place_of(t):
        return pl.multiple_of((t % steps) * rows, rows), pl.multiple_of((t // steps) * cols, cols)

    @pl.loop(0, total // 2)
    def _(i):
        left_a, right_a = place_of(i * 2)
        left_b, right_b = place_of(i * 2 + 1)
        left_c, right_c = place_of(jnp.minimum(i * 2 + 2, total - 1))
        product(right_ref, left_b, block_ref, right_b, prod_b)
        weigh(prod_a, left_a, left_meta, right_a, right_meta, keep, row_sum, col_sum, False)
        product(right_ref, left_c, block_ref, right_c, prod_a)
        weigh(prod_b, left_b, left_meta, right_b, right_meta, keep, row_sum, col_sum, False)

    right = rows_to_lanes(row_sum)
    own = cols_to_lanes(col_sum, 0)
    other = cols_to_lanes(col_sum, 1024)
    left = cols_to_lanes(col_sum, 2048)
    for u in range(8):
        row = slice(u, u + 1)
        stay_ref[0, row, :] = own[u] + near_ref[0, row, :]
        stay_ref[1, row, :] = right[u]
        stay_ref[2, row, :] = jnp.where(cross == 0, left[u], 0.0)
        move_ref[0, row, :] = other[u] + near_ref[1, row, :]
        move_ref[1, row, :] = jnp.where(cross == 0, 0.0, left[u])


FAR_TILE = (1024, 256)


def pair_scratch(columns, tile):
    return [
        pltpu.VMEM((3, 1024, LANES), jnp.float32),
        pltpu.VMEM((2, 8, columns), jnp.float32),
        pltpu.VMEM((2, 8, columns), jnp.float32),
        pltpu.VMEM(tile, jnp.float32),
        pltpu.VMEM(tile, jnp.float32),
        pltpu.VMEM((1024, LANES), jnp.float32),
        pltpu.VMEM((8, columns), jnp.float32),
    ]


def near_pairs(scalars, keep, own, other, rows, cols):
    return pl.pallas_call(
        near_kernel,
        out_shape=(
            jax.ShapeDtypeStruct((2, 8, LANES), jnp.float32),
            jax.ShapeDtypeStruct((8, 2048), jnp.float32),
        ),
        in_specs=[smem(), smem(), vmem(), vmem(), vmem(), vmem()],
        out_specs=(vmem(), vmem()),
        scratch_shapes=pair_scratch(2048, (256, 512)),
        compiler_params=pltpu.CompilerParams(vmem_limit_bytes=VMEM),
        cost_estimate=pl.CostEstimate(flops=2 * 10**9, bytes_accessed=10**7, transcendentals=0),
        name="near_pairs",
    )(scalars, keep, own, other, rows, cols)


def far_pairs(scalars, keep, own, other, left, right, rows, cols, near):
    return pl.pallas_call(
        far_kernel,
        out_shape=(
            jax.ShapeDtypeStruct((3, 8, LANES), jnp.float32),
            jax.ShapeDtypeStruct((2, 8, LANES), jnp.float32),
        ),
        in_specs=[smem(), smem(), hbm(), hbm(), hbm()] + [vmem()] * 5,
        out_specs=(vmem(), vmem()),
        scratch_shapes=[pltpu.VMEM((3072, 256), jnp.bfloat16)]
        + pair_scratch(3072, FAR_TILE)
        + [pltpu.SemaphoreType.DMA((3,))],
        compiler_params=pltpu.CompilerParams(vmem_limit_bytes=VMEM),
        cost_estimate=pl.CostEstimate(flops=4 * 10**9, bytes_accessed=10**7, transcendentals=0),
        name="far_pairs",
    )(scalars, keep, own, other, left, right, rows, cols, *near)


def rank_kernel(place_ref, *refs):
    pieces, out_ref = refs[:-1], refs[-1]
    place_at = place_ref[...]
    lane = place_at & 127
    which = place_at >> 7
    total = jnp.zeros((32, LANES), jnp.float32)
    for s in range(4):
        block = pieces[s][0] + pieces[(s + 1) % 4][1] + pieces[(s + 3) % 4][2]
        for u in range(8):
            row = jnp.broadcast_to(block[u : u + 1, :], (32, LANES))
            value = jnp.take_along_axis(row, lane, axis=1)
            total = jnp.where(which == s * 8 + u, value, total)
    out_ref[...] = total * (1.0 / TILE)


def to_rank_order(place_at, pieces):
    return pl.pallas_call(
        rank_kernel,
        out_shape=jax.ShapeDtypeStruct((32, LANES), jnp.float32),
        in_specs=[vmem()] * 5,
        out_specs=vmem(),
        compiler_params=pltpu.CompilerParams(vmem_limit_bytes=VMEM),
        name="to_rank_order",
    )(place_at, *pieces)


def on_device(points, rank_source, thresholds, kept_tiles):
    bands = lax.axis_size("band")
    reps = lax.axis_size("rep")
    device = lax.axis_index("band").astype(jnp.int32)
    rep = lax.axis_index("rep").astype(jnp.int32)
    core = device & 1
    host = device ^ 8
    own_band = jnp.where(core == 0, host, bands - host)
    other_band = bands - 1 - own_band
    own_offset = jnp.where(own_band < bands // 2, 0, 2)
    other_offset = 2 - own_offset
    cross = (rep >= 2).astype(jnp.int32)
    left_offset = jnp.where(cross == 1, other_offset, own_offset)
    scalars = jnp.stack([
        device, rep * 16, rep, own_band, other_band, device, core,
        own_offset, other_offset, cross, left_offset,
    ]).astype(jnp.int32)
    codes = lax.dynamic_index_in_dim(kept_tiles, jnp.minimum(own_band, other_band), 0, keepdims=False)
    ids = jnp.arange(16, dtype=jnp.int32)
    a, c = ids // 4, ids % 4
    wanted = jnp.minimum(a, c) * 4 + jnp.maximum(a, c)
    keep = jnp.where(jnp.any(codes[:, None] == wanted[None, :], axis=0), 1.0, -1e30).astype(jnp.float32)

    rank2d = rank_source.reshape(2048, LANES)
    thr2d = thresholds.reshape(2048, LANES)

    def joint(move):
        return [
            (d * reps + r, e * reps + q)
            for d in range(bands)
            for r in range(reps)
            for e, q in (move(d, r),)
        ]

    def shift(value, move):
        return lax.ppermute(value, ("band", "rep"), joint(move))

    payload = send_rows(rank2d, points)
    own = lax.all_to_all(
        payload.reshape(bands, 16, 256), "band", split_axis=0, concat_axis=0, tiled=True
    ).reshape(1024, 256)
    own, rows, cols, place_at = lax.optimization_barrier((own, *place(scalars, rank2d, thr2d)))

    def to_right(d, r):
        q = (r + 1) % reps
        return (d if q < 2 else d ^ 1), q

    other = shift(own, lambda d, r: (d ^ 1, r))
    right = shift(own, lambda d, r: (d, (r - 1) % reps))
    left = shift(own, to_right)

    near = near_pairs(scalars, keep, own, other, rows, cols)
    stay, move = far_pairs(scalars, keep, own, other, left, right, rows, cols, near)
    moved = shift(move, lambda d, r: (d ^ 1, r))
    sums = stay + jnp.stack([moved[0], jnp.zeros_like(moved[0]), moved[1]])
    home = shift(sums, lambda d, r: (block_band(d), r))
    moved = {s: shift(home, lambda d, r, s=s: (d, (r + s) % reps)) for s in (2, 1, 3)}
    return to_rank_order(place_at, [home, moved[1], moved[2], moved[3]]).reshape(points.shape[0])


def solution(mesh):
    in_specs = (P("band", None), P(), P(), P())
    out_specs = P("band")
    return jax.shard_map(
        on_device, mesh=mesh, in_specs=in_specs, out_specs=out_specs, check_vma=False
    )
```
